1024 devices in a mesh: gx: 8 (over x, core), gy: 8 (over y), gz: 16 (over z).
Axes of the slice: x: 4, y: 8, z: 16, core: 2. Of those that a mesh axis runs over, the one named last changes fastest.
Arguments:
- right_side: float32 [64, 256, 2048], P('gx', 'gy', 'gz'), may hold values from -6 to 6
- sigma: float32 [64, 256, 2048], P('gx', 'gy', 'gz'), may hold values from 0.0001 to 0.001
- kappa: float32 [3, 64, 256, 2048], P(None, 'gx', 'gy', 'gz'), may hold values from 0.5 to 2
- coarse_inverse: float32 [1024, 1024], P(('gx', 'gy', 'gz')), as said below
Outputs:
- solution_field: float32 [64, 256, 2048], P('gx', 'gy', 'gz')
- residual: float32 [64, 256, 2048], P('gx', 'gy', 'gz')
The draws below stay inside these ranges and needn't reach their ends.
Inputs may be any that keep to these rules, and one draw needn't show every extreme that they name: `coarse_inverse`: symmetric, with a positive diagonal that dominates each row.
All inputs are finite; a program needn't handle non-finite values.
Results may differ from the reference program's by a relative error of at most 0.0003.
Values sent between devices are 32-bit elements; how exact they have to be, the bound alone decides.
No kernel may reach another device: no remote copies, remote signals or barrier semaphores. Data moves between devices by JAX's collectives and lax.ppermute only.
A program may use at most 32 MiB of HBM per device.

```python
import math
import jax
import jax.numpy as jnp
from jax import lax

CX = 8
CY = 32
CZ = 128
AX = 4
AY = 4
AZ = 8
ITERS = 1
NX = 64
NY = 256
NZ = 2048
BLOCKS = 1024
N_GX = 8
N_GY = 8
N_GZ = 16


def draw_coarse_inverse(key, part):
    key_diag = jax.random.fold_in(key, 11)
    key_off = jax.random.fold_in(key, 12)
    diagonal_vals = jax.random.uniform(key_diag, (BLOCKS,), jnp.float32, 0.5, 1.5)
    gaussian = jax.random.normal(key_off, (BLOCKS, BLOCKS), jnp.float32)
    off_part = (gaussian + gaussian.T) * (0.2 / BLOCKS)
    whole = jnp.diag(diagonal_vals) + off_part
    return whole / jnp.sqrt(jnp.float32(CX * CY * CZ))


def steps_of(stream_key, shape, shards, low, high):
    factor_of, own = 1.0, jax.random.fold_in(stream_key, 6)
    for dim, blocks in shards:
        heights = jnp.exp(jax.random.uniform(jax.random.fold_in(own, dim), (blocks,), jnp.float32, low / len(shards), high / len(shards)))
        factor_of = factor_of * jnp.repeat(heights, shape[dim] // blocks).reshape([-1 if axis == dim else 1 for axis in range(len(shape))])
    return factor_of


def noise(key, dims, deviation, bound, split=(), kind=jnp.bfloat16):
    gain = steps_of(key, dims, split, -0.22, 0.18) if split else 1.0
    result = jax.random.normal(key, dims, jnp.float32) * deviation * gain
    return jnp.minimum(jnp.maximum(result, -bound), bound).astype(kind)


def setup_inputs(seed: int = 0) -> dict:
    key_of = jax.random.split(jax.random.key(seed), 5)
    return {
        "right_side": noise(key_of[0], (NX, NY, NZ), 1.0, 6.0, ((0, 8), (1, 8), (2, 16)), jnp.float32),
        "sigma": jnp.clip(jnp.exp(math.log(0.001) - 2.3025852 * jax.random.uniform(key_of[1], (NX, NY, NZ), jnp.float32) ** steps_of(key_of[1], (NX, NY, NZ), ((0, 8), (1, 8), (2, 16)), -0.2, 0.2)), 0.0001, 0.001),
        "kappa": jnp.clip(jnp.exp(math.log(2.0) - 1.3862944 * jax.random.uniform(key_of[2], (3, NX, NY, NZ), jnp.float32) ** steps_of(key_of[2], (3, NX, NY, NZ), ((1, 8), (2, 8), (3, 16)), -0.2, 0.2)), 0.5, 2.0),
        "coarse_inverse": draw_coarse_inverse(jax.random.fold_in(key_of[4], 71), 0),
    }


jacobi_weight = 0.6

def apply_operator(field, sigma, kappa):
    padded = jnp.pad(field, 1)
    lap_x = 2.0 * field - padded[2:, 1:-1, 1:-1] - padded[:-2, 1:-1, 1:-1]
    lap_y = 2.0 * field - padded[1:-1, 2:, 1:-1] - padded[1:-1, :-2, 1:-1]
    lap_z = 2.0 * field - padded[1:-1, 1:-1, 2:] - padded[1:-1, 1:-1, :-2]
    return sigma * field + kappa[0] * lap_x + kappa[1] * lap_y + kappa[2] * lap_z

def aggregate(field, fac_x, fac_y, fac_z):
    size_x, size_y, size_z = field.shape
    shaped = field.reshape(size_x // fac_x, fac_x, size_y // fac_y, fac_y, size_z // fac_z, fac_z)
    return jnp.sum(shaped, axis=(1, 3, 5))

def spread(coarse, fac_x, fac_y, fac_z):
    size_x, size_y, size_z = coarse.shape
    wide = jnp.broadcast_to(coarse[:, None, :, None, :, None], (size_x, fac_x, size_y, fac_y, size_z, fac_z))
    return wide.reshape(size_x * fac_x, size_y * fac_y, size_z * fac_z)

def solve_lines(rhs_lines, line_e, line_g):
    zero_col = jnp.zeros_like(line_g[:, :1])
    below = jnp.concatenate([zero_col, line_g[:, :-1]], axis=1)
    main_band = line_e + line_g + below
    lower_band = -below
    upper_band = jnp.concatenate([-line_g[:, :-1], zero_col], axis=1)
    solved = lax.linalg.tridiagonal_solve(lower_band, main_band, upper_band, rhs_lines[..., None])
    return solved[..., 0]

def reference(right_side, sigma, kappa, coarse_inverse):
    diag = sigma + 2.0 * (kappa[0] + kappa[1] + kappa[2])
    coarse_shape = (NX // AX, NY // AY, NZ // AZ)
    line_count = coarse_shape[0] * coarse_shape[1]
    line_e = aggregate(sigma, AX, AY, AZ).reshape(line_count, coarse_shape[2])
    line_g = (aggregate(kappa[2], AX, AY, AZ) / AZ).reshape(line_count, coarse_shape[2])
    theta = 1.0 / (AX * AY * AZ)

    def precondition(vector):
        rhs_lines = aggregate(vector, AX, AY, AZ).reshape(line_count, coarse_shape[2])
        line_part = solve_lines(rhs_lines, line_e, line_g).reshape(coarse_shape)
        block_sums = aggregate(vector, NX // N_GX, NY // N_GY, NZ // N_GZ).reshape(-1)
        coarse_vals = jnp.dot(coarse_inverse, block_sums, precision=lax.Precision.HIGHEST)
        coarse_part = spread(coarse_vals.reshape(N_GX, N_GY, N_GZ), NX // N_GX, NY // N_GY, NZ // N_GZ)
        return jacobi_weight * vector / diag + theta * spread(line_part, AX, AY, AZ) + coarse_part
    solution_field = jnp.zeros_like(right_side)
    residual = right_side
    for cycle in range(ITERS):
        first_dir = precondition(residual)
        first_img = apply_operator(first_dir, sigma, kappa)
        second_dir = precondition(first_img)
        second_img = apply_operator(second_dir, sigma, kappa)
        g_one = jnp.sum(first_img * first_img)
        g_cross = jnp.sum(first_img * second_img)
        g_two = jnp.sum(second_img * second_img)
        h_one = jnp.sum(first_img * residual)
        h_two = jnp.sum(second_img * residual)
        determinant = g_one * g_two - g_cross * g_cross
        coef_one = (g_two * h_one - g_cross * h_two) / determinant
        coef_two = (g_one * h_two - g_cross * h_one) / determinant
        solution_field = solution_field + coef_one * first_dir + coef_two * second_dir
        residual = residual - coef_one * first_img - coef_two * second_img
    return (solution_field, residual)
```

```python
import functools

import jax
import jax.numpy as jnp
from jax import lax
from jax.experimental import pallas as pl
from jax.experimental.pallas import tpu as pltpu
from jax.sharding import PartitionSpec as P

CX, CY, CZ = 8, 32, 128
CELLS = 16
LINES = 16
THETA = 1.0 / 128.0
WEIGHT = 0.6
PART_AT, LOW_AT, HIGH_AT = 32, 64, 96
HIGHEST = lax.Precision.HIGHEST
F32 = jnp.float32


def iota(shape, dim):
    return lax.broadcasted_iota(jnp.int32, shape, dim)


def dot(a, b):
    return lax.dot_general(
        a, b, (((1,), (0,)), ((), ())), precision=HIGHEST, preferred_element_type=F32
    )


def dot_t(a, b):
    return lax.dot_general(
        a, b, (((1,), (1,)), ((), ())), precision=HIGHEST, preferred_element_type=F32
    )


def one_where(cond):
    return jnp.where(cond, 1.0, 0.0).astype(F32)


def lines_of(field):
    low = (field[0] + field[1]) + (field[2] + field[3])
    high = (field[4] + field[5]) + (field[6] + field[7])
    stacked = jnp.concatenate([low, high], axis=0)
    by_line = one_where(iota((128, 64), 1) // 4 == iota((128, 64), 0))
    by_cell = one_where(iota((CELLS, 128), 1) // 8 == iota((CELLS, 128), 0))
    return dot_t(by_cell, dot(by_line, stacked))


def faces_of(field):
    lane, row = iota((CX, CY, 128), 2), iota((CX, CY, 128), 1)
    low = jnp.where(lane == LOW_AT + row, field[:, :, 0:1], 0.0)
    both = jnp.where(lane == HIGH_AT + row, field[:, :, CZ - 1 : CZ], low)
    return jnp.sum(both, axis=1)


def write_z_message(zmsg_ref, rows, faces, spread_inverse, total, sizes):
    lane = iota((8, 128), 1)
    zero = jnp.zeros((1, 128), F32)
    head = jnp.concatenate(rows + [zero] * (8 - len(rows)), axis=0)
    base = jnp.where(lane < LINES, head, faces)
    mine = spread_inverse * total
    inside = (lane >= PART_AT) & (lane < PART_AT + 24)
    for p in range(sizes[2]):
        moved = pltpu.roll(mine, (PART_AT + 8 - 8 * p) % 128, 1)
        zmsg_ref[p] = jnp.where(inside, moved, base)


def write_planes(field, planes):
    xlo, xhi, ylo, yhi = planes
    xlo[...] = field[0]
    xhi[...] = field[CX - 1]
    ylo[...] = field[:, 0, :]
    yhi[...] = field[:, CY - 1, :]


def begin_kernel(
    sizes, r_ref, sigma_ref, kappa_ref, inv_ref,
    jac_ref, dinv_ref, zmsg_ref, loc_ref, alpha_ref, spread_ref, *planes
):
    r, sigma = r_ref[...], sigma_ref[...]
    kx, ky, kz = kappa_ref[0], kappa_ref[1], kappa_ref[2]
    dinv = WEIGHT / (sigma + 2.0 * (kx + ky + kz))
    jac = dinv * r
    dinv_ref[...] = dinv
    jac_ref[...] = jac
    write_planes(jac, planes)
    unused = iota((CELLS, 128), 1) >= LINES
    e = jnp.where(unused, 1.0, lines_of(sigma))
    g = jnp.where(unused, 1.0, lines_of(kz) * 0.125)
    rhs = lines_of(r)
    row = lambda a, k: a[k : k + 1, :]
    first, mid, last = row(e, 0), row(g, 0), row(e, 1)
    cur_first, cur = row(rhs, 0), row(rhs, 1)
    zero = jnp.zeros((1, 128), F32)
    for c in range(3):
        for k in (0, CELLS - 1):
            loc_ref[c, k : k + 1, :] = zero
    for k in (0, CELLS - 1):
        alpha_ref[k : k + 1, :] = zero
    for k in range(1, CELLS - 1):
        inv = 1.0 / (mid + last + row(g, k))
        mu, gam = mid * inv, row(g, k) * inv
        loc_ref[0, k : k + 1, :] = mu
        loc_ref[1, k : k + 1, :] = gam
        loc_ref[2, k : k + 1, :] = inv
        alpha_ref[k : k + 1, :] = cur * inv
        first = first + mu * last
        mid = mu * row(g, k)
        last = row(e, k + 1) + gam * last
        cur_first = cur_first + mu * cur
        cur = row(rhs, k + 1) + gam * cur
    move = one_where((iota((128, 128), 0) % 16) * 8 + iota((128, 128), 0) // 16 == iota((128, 128), 1))
    spread_inverse = dot(inv_ref[...], move)
    spread_ref[...] = spread_inverse
    rows = [cur_first, cur, first, mid, last, row(g, CELLS - 1)]
    write_z_message(zmsg_ref, rows, faces_of(jac), spread_inverse, jnp.sum(r), sizes)


def chain_kernel(sizes, fresh, zrec_ref, loc_ref, alpha_ref, *refs):
    if fresh:
        xmsg_ref, own_ref, zhalo_ref, chain_ref, final_ref, sol_ref = refs
    else:
        chain_ref, final_ref, xmsg_ref, own_ref, zhalo_ref, sol_ref = refs
    nx, ny, nz = sizes
    mx, my, mz = lax.axis_index("gx"), lax.axis_index("gy"), lax.axis_index("gz")
    used = iota((8, 128), 1) < LINES
    tiles = [jnp.where(used, zrec_ref[p], 1.0) for p in range(nz)]
    part = lambda p, i: tiles[p][i : i + 1, :]
    zero = jnp.zeros((1, 128), F32)

    if fresh:
        one = zero + 1.0
        cond, cond_own, hold, ginv = zero, zero, one, one
        for p in range(nz - 1):
            a, m, b, g = part(p, 2), part(p, 3), part(p, 4), part(p, 5)
            at_first = a + cond
            s = m + at_first
            n = b * s + m * at_first
            inv = 1.0 / (n + g * s)
            chain_ref[0, p : p + 1, :] = g * m * inv
            c2 = g * s * inv
            chain_ref[1, p : p + 1, :] = c2
            cond = g * n * inv
            here = mz == p + 1
            cond_own = jnp.where(here, cond, cond_own)
            hold = jnp.where(here, c2, hold)
            ginv = jnp.where(here, g, ginv)
        left_cond, left_hold, left_ginv = cond_own, hold, 1.0 / ginv
        cond = part(nz - 1, 5)
        cond_own, hold, ginv = cond, one, one
        for p in range(nz - 1, 0, -1):
            a, m, b, g = part(p, 2), part(p, 3), part(p, 4), part(p - 1, 5)
            at_last = b + cond
            s = m + at_last
            n = a * s + m * at_last
            inv = 1.0 / (n + g * s)
            chain_ref[2, p : p + 1, :] = g * m * inv
            c2 = g * s * inv
            chain_ref[3, p : p + 1, :] = c2
            cond = g * n * inv
            here = mz == p - 1
            cond_own = jnp.where(here, cond, cond_own)
            hold = jnp.where(here, c2, hold)
            ginv = jnp.where(here, g, ginv)
        right_cond, right_hold, right_ginv = cond_own, hold, 1.0 / ginv
        for c, p in ((0, nz - 1), (1, nz - 1), (2, 0), (3, 0)):
            chain_ref[c, p : p + 1, :] = zero
        mine = jnp.where(used, zrec_ref[mz], 1.0)
        big_a = mine[2:3, :] + left_cond
        big_b = mine[4:5, :] + right_cond
        m = mine[3:4, :]
        det_inv = 1.0 / (big_a * m + big_b * m + big_a * big_b)
        f1, f2, f3 = (big_b + m) * det_inv, m * det_inv, (big_a + m) * det_inv
        final_ref[...] = jnp.concatenate(
            [f1, f2, f3, left_ginv, left_hold, right_ginv, right_hold, zero], axis=0
        )
    else:
        mine = jnp.where(used, zrec_ref[mz], 0.0)
        f1, f2, f3, left_ginv, left_hold, right_ginv, right_hold = [
            final_ref[i : i + 1, :] for i in range(7)
        ]
    chain = lambda c, p: chain_ref[c, p : p + 1, :]
    cur, cur_left = zero, zero
    for p in range(nz - 1):
        cur = chain(0, p) * (part(p, 0) + cur) + chain(1, p) * part(p, 1)
        cur_left = jnp.where(mz == p + 1, cur, cur_left)
    cur, cur_right = zero, zero
    for p in range(nz - 1, 0, -1):
        cur = chain(2, p) * (part(p, 1) + cur) + chain(3, p) * part(p, 0)
        cur_right = jnp.where(mz == p - 1, cur, cur_right)
    cur_first = mine[0:1, :] + cur_left
    cur_last = mine[1:2, :] + cur_right
    sol_first = f1 * cur_first + f2 * cur_last
    sol_last = f2 * cur_first + f3 * cur_last
    below = cur_left * left_ginv + left_hold * sol_first
    above = cur_right * right_ginv + right_hold * sol_last
    sol_ref[0:1, :] = sol_first
    sol_ref[CELLS - 1 : CELLS, :] = sol_last
    value = sol_last
    for k in range(CELLS - 2, 0, -1):
        value = alpha_ref[k : k + 1, :] + loc_ref[0, k : k + 1, :] * sol_first + loc_ref[1, k : k + 1, :] * value
        sol_ref[k : k + 1, :] = value
    lanes16 = iota((CELLS, 128), 1) < LINES
    sol = jnp.where(lanes16, sol_ref[...], 0.0) * THETA

    line, lane = iota((128, 128), 0), iota((128, 128), 1)
    picks = [
        one_where(line == lane // 16),
        one_where(line == 8 + lane // 16),
        one_where((line == (lane // 16) * 8) & (lane < 32)),
        one_where((line == (lane // 16) * 8 + 7) & (lane < 32)),
    ]
    keep = iota((CELLS, 128), 1) % 16 == iota((CELLS, 128), 0)
    x_low, x_high, y_low, y_high = [
        jnp.sum(jnp.where(keep, dot(sol, pick), 0.0), axis=0, keepdims=True) for pick in picks
    ]
    own_ref[...] = jnp.concatenate([x_low, x_high] + [zero] * 6, axis=0)

    lane8, row8 = iota((8, 128), 1), iota((8, 128), 0)
    of_row = (lane8 // 8 == row8 // 4) & (lane8 < LINES)
    to_high = one_where((lane >= HIGH_AT) & ((lane - HIGH_AT) // 4 == line % 8) & (line < LINES))
    to_low = one_where(
        (lane >= LOW_AT) & (lane < HIGH_AT) & ((lane - LOW_AT) // 4 == line % 8) & (line < LINES)
    )
    lines_part = dot(jnp.where(of_row, below, 0.0), to_high) + dot(jnp.where(of_row, above, 0.0), to_low)
    from_below = zrec_ref[jnp.maximum(mz - 1, 0)]
    from_above = zrec_ref[jnp.minimum(mz + 1, nz - 1)]
    face = jnp.where(lane8 >= HIGH_AT, from_below, from_above)
    zhalo_ref[...] = jnp.where(lane8 >= LOW_AT, face + THETA * lines_part, 0.0)

    total = zrec_ref[0]
    for p in range(1, nz):
        total = total + zrec_ref[p]
    at = lambda lo: (lane8 >= lo) & (lane8 < lo + 8)
    x_less = pltpu.roll(pltpu.roll(total, 1, 0), 16, 1)
    x_more = pltpu.roll(pltpu.roll(total, 7, 0), 24, 1)
    sums = jnp.where((lane8 >= PART_AT) & (lane8 < PART_AT + 24), total, 0.0)
    sums = jnp.where(at(PART_AT + 24), x_less, sums)
    sums = jnp.where(at(PART_AT + 32), x_more, sums)
    second = iota((2, 128), 0) == 1
    for i in range(nx):
        both = jnp.where(second, sums[i : i + 1, :], 0.0)
        for j in range(ny):
            xmsg_ref[i * ny + j] = both
    here = mx * ny + my

    @pl.when(mx > 0)
    def _():
        xmsg_ref[here - ny, 0:1, :] = x_low

    @pl.when(mx < nx - 1)
    def _():
        xmsg_ref[here + ny, 0:1, :] = x_high

    @pl.when(my > 0)
    def _():
        xmsg_ref[here - 1, 0:1, :] = y_low

    @pl.when(my < ny - 1)
    def _():
        xmsg_ref[here + 1, 0:1, :] = y_high


def operator(sizes, base, sigma_ref, kappa_ref, xrec_ref, own_ref, zhalo_ref, halos, z_ref, w_ref):
    nx, ny, nz = sizes
    mx, my, mz = lax.axis_index("gx"), lax.axis_index("gy"), lax.axis_index("gz")
    here = mx * ny + my
    sums = xrec_ref[0, 1:2, :]
    for q in range(1, nx * ny):
        sums = sums + xrec_ref[q, 1:2, :]
    lane1 = iota((1, 128), 1)
    coarse = lambda at: jnp.sum(jnp.where(lane1 == at + my, sums, 0.0))
    c_own = coarse(PART_AT + 8)
    c_zlo, c_zhi = coarse(PART_AT), coarse(PART_AT + 16)
    c_ylo, c_yhi = coarse(PART_AT + 7), coarse(PART_AT + 9)
    c_xlo, c_xhi = coarse(PART_AT + 24), coarse(PART_AT + 32)

    lane32, row32 = iota((CY, 128), 1), iota((CY, 128), 0)
    lane8, row8 = iota((8, 128), 1), iota((8, 128), 0)
    wide = lambda row: jnp.where(lane32 // 16 == row32 // 4, row, 0.0)
    thin = lambda row: jnp.where(lane8 // 16 == row8 // 4, row, 0.0)
    left = xrec_ref[jnp.maximum(here - ny, 0), 0:1, :]
    right = xrec_ref[jnp.minimum(here + ny, nx * ny - 1), 0:1, :]
    front = xrec_ref[jnp.maximum(here - 1, 0), 0:1, :]
    back = xrec_ref[jnp.minimum(here + 1, nx * ny - 1), 0:1, :]
    rows = jnp.concatenate(
        [wide(own_ref[0:1, :]), wide(own_ref[1:2, :]), wide(left), wide(right), thin(front), thin(back)],
        axis=0,
    )
    to_cells = one_where(iota((128, 128), 0) % 16 == iota((128, 128), 1) // 8)
    lines = dot(rows, to_cells)
    xlo, xhi, ylo, yhi = halos
    xlo = jnp.where(mx > 0, xlo[...] + lines[64:96] + c_xlo, 0.0)
    xhi = jnp.where(mx < nx - 1, xhi[...] + lines[96:128] + c_xhi, 0.0)
    ylo = jnp.where(my > 0, ylo[...] + lines[128:136] + c_ylo, 0.0)
    yhi = jnp.where(my < ny - 1, yhi[...] + lines[136:144] + c_yhi, 0.0)
    face = zhalo_ref[...]
    high = jnp.where(mz > 0, face + c_zlo, 0.0)
    low = jnp.where(mz < nz - 1, face + c_zhi, 0.0)
    face = jnp.where(lane8 >= HIGH_AT, high, low)
    diagonal = (lane32 == row32 + HIGH_AT) | (lane32 == row32 + LOW_AT)
    spots = jnp.concatenate([jnp.where(diagonal, face[x : x + 1, :], 0.0) for x in range(CX)], axis=0)
    j, k = iota((128, 128), 0), iota((128, 128), 1)
    to_ends = one_where(((j >= HIGH_AT) & (k == 0)) | ((j >= LOW_AT) & (j < HIGH_AT) & (k == CZ - 1)))
    ends = dot(spots, to_ends)

    z = [base(x) + lines[(x // 4) * 32 : (x // 4) * 32 + 32] + c_own for x in range(CX)]
    w = []
    for x in range(CX):
        here_z = z[x]
        z_ref[x] = here_z
        before = z[x - 1] if x > 0 else xlo
        after = z[x + 1] if x < CX - 1 else xhi
        y_less = jnp.where(row32 == 0, ylo[x : x + 1, :], pltpu.roll(here_z, 1, 0))
        y_more = jnp.where(row32 == CY - 1, yhi[x : x + 1, :], pltpu.roll(here_z, CY - 1, 0))
        z_less = jnp.where(lane32 == 0, 0.0, pltpu.roll(here_z, 1, 1))
        z_more = jnp.where(lane32 == CZ - 1, 0.0, pltpu.roll(here_z, CZ - 1, 1))
        twice = 2.0 * here_z
        value = (
            sigma_ref[x] * here_z
            + kappa_ref[0, x] * (twice - before - after)
            + kappa_ref[1, x] * (twice - y_less - y_more)
            + kappa_ref[2, x] * (twice - z_less - z_more - ends[x * 32 : x * 32 + 32])
        )
        w_ref[x] = value
        w.append(value)
    return z, w


def first_kernel(
    sizes, jac_ref, dinv_ref, sigma_ref, kappa_ref, xrec_ref, own_ref, zhalo_ref, h0, h1, h2, h3,
    loc_ref, spread_ref, z_ref, w_ref, zmsg_ref, alpha_ref, *planes
):
    base = lambda x: jac_ref[x]
    operator(sizes, base, sigma_ref, kappa_ref, xrec_ref, own_ref, zhalo_ref, (h0, h1, h2, h3), z_ref, w_ref)
    field = w_ref[...]
    jac = dinv_ref[...] * field
    write_planes(jac, planes)
    rhs = lines_of(field)
    row = lambda a, k: a[k : k + 1, :]
    cur_first, cur = row(rhs, 0), row(rhs, 1)
    zero = jnp.zeros((1, 128), F32)
    for k in (0, CELLS - 1):
        alpha_ref[k : k + 1, :] = zero
    for k in range(1, CELLS - 1):
        alpha_ref[k : k + 1, :] = cur * loc_ref[2, k : k + 1, :]
        cur_first = cur_first + loc_ref[0, k : k + 1, :] * cur
        cur = row(rhs, k + 1) + loc_ref[1, k : k + 1, :] * cur
    write_z_message(
        zmsg_ref, [cur_first, cur], faces_of(jac), spread_ref[...], jnp.sum(field), sizes
    )


def second_kernel(
    sizes, r_ref, w1_ref, dinv_ref, sigma_ref, kappa_ref, xrec_ref, own_ref, zhalo_ref, h0, h1, h2, h3,
    z_ref, w_ref, sums_ref
):
    base = lambda x: dinv_ref[x] * w1_ref[x]
    operator(sizes, base, sigma_ref, kappa_ref, xrec_ref, own_ref, zhalo_ref, (h0, h1, h2, h3), z_ref, w_ref)
    w1, w2, r = w1_ref[...], w_ref[...], r_ref[...]
    lane = iota((1, 128), 1)
    out = jnp.zeros((1, 128), F32)
    for i, product in enumerate((w1 * w1, w1 * w2, w2 * w2, w1 * r, w2 * r)):
        out = jnp.where(lane == i, jnp.sum(product), out)
    sums_ref[...] = out


def end_kernel(all_ref, r_ref, z1_ref, w1_ref, z2_ref, w2_ref, field_ref, res_ref):
    sums = all_ref[0]
    for q in range(1, all_ref.shape[0]):
        sums = sums + all_ref[q]
    lane = iota((1, 128), 1)
    spread = lambda i: jnp.sum(jnp.where(lane == i, sums, 0.0), axis=1, keepdims=True)
    g11, g12, g22, h1, h2 = [spread(i) for i in range(5)]
    inv = 1.0 / (g11 * g22 - g12 * g12)
    y1 = (g22 * h1 - g12 * h2) * inv
    y2 = (g11 * h2 - g12 * h1) * inv
    for x in range(CX):
        field_ref[x] = y1 * z1_ref[x] + y2 * z2_ref[x]
        res_ref[x] = r_ref[x] - y1 * w1_ref[x] - y2 * w2_ref[x]


def call(kernel, out_shapes, scratch=(), name=None, **kw):
    vmem = pl.BlockSpec(memory_space=pltpu.VMEM)

    def run(*args):
        return pl.pallas_call(
            kernel,
            out_shape=[jax.ShapeDtypeStruct(s, F32) for s in out_shapes],
            in_specs=[vmem] * len(args),
            out_specs=[vmem] * len(out_shapes),
            scratch_shapes=[pltpu.VMEM(s, F32) for s in scratch],
            compiler_params=pltpu.CompilerParams(vmem_limit_bytes=24 * 1024 * 1024),
            name=name,
            **kw,
        )(*args)

    return run


def shards(sizes, r, sigma, kappa, inverse_rows):
    nx, ny, nz = sizes
    field, plane, tile, coarse = (CX, CY, CZ), (CY, CZ), (8, 128), (CELLS, 128)
    planes = [plane, plane, tile, tile]
    to_z, to_xy = (nz, 8, 128), (nx * ny, 2, 128)

    def halo(parts):
        xlo, xhi, ylo, yhi = parts
        up = lambda n: [(i, (i + 1) % n) for i in range(n)]
        down = lambda n: [((i + 1) % n, i) for i in range(n)]
        return (
            lax.ppermute(xhi, "gx", up(nx)),
            lax.ppermute(xlo, "gx", down(nx)),
            lax.ppermute(yhi, "gy", up(ny)),
            lax.ppermute(ylo, "gy", down(ny)),
        )

    def along_z(message):
        return lax.all_to_all(message, "gz", split_axis=0, concat_axis=0, tiled=True)

    def along_xy(message):
        return lax.all_to_all(message, ("gx", "gy"), split_axis=0, concat_axis=0, tiled=True)

    bind = lambda kernel, *a: functools.partial(kernel, sizes, *a)
    jac, dinv, zmsg, loc, alpha, spread, *sides = call(
        bind(begin_kernel), [field, field, to_z, (3, *coarse), coarse, tile, *planes], name="begin"
    )(r, sigma, kappa, inverse_rows)
    zrec = along_z(zmsg)
    halos = halo(sides)
    xmsg, own, zhalo, chain, final = call(
        bind(chain_kernel, True), [to_xy, tile, tile, (4, nz, 128), tile], [coarse], name="lines_first"
    )(zrec, loc, alpha)
    xrec = along_xy(xmsg)
    z1, w1, zmsg, alpha, *sides = call(
        bind(first_kernel), [field, field, to_z, coarse, *planes], name="operator_first"
    )(jac, dinv, sigma, kappa, xrec, own, zhalo, *halos, loc, spread)
    zrec = along_z(zmsg)
    halos = halo(sides)
    xmsg, own, zhalo = call(
        bind(chain_kernel, False), [to_xy, tile, tile], [coarse], name="lines_second"
    )(zrec, loc, alpha, chain, final)
    xrec = along_xy(xmsg)
    z2, w2, sums = call(bind(second_kernel), [field, field, (1, 128)], name="operator_second")(
        r, w1, dinv, sigma, kappa, xrec, own, zhalo, *halos
    )
    sums = jnp.sum(along_z(jnp.broadcast_to(sums[None], (nz, 1, 128))), axis=0)
    sums = along_xy(jnp.broadcast_to(sums[None], (nx * ny, 1, 128)))
    return tuple(call(end_kernel, [field, field], name="end")(sums, r, z1, w1, z2, w2))


def solution(mesh):
    sizes = (mesh.shape["gx"], mesh.shape["gy"], mesh.shape["gz"])
    spec = P("gx", "gy", "gz")

    def run(r, sigma, kappa, inverse):
        return shards(sizes, r, sigma, kappa, inverse.reshape(8, 128))

    return jax.shard_map(
        run,
        mesh=mesh,
        in_specs=(spec, spec, P(None, "gx", "gy", "gz"), P(("gx", "gy", "gz"), None)),
        out_specs=(spec, spec),
        check_vma=False,
    )
```

```python
import functools

import jax
import jax.numpy as jnp
from jax import lax
from jax.experimental import pallas as pl
from jax.experimental.pallas import tpu as pltpu
from jax.sharding import PartitionSpec as P

CX, CY, CZ = 8, 32, 128
CELLS = 16
LINES = 16
THETA = 1.0 / 128.0
WEIGHT = 0.6
PART_AT, LOW_AT, HIGH_AT = 32, 64, 96
HIGHEST = lax.Precision.HIGHEST
F32 = jnp.float32


def iota(shape, dim):
    return lax.broadcasted_iota(jnp.int32, shape, dim)


def dot(a, b):
    return lax.dot_general(
        a, b, (((1,), (0,)), ((), ())), precision=HIGHEST, preferred_element_type=F32
    )


def dot_t(a, b):
    return lax.dot_general(
        a, b, (((1,), (1,)), ((), ())), precision=HIGHEST, preferred_element_type=F32
    )


def one_where(cond):
    return jnp.where(cond, 1.0, 0.0).astype(F32)


def lines_of(field):
    low = (field[0] + field[1]) + (field[2] + field[3])
    high = (field[4] + field[5]) + (field[6] + field[7])
    stacked = jnp.concatenate([low, high], axis=0)
    by_line = one_where(iota((128, 64), 1) // 4 == iota((128, 64), 0))
    by_cell = one_where(iota((CELLS, 128), 1) // 8 == iota((CELLS, 128), 0))
    return dot_t(by_cell, dot(by_line, stacked))


def faces_of(field):
    lane, row = iota((CX, CY, 128), 2), iota((CX, CY, 128), 1)
    low = jnp.where(lane == LOW_AT + row, field[:, :, 0:1], 0.0)
    both = jnp.where(lane == HIGH_AT + row, field[:, :, CZ - 1 : CZ], low)
    return jnp.sum(both, axis=1)


def write_z_message(zmsg_ref, rows, faces, spread_inverse, total, sizes):
    lane = iota((8, 128), 1)
    zero = jnp.zeros((1, 128), F32)
    head = jnp.concatenate(rows + [zero] * (8 - len(rows)), axis=0)
    base = jnp.where(lane < LINES, head, faces)
    mine = spread_inverse * total
    inside = (lane >= PART_AT) & (lane < PART_AT + 24)
    for p in range(sizes[2]):
        moved = pltpu.roll(mine, (PART_AT + 8 - 8 * p) % 128, 1)
        zmsg_ref[p] = jnp.where(inside, moved, base)


def write_planes(field, planes):
    xlo, xhi, ylo, yhi = planes
    xlo[...] = field[0]
    xhi[...] = field[CX - 1]
    ylo[...] = field[:, 0, :]
    yhi[...] = field[:, CY - 1, :]


def begin_kernel(
    sizes, r_hbm, sigma_hbm, kappa_hbm, inv_hbm,
    jac_ref, dinv_ref, zmsg_ref, loc_ref, alpha_ref, spread_ref, xlo, xhi, ylo, yhi,
    r_ref, sigma_ref, kappa_ref, inv_ref, sems
):
    planes = (xlo, xhi, ylo, yhi)
    pairs = ((kappa_hbm, kappa_ref), (sigma_hbm, sigma_ref), (r_hbm, r_ref), (inv_hbm, inv_ref))
    copies = [pltpu.make_async_copy(a, b, sems.at[i]) for i, (a, b) in enumerate(pairs)]
    for copy in copies:
        copy.start()
    for copy in copies:
        copy.wait()
    r, sigma = r_ref[...], sigma_ref[...]
    kx, ky, kz = kappa_ref[0], kappa_ref[1], kappa_ref[2]
    dinv = WEIGHT / (sigma + 2.0 * (kx + ky + kz))
    jac = dinv * r
    dinv_ref[...] = dinv
    jac_ref[...] = jac
    write_planes(jac, planes)
    unused = iota((CELLS, 128), 1) >= LINES
    e = jnp.where(unused, 1.0, lines_of(sigma))
    g = jnp.where(unused, 1.0, lines_of(kz) * 0.125)
    rhs = lines_of(r)
    row = lambda a, k: a[k : k + 1, :]
    first, mid, last = row(e, 0), row(g, 0), row(e, 1)
    cur_first, cur = row(rhs, 0), row(rhs, 1)
    zero = jnp.zeros((1, 128), F32)
    for c in range(3):
        for k in (0, CELLS - 1):
            loc_ref[c, k : k + 1, :] = zero
    for k in (0, CELLS - 1):
        alpha_ref[k : k + 1, :] = zero
    for k in range(1, CELLS - 1):
        inv = 1.0 / (mid + last + row(g, k))
        mu, gam = mid * inv, row(g, k) * inv
        loc_ref[0, k : k + 1, :] = mu
        loc_ref[1, k : k + 1, :] = gam
        loc_ref[2, k : k + 1, :] = inv
        alpha_ref[k : k + 1, :] = cur * inv
        first = first + mu * last
        mid = mu * row(g, k)
        last = row(e, k + 1) + gam * last
        cur_first = cur_first + mu * cur
        cur = row(rhs, k + 1) + gam * cur
    move = one_where((iota((128, 128), 0) % 16) * 8 + iota((128, 128), 0) // 16 == iota((128, 128), 1))
    spread_inverse = dot(inv_ref[...], move)
    spread_ref[...] = spread_inverse
    rows = [cur_first, cur, first, mid, last, row(g, CELLS - 1)]
    write_z_message(zmsg_ref, rows, faces_of(jac), spread_inverse, jnp.sum(r), sizes)


def chain_kernel(sizes, fresh, zrec_ref, loc_ref, alpha_ref, _, __, *refs):
    if fresh:
        xmsg_ref, own_ref, zhalo_ref, chain_ref, final_ref, sol_ref = refs
    else:
        chain_ref, final_ref, xmsg_ref, own_ref, zhalo_ref, sol_ref = refs
    nx, ny, nz = sizes
    mx, my, mz = lax.axis_index("gx"), lax.axis_index("gy"), lax.axis_index("gz")
    used = iota((8, 128), 1) < LINES
    tiles = [jnp.where(used, zrec_ref[p], 1.0) for p in range(nz)]
    part = lambda p, i: tiles[p][i : i + 1, :]
    zero = jnp.zeros((1, 128), F32)

    if fresh:
        one = zero + 1.0
        cond, cond_own, hold, ginv = zero, zero, one, one
        for p in range(nz - 1):
            a, m, b, g = part(p, 2), part(p, 3), part(p, 4), part(p, 5)
            at_first = a + cond
            s = m + at_first
            n = b * s + m * at_first
            inv = 1.0 / (n + g * s)
            chain_ref[0, p : p + 1, :] = g * m * inv
            c2 = g * s * inv
            chain_ref[1, p : p + 1, :] = c2
            cond = g * n * inv
            here = mz == p + 1
            cond_own = jnp.where(here, cond, cond_own)
            hold = jnp.where(here, c2, hold)
            ginv = jnp.where(here, g, ginv)
        left_cond, left_hold, left_ginv = cond_own, hold, 1.0 / ginv
        cond = part(nz - 1, 5)
        cond_own, hold, ginv = cond, one, one
        for p in range(nz - 1, 0, -1):
            a, m, b, g = part(p, 2), part(p, 3), part(p, 4), part(p - 1, 5)
            at_last = b + cond
            s = m + at_last
            n = a * s + m * at_last
            inv = 1.0 / (n + g * s)
            chain_ref[2, p : p + 1, :] = g * m * inv
            c2 = g * s * inv
            chain_ref[3, p : p + 1, :] = c2
            cond = g * n * inv
            here = mz == p - 1
            cond_own = jnp.where(here, cond, cond_own)
            hold = jnp.where(here, c2, hold)
            ginv = jnp.where(here, g, ginv)
        right_cond, right_hold, right_ginv = cond_own, hold, 1.0 / ginv
        for c, p in ((0, nz - 1), (1, nz - 1), (2, 0), (3, 0)):
            chain_ref[c, p : p + 1, :] = zero
        mine = jnp.where(used, zrec_ref[mz], 1.0)
        big_a = mine[2:3, :] + left_cond
        big_b = mine[4:5, :] + right_cond
        m = mine[3:4, :]
        det_inv = 1.0 / (big_a * m + big_b * m + big_a * big_b)
        f1, f2, f3 = (big_b + m) * det_inv, m * det_inv, (big_a + m) * det_inv
        final_ref[...] = jnp.concatenate(
            [f1, f2, f3, left_ginv, left_hold, right_ginv, right_hold, zero], axis=0
        )
    else:
        mine = jnp.where(used, zrec_ref[mz], 0.0)
        f1, f2, f3, left_ginv, left_hold, right_ginv, right_hold = [
            final_ref[i : i + 1, :] for i in range(7)
        ]
    chain = lambda c, p: chain_ref[c, p : p + 1, :]
    cur, cur_left = zero, zero
    for p in range(nz - 1):
        cur = chain(0, p) * (part(p, 0) + cur) + chain(1, p) * part(p, 1)
        cur_left = jnp.where(mz == p + 1, cur, cur_left)
    cur, cur_right = zero, zero
    for p in range(nz - 1, 0, -1):
        cur = chain(2, p) * (part(p, 1) + cur) + chain(3, p) * part(p, 0)
        cur_right = jnp.where(mz == p - 1, cur, cur_right)
    cur_first = mine[0:1, :] + cur_left
    cur_last = mine[1:2, :] + cur_right
    sol_first = f1 * cur_first + f2 * cur_last
    sol_last = f2 * cur_first + f3 * cur_last
    below = cur_left * left_ginv + left_hold * sol_first
    above = cur_right * right_ginv + right_hold * sol_last
    sol_ref[0:1, :] = sol_first
    sol_ref[CELLS - 1 : CELLS, :] = sol_last
    value = sol_last
    for k in range(CELLS - 2, 0, -1):
        value = alpha_ref[k : k + 1, :] + loc_ref[0, k : k + 1, :] * sol_first + loc_ref[1, k : k + 1, :] * value
        sol_ref[k : k + 1, :] = value
    lanes16 = iota((CELLS, 128), 1) < LINES
    sol = jnp.where(lanes16, sol_ref[...], 0.0) * THETA

    line, lane = iota((128, 128), 0), iota((128, 128), 1)
    picks = [
        one_where(line == lane // 16),
        one_where(line == 8 + lane // 16),
        one_where((line == (lane // 16) * 8) & (lane < 32)),
        one_where((line == (lane // 16) * 8 + 7) & (lane < 32)),
    ]
    keep = iota((CELLS, 128), 1) % 16 == iota((CELLS, 128), 0)
    x_low, x_high, y_low, y_high = [
        jnp.sum(jnp.where(keep, dot(sol, pick), 0.0), axis=0, keepdims=True) for pick in picks
    ]
    own_ref[...] = jnp.concatenate([x_low, x_high] + [zero] * 6, axis=0)

    lane8, row8 = iota((8, 128), 1), iota((8, 128), 0)
    of_row = (lane8 // 8 == row8 // 4) & (lane8 < LINES)
    to_high = one_where((lane >= HIGH_AT) & ((lane - HIGH_AT) // 4 == line % 8) & (line < LINES))
    to_low = one_where(
        (lane >= LOW_AT) & (lane < HIGH_AT) & ((lane - LOW_AT) // 4 == line % 8) & (line < LINES)
    )
    lines_part = dot(jnp.where(of_row, below, 0.0), to_high) + dot(jnp.where(of_row, above, 0.0), to_low)
    from_below = zrec_ref[jnp.maximum(mz - 1, 0)]
    from_above = zrec_ref[jnp.minimum(mz + 1, nz - 1)]
    face = jnp.where(lane8 >= HIGH_AT, from_below, from_above)
    zhalo_ref[...] = jnp.where(lane8 >= LOW_AT, face + THETA * lines_part, 0.0)

    total = zrec_ref[0]
    for p in range(1, nz):
        total = total + zrec_ref[p]
    at = lambda lo: (lane8 >= lo) & (lane8 < lo + 8)
    x_less = pltpu.roll(pltpu.roll(total, 1, 0), 16, 1)
    x_more = pltpu.roll(pltpu.roll(total, 7, 0), 24, 1)
    sums = jnp.where((lane8 >= PART_AT) & (lane8 < PART_AT + 24), total, 0.0)
    sums = jnp.where(at(PART_AT + 24), x_less, sums)
    sums = jnp.where(at(PART_AT + 32), x_more, sums)
    second = iota((2, 128), 0) == 1
    for i in range(nx):
        both = jnp.where(second, sums[i : i + 1, :], 0.0)
        for j in range(ny):
            xmsg_ref[i * ny + j] = both
    here = mx * ny + my

    @pl.when(mx > 0)
    def _():
        xmsg_ref[here - ny, 0:1, :] = x_low

    @pl.when(mx < nx - 1)
    def _():
        xmsg_ref[here + ny, 0:1, :] = x_high

    @pl.when(my > 0)
    def _():
        xmsg_ref[here - 1, 0:1, :] = y_low

    @pl.when(my < ny - 1)
    def _():
        xmsg_ref[here + 1, 0:1, :] = y_high


def operator(sizes, base, sigma_ref, kappa_ref, xrec_ref, own_ref, zhalo_ref, halos, z_ref, w_ref):
    nx, ny, nz = sizes
    mx, my, mz = lax.axis_index("gx"), lax.axis_index("gy"), lax.axis_index("gz")
    here = mx * ny + my
    sums = xrec_ref[0, 1:2, :]
    for q in range(1, nx * ny):
        sums = sums + xrec_ref[q, 1:2, :]
    lane1 = iota((1, 128), 1)
    coarse = lambda at: jnp.sum(jnp.where(lane1 == at + my, sums, 0.0))
    c_own = coarse(PART_AT + 8)
    c_zlo, c_zhi = coarse(PART_AT), coarse(PART_AT + 16)
    c_ylo, c_yhi = coarse(PART_AT + 7), coarse(PART_AT + 9)
    c_xlo, c_xhi = coarse(PART_AT + 24), coarse(PART_AT + 32)

    lane32, row32 = iota((CY, 128), 1), iota((CY, 128), 0)
    lane8, row8 = iota((8, 128), 1), iota((8, 128), 0)
    wide = lambda row: jnp.where(lane32 // 16 == row32 // 4, row, 0.0)
    thin = lambda row: jnp.where(lane8 // 16 == row8 // 4, row, 0.0)
    left = xrec_ref[jnp.maximum(here - ny, 0), 0:1, :]
    right = xrec_ref[jnp.minimum(here + ny, nx * ny - 1), 0:1, :]
    front = xrec_ref[jnp.maximum(here - 1, 0), 0:1, :]
    back = xrec_ref[jnp.minimum(here + 1, nx * ny - 1), 0:1, :]
    rows = jnp.concatenate(
        [wide(own_ref[0:1, :]), wide(own_ref[1:2, :]), wide(left), wide(right), thin(front), thin(back)],
        axis=0,
    )
    to_cells = one_where(iota((128, 128), 0) % 16 == iota((128, 128), 1) // 8)
    lines = dot(rows, to_cells)
    xlo, xhi, ylo, yhi = halos
    xlo = jnp.where(mx > 0, xlo[...] + lines[64:96] + c_xlo, 0.0)
    xhi = jnp.where(mx < nx - 1, xhi[...] + lines[96:128] + c_xhi, 0.0)
    ylo = jnp.where(my > 0, ylo[...] + lines[128:136] + c_ylo, 0.0)
    yhi = jnp.where(my < ny - 1, yhi[...] + lines[136:144] + c_yhi, 0.0)
    face = zhalo_ref[...]
    high = jnp.where(mz > 0, face + c_zlo, 0.0)
    low = jnp.where(mz < nz - 1, face + c_zhi, 0.0)
    face = jnp.where(lane8 >= HIGH_AT, high, low)
    diagonal = (lane32 == row32 + HIGH_AT) | (lane32 == row32 + LOW_AT)
    spots = jnp.concatenate([jnp.where(diagonal, face[x : x + 1, :], 0.0) for x in range(CX)], axis=0)
    j, k = iota((128, 128), 0), iota((128, 128), 1)
    to_ends = one_where(((j >= HIGH_AT) & (k == 0)) | ((j >= LOW_AT) & (j < HIGH_AT) & (k == CZ - 1)))
    ends = dot(spots, to_ends)

    z = [base(x) + lines[(x // 4) * 32 : (x // 4) * 32 + 32] + c_own for x in range(CX)]
    w = []
    for x in range(CX):
        here_z = z[x]
        z_ref[x] = here_z
        before = z[x - 1] if x > 0 else xlo
        after = z[x + 1] if x < CX - 1 else xhi
        y_less = jnp.where(row32 == 0, ylo[x : x + 1, :], pltpu.roll(here_z, 1, 0))
        y_more = jnp.where(row32 == CY - 1, yhi[x : x + 1, :], pltpu.roll(here_z, CY - 1, 0))
        z_less = jnp.where(lane32 == 0, 0.0, pltpu.roll(here_z, 1, 1))
        z_more = jnp.where(lane32 == CZ - 1, 0.0, pltpu.roll(here_z, CZ - 1, 1))
        twice = 2.0 * here_z
        value = (
            sigma_ref[x] * here_z
            + kappa_ref[0, x] * (twice - before - after)
            + kappa_ref[1, x] * (twice - y_less - y_more)
            + kappa_ref[2, x] * (twice - z_less - z_more - ends[x * 32 : x * 32 + 32])
        )
        w_ref[x] = value
        w.append(value)
    return z, w


def first_kernel(
    sizes, jac_ref, dinv_ref, sigma_ref, kappa_ref, xrec_ref, own_ref, zhalo_ref, h0, h1, h2, h3,
    loc_ref, spread_ref, z_ref, w_ref, zmsg_ref, alpha_ref, *planes
):
    base = lambda x: jac_ref[x]
    operator(sizes, base, sigma_ref, kappa_ref, xrec_ref, own_ref, zhalo_ref, (h0, h1, h2, h3), z_ref, w_ref)
    field = w_ref[...]
    jac = dinv_ref[...] * field
    write_planes(jac, planes)
    rhs = lines_of(field)
    row = lambda a, k: a[k : k + 1, :]
    cur_first, cur = row(rhs, 0), row(rhs, 1)
    zero = jnp.zeros((1, 128), F32)
    for k in (0, CELLS - 1):
        alpha_ref[k : k + 1, :] = zero
    for k in range(1, CELLS - 1):
        alpha_ref[k : k + 1, :] = cur * loc_ref[2, k : k + 1, :]
        cur_first = cur_first + loc_ref[0, k : k + 1, :] * cur
        cur = row(rhs, k + 1) + loc_ref[1, k : k + 1, :] * cur
    write_z_message(
        zmsg_ref, [cur_first, cur], faces_of(jac), spread_ref[...], jnp.sum(field), sizes
    )


def second_kernel(
    sizes, r_ref, w1_ref, dinv_ref, sigma_ref, kappa_ref, xrec_ref, own_ref, zhalo_ref, h0, h1, h2, h3,
    z_ref, w_ref, sums_ref
):
    base = lambda x: dinv_ref[x] * w1_ref[x]
    operator(sizes, base, sigma_ref, kappa_ref, xrec_ref, own_ref, zhalo_ref, (h0, h1, h2, h3), z_ref, w_ref)
    w1, w2, r = w1_ref[...], w_ref[...], r_ref[...]
    lane = iota((1, 128), 1)
    out = jnp.zeros((1, 128), F32)
    for i, product in enumerate((w1 * w1, w1 * w2, w2 * w2, w1 * r, w2 * r)):
        out = jnp.where(lane == i, jnp.sum(product), out)
    sums_ref[...] = out


def end_kernel(all_ref, r_ref, z1_ref, w1_ref, z2_ref, w2_ref, field_ref, res_ref):
    sums = all_ref[0]
    for q in range(1, all_ref.shape[0]):
        sums = sums + all_ref[q]
    lane = iota((1, 128), 1)
    spread = lambda i: jnp.sum(jnp.where(lane == i, sums, 0.0), axis=1, keepdims=True)
    g11, g12, g22, h1, h2 = [spread(i) for i in range(5)]
    inv = 1.0 / (g11 * g22 - g12 * g12)
    y1 = (g22 * h1 - g12 * h2) * inv
    y2 = (g11 * h2 - g12 * h1) * inv
    for x in range(CX):
        field_ref[x] = y1 * z1_ref[x] + y2 * z2_ref[x]
        res_ref[x] = r_ref[x] - y1 * w1_ref[x] - y2 * w2_ref[x]


def call(kernel, out_shapes, scratch=(), name=None, inputs=pltpu.VMEM, semaphores=(), limit=24 << 20):
    vmem = pl.BlockSpec(memory_space=pltpu.VMEM)

    def run(*args):
        return pl.pallas_call(
            kernel,
            out_shape=[jax.ShapeDtypeStruct(s, F32) for s in out_shapes],
            in_specs=[pl.BlockSpec(memory_space=inputs)] * len(args),
            out_specs=[vmem] * len(out_shapes),
            scratch_shapes=[pltpu.VMEM(s, F32) for s in scratch] + list(semaphores),
            compiler_params=pltpu.CompilerParams(vmem_limit_bytes=limit),
            name=name,
        )(*args)

    return run


def shards(sizes, r, sigma, kappa, inverse_rows):
    nx, ny, nz = sizes
    field, plane, tile, coarse = (CX, CY, CZ), (CY, CZ), (8, 128), (CELLS, 128)
    planes = [plane, plane, tile, tile]
    to_z, to_xy = (nz, 8, 128), (nx * ny, 2, 128)

    def halo(parts):
        xlo, xhi, ylo, yhi = parts
        up = lambda n: [(i, (i + 1) % n) for i in range(n)]
        down = lambda n: [((i + 1) % n, i) for i in range(n)]
        return (
            lax.ppermute(xhi, "gx", up(nx)),
            lax.ppermute(xlo, "gx", down(nx)),
            lax.ppermute(yhi, "gy", up(ny)),
            lax.ppermute(ylo, "gy", down(ny)),
        )

    def along_z(message):
        return lax.all_to_all(message, "gz", split_axis=0, concat_axis=0, tiled=True)

    def along_xy(message):
        return lax.all_to_all(message, ("gx", "gy"), split_axis=0, concat_axis=0, tiled=True)

    bind = lambda kernel, *a: functools.partial(kernel, sizes, *a)
    jac, dinv, zmsg, loc, alpha, spread, *sides = call(
        bind(begin_kernel), [field, field, to_z, (3, *coarse), coarse, tile, *planes],
        [field, field, (3, *field), tile], "begin", pltpu.HBM, [pltpu.SemaphoreType.DMA((4,))], 54875 << 10,
    )(r, sigma, kappa, inverse_rows)
    zrec = along_z(zmsg)
    halos = halo(sides)
    xmsg, own, zhalo, chain, final = call(
        bind(chain_kernel, True), [to_xy, tile, tile, (4, nz, 128), tile], [coarse], "lines_first"
    )(zrec, loc, alpha, *halos[2:])
    xrec = along_xy(xmsg)
    z1, w1, zmsg, alpha, *sides = call(
        bind(first_kernel), [field, field, to_z, coarse, *planes], name="operator_first"
    )(jac, dinv, sigma, kappa, xrec, own, zhalo, *halos, loc, spread)
    zrec = along_z(zmsg)
    halos = halo(sides)
    xmsg, own, zhalo = call(
        bind(chain_kernel, False), [to_xy, tile, tile], [coarse], "lines_second"
    )(zrec, loc, alpha, *halos[2:], chain, final)
    xrec = along_xy(xmsg)
    z2, w2, sums = call(bind(second_kernel), [field, field, (1, 128)], name="operator_second")(
        r, w1, dinv, sigma, kappa, xrec, own, zhalo, *halos
    )
    sums = jnp.sum(along_z(jnp.broadcast_to(sums[None], (nz, 1, 128))), axis=0)
    sums = along_xy(jnp.broadcast_to(sums[None], (nx * ny, 1, 128)))
    return tuple(call(end_kernel, [field, field], name="end")(sums, r, z1, w1, z2, w2))


def solution(mesh):
    sizes = (mesh.shape["gx"], mesh.shape["gy"], mesh.shape["gz"])
    spec = P("gx", "gy", "gz")

    def run(r, sigma, kappa, inverse):
        return shards(sizes, r, sigma, kappa, inverse.reshape(8, 128))

    return jax.shard_map(
        run,
        mesh=mesh,
        in_specs=(spec, spec, P(None, "gx", "gy", "gz"), P(("gx", "gy", "gz"), None)),
        out_specs=(spec, spec),
        check_vma=False,
    )
```

```python
import functools

import jax
import jax.numpy as jnp
from jax import lax
from jax.experimental import pallas as pl
from jax.experimental.pallas import tpu as pltpu
from jax.sharding import PartitionSpec as P

CX, CY, CZ = 8, 32, 128
CELLS = 16
LINES = 16
THETA = 1.0 / 128.0
WEIGHT = 0.6
PART_AT, LOW_AT, HIGH_AT = 32, 64, 96
HIGHEST = lax.Precision.HIGHEST
F32 = jnp.float32


def iota(shape, dim):
    return lax.broadcasted_iota(jnp.int32, shape, dim)


def dot(a, b):
    return lax.dot_general(
        a, b, (((1,), (0,)), ((), ())), precision=HIGHEST, preferred_element_type=F32
    )


def dot_t(a, b):
    return lax.dot_general(
        a, b, (((1,), (1,)), ((), ())), precision=HIGHEST, preferred_element_type=F32
    )


def one_where(cond):
    return jnp.where(cond, 1.0, 0.0).astype(F32)


def lines_of(field):
    low = (field[0] + field[1]) + (field[2] + field[3])
    high = (field[4] + field[5]) + (field[6] + field[7])
    stacked = jnp.concatenate([low, high], axis=0)
    by_line = one_where(iota((128, 64), 1) // 4 == iota((128, 64), 0))
    by_cell = one_where(iota((CELLS, 128), 1) // 8 == iota((CELLS, 128), 0))
    return dot_t(by_cell, dot(by_line, stacked))


def faces_of(field):
    lane, row = iota((CX, CY, 128), 2), iota((CX, CY, 128), 1)
    low = jnp.where(lane == LOW_AT + row, field[:, :, 0:1], 0.0)
    both = jnp.where(lane == HIGH_AT + row, field[:, :, CZ - 1 : CZ], low)
    return jnp.sum(both, axis=1)


def write_z_message(zmsg_ref, rows, faces, spread_inverse, total, sizes):
    lane = iota((8, 128), 1)
    zero = jnp.zeros((1, 128), F32)
    head = jnp.concatenate(rows + [zero] * (8 - len(rows)), axis=0)
    base = jnp.where(lane < LINES, head, faces)
    mine = spread_inverse * total
    inside = (lane >= PART_AT) & (lane < PART_AT + 24)
    for p in range(sizes[2]):
        moved = pltpu.roll(mine, (PART_AT + 8 - 8 * p) % 128, 1)
        zmsg_ref[p] = jnp.where(inside, moved, base)


def write_planes(field, planes):
    x_in, x_out, y_in, y_out = planes
    even_x, even_y = lax.axis_index("gx") % 2 == 0, lax.axis_index("gy") % 2 == 0
    low, high = field[0], field[CX - 1]
    x_in[...] = jnp.where(even_x, high, low)
    x_out[...] = jnp.where(even_x, low, high)
    low, high = field[:, 0, :], field[:, CY - 1, :]
    y_in[...] = jnp.where(even_y, high, low)
    y_out[...] = jnp.where(even_y, low, high)


def begin_kernel(
    sizes, r_hbm, sigma_hbm, kappa_hbm, inv_hbm,
    zmsg_ref, loc_ref, alpha_ref, spread_ref, x_in, x_out, y_in, y_out,
    r_ref, sigma_ref, kappa_ref, inv_ref, sems
):
    pairs = ((kappa_hbm, kappa_ref), (sigma_hbm, sigma_ref), (r_hbm, r_ref), (inv_hbm, inv_ref))
    copies = [pltpu.make_async_copy(a, b, sems.at[i]) for i, (a, b) in enumerate(pairs)]
    for copy in copies:
        copy.start()
    for copy in copies:
        copy.wait()
    r, sigma = r_ref[...], sigma_ref[...]
    kx, ky, kz = kappa_ref[0], kappa_ref[1], kappa_ref[2]
    jac = r * (WEIGHT / (sigma + 2.0 * (kx + ky + kz)))
    write_planes(jac, (x_in, x_out, y_in, y_out))
    unused = iota((CELLS, 128), 1) >= LINES
    e = jnp.where(unused, 1.0, lines_of(sigma))
    g = jnp.where(unused, 1.0, lines_of(kz) * 0.125)
    rhs = lines_of(r)
    row = lambda a, k: a[k : k + 1, :]
    first, mid, last = row(e, 0), row(g, 0), row(e, 1)
    cur_first, cur = row(rhs, 0), row(rhs, 1)
    zero = jnp.zeros((1, 128), F32)
    for c in range(3):
        for k in (0, CELLS - 1):
            loc_ref[c, k : k + 1, :] = zero
    for k in (0, CELLS - 1):
        alpha_ref[k : k + 1, :] = zero
    for k in range(1, CELLS - 1):
        inv = 1.0 / (mid + last + row(g, k))
        mu, gam = mid * inv, row(g, k) * inv
        loc_ref[0, k : k + 1, :] = mu
        loc_ref[1, k : k + 1, :] = gam
        loc_ref[2, k : k + 1, :] = inv
        alpha_ref[k : k + 1, :] = cur * inv
        first = first + mu * last
        mid = mu * row(g, k)
        last = row(e, k + 1) + gam * last
        cur_first = cur_first + mu * cur
        cur = row(rhs, k + 1) + gam * cur
    move = one_where((iota((128, 128), 0) % 16) * 8 + iota((128, 128), 0) // 16 == iota((128, 128), 1))
    spread_inverse = dot(inv_ref[...], move)
    spread_ref[...] = spread_inverse
    rows = [cur_first, cur, first, mid, last, row(g, CELLS - 1)]
    write_z_message(zmsg_ref, rows, faces_of(jac), spread_inverse, jnp.sum(r), sizes)


def chain_kernel(sizes, fresh, zrec_ref, loc_ref, alpha_ref, h0, h1, h2, h3, *refs):
    if fresh:
        xmsg_ref, own_ref, zhalo_ref, chain_ref, final_ref, sol_ref = refs
    else:
        chain_ref, final_ref, xmsg_ref, own_ref, zhalo_ref, sol_ref = refs
    nx, ny, nz = sizes
    mx, my, mz = lax.axis_index("gx"), lax.axis_index("gy"), lax.axis_index("gz")
    used = iota((8, 128), 1) < LINES
    tiles = [jnp.where(used, zrec_ref[p], 1.0) for p in range(nz)]
    part = lambda p, i: tiles[p][i : i + 1, :]
    zero = jnp.zeros((1, 128), F32)

    if fresh:
        one = zero + 1.0
        cond, cond_own, hold, ginv = zero, zero, one, one
        for p in range(nz - 1):
            a, m, b, g = part(p, 2), part(p, 3), part(p, 4), part(p, 5)
            at_first = a + cond
            s = m + at_first
            n = b * s + m * at_first
            inv = 1.0 / (n + g * s)
            chain_ref[0, p : p + 1, :] = g * m * inv
            c2 = g * s * inv
            chain_ref[1, p : p + 1, :] = c2
            cond = g * n * inv
            here = mz == p + 1
            cond_own = jnp.where(here, cond, cond_own)
            hold = jnp.where(here, c2, hold)
            ginv = jnp.where(here, g, ginv)
        left_cond, left_hold, left_ginv = cond_own, hold, 1.0 / ginv
        cond = part(nz - 1, 5)
        cond_own, hold, ginv = cond, one, one
        for p in range(nz - 1, 0, -1):
            a, m, b, g = part(p, 2), part(p, 3), part(p, 4), part(p - 1, 5)
            at_last = b + cond
            s = m + at_last
            n = a * s + m * at_last
            inv = 1.0 / (n + g * s)
            chain_ref[2, p : p + 1, :] = g * m * inv
            c2 = g * s * inv
            chain_ref[3, p : p + 1, :] = c2
            cond = g * n * inv
            here = mz == p - 1
            cond_own = jnp.where(here, cond, cond_own)
            hold = jnp.where(here, c2, hold)
            ginv = jnp.where(here, g, ginv)
        right_cond, right_hold, right_ginv = cond_own, hold, 1.0 / ginv
        for c, p in ((0, nz - 1), (1, nz - 1), (2, 0), (3, 0)):
            chain_ref[c, p : p + 1, :] = zero
        mine = jnp.where(used, zrec_ref[mz], 1.0)
        big_a = mine[2:3, :] + left_cond
        big_b = mine[4:5, :] + right_cond
        m = mine[3:4, :]
        det_inv = 1.0 / (big_a * m + big_b * m + big_a * big_b)
        f1, f2, f3 = (big_b + m) * det_inv, m * det_inv, (big_a + m) * det_inv
        final_ref[...] = jnp.concatenate(
            [f1, f2, f3, left_ginv, left_hold, right_ginv, right_hold, zero], axis=0
        )
    else:
        mine = jnp.where(used, zrec_ref[mz], 0.0)
        f1, f2, f3, left_ginv, left_hold, right_ginv, right_hold = [
            final_ref[i : i + 1, :] for i in range(7)
        ]
    chain = lambda c, p: chain_ref[c, p : p + 1, :]
    cur, cur_left = zero, zero
    for p in range(nz - 1):
        cur = chain(0, p) * (part(p, 0) + cur) + chain(1, p) * part(p, 1)
        cur_left = jnp.where(mz == p + 1, cur, cur_left)
    cur, cur_right = zero, zero
    for p in range(nz - 1, 0, -1):
        cur = chain(2, p) * (part(p, 1) + cur) + chain(3, p) * part(p, 0)
        cur_right = jnp.where(mz == p - 1, cur, cur_right)
    cur_first = mine[0:1, :] + cur_left
    cur_last = mine[1:2, :] + cur_right
    sol_first = f1 * cur_first + f2 * cur_last
    sol_last = f2 * cur_first + f3 * cur_last
    below = cur_left * left_ginv + left_hold * sol_first
    above = cur_right * right_ginv + right_hold * sol_last
    sol_ref[0:1, :] = sol_first
    sol_ref[CELLS - 1 : CELLS, :] = sol_last
    value = sol_last
    for k in range(CELLS - 2, 0, -1):
        value = alpha_ref[k : k + 1, :] + loc_ref[0, k : k + 1, :] * sol_first + loc_ref[1, k : k + 1, :] * value
        sol_ref[k : k + 1, :] = value
    lanes16 = iota((CELLS, 128), 1) < LINES
    sol = jnp.where(lanes16, sol_ref[...], 0.0) * THETA

    line, lane = iota((128, 128), 0), iota((128, 128), 1)
    picks = [
        one_where(line == lane // 16),
        one_where(line == 8 + lane // 16),
        one_where((line == (lane // 16) * 8) & (lane < 32)),
        one_where((line == (lane // 16) * 8 + 7) & (lane < 32)),
    ]
    keep = iota((CELLS, 128), 1) % 16 == iota((CELLS, 128), 0)
    x_low, x_high, y_low, y_high = [
        jnp.sum(jnp.where(keep, dot(sol, pick), 0.0), axis=0, keepdims=True) for pick in picks
    ]
    own_ref[...] = jnp.concatenate([x_low, x_high] + [zero] * 6, axis=0)

    lane8, row8 = iota((8, 128), 1), iota((8, 128), 0)
    of_row = (lane8 // 8 == row8 // 4) & (lane8 < LINES)
    to_high = one_where((lane >= HIGH_AT) & ((lane - HIGH_AT) // 4 == line % 8) & (line < LINES))
    to_low = one_where(
        (lane >= LOW_AT) & (lane < HIGH_AT) & ((lane - LOW_AT) // 4 == line % 8) & (line < LINES)
    )
    lines_part = dot(jnp.where(of_row, below, 0.0), to_high) + dot(jnp.where(of_row, above, 0.0), to_low)
    from_below = zrec_ref[jnp.maximum(mz - 1, 0)]
    from_above = zrec_ref[jnp.minimum(mz + 1, nz - 1)]
    face = jnp.where(lane8 >= HIGH_AT, from_below, from_above)
    zhalo_ref[...] = jnp.where(lane8 >= LOW_AT, face + THETA * lines_part, 0.0)

    total = zrec_ref[0]
    for p in range(1, nz):
        total = total + zrec_ref[p]
    at = lambda lo: (lane8 >= lo) & (lane8 < lo + 8)
    x_less = pltpu.roll(pltpu.roll(total, 1, 0), 16, 1)
    x_more = pltpu.roll(pltpu.roll(total, 7, 0), 24, 1)
    sums = jnp.where((lane8 >= PART_AT) & (lane8 < PART_AT + 24), total, 0.0)
    sums = jnp.where(at(PART_AT + 24), x_less, sums)
    sums = jnp.where(at(PART_AT + 32), x_more, sums)
    second = iota((2, 128), 0) == 1
    for i in range(nx):
        both = jnp.where(second, sums[i : i + 1, :], 0.0)
        for j in range(ny):
            xmsg_ref[i * ny + j] = both
    here = mx * ny + my

    @pl.when(mx > 0)
    def _():
        xmsg_ref[here - ny, 0:1, :] = x_low

    @pl.when(mx < nx - 1)
    def _():
        xmsg_ref[here + ny, 0:1, :] = x_high

    @pl.when(my > 0)
    def _():
        xmsg_ref[here - 1, 0:1, :] = y_low

    @pl.when(my < ny - 1)
    def _():
        xmsg_ref[here + 1, 0:1, :] = y_high


def scale(sigma_ref, kappa_ref, x):
    return WEIGHT / (sigma_ref[x] + 2.0 * (kappa_ref[0, x] + kappa_ref[1, x] + kappa_ref[2, x]))


def operator(sizes, base, sigma_ref, kappa_ref, xrec_ref, own_ref, zhalo_ref, halos, z_ref, w_ref):
    nx, ny, nz = sizes
    mx, my, mz = lax.axis_index("gx"), lax.axis_index("gy"), lax.axis_index("gz")
    here = mx * ny + my
    sums = xrec_ref[0, 1:2, :]
    for q in range(1, nx * ny):
        sums = sums + xrec_ref[q, 1:2, :]
    lane1 = iota((1, 128), 1)
    coarse = lambda at: jnp.sum(jnp.where(lane1 == at + my, sums, 0.0))
    c_own = coarse(PART_AT + 8)
    c_zlo, c_zhi = coarse(PART_AT), coarse(PART_AT + 16)
    c_ylo, c_yhi = coarse(PART_AT + 7), coarse(PART_AT + 9)
    c_xlo, c_xhi = coarse(PART_AT + 24), coarse(PART_AT + 32)

    lane32, row32 = iota((CY, 128), 1), iota((CY, 128), 0)
    lane8, row8 = iota((8, 128), 1), iota((8, 128), 0)
    wide = lambda row: jnp.where(lane32 // 16 == row32 // 4, row, 0.0)
    thin = lambda row: jnp.where(lane8 // 16 == row8 // 4, row, 0.0)
    left = xrec_ref[jnp.maximum(here - ny, 0), 0:1, :]
    right = xrec_ref[jnp.minimum(here + ny, nx * ny - 1), 0:1, :]
    front = xrec_ref[jnp.maximum(here - 1, 0), 0:1, :]
    back = xrec_ref[jnp.minimum(here + 1, nx * ny - 1), 0:1, :]
    rows = jnp.concatenate(
        [wide(own_ref[0:1, :]), wide(own_ref[1:2, :]), wide(left), wide(right), thin(front), thin(back)],
        axis=0,
    )
    to_cells = one_where(iota((128, 128), 0) % 16 == iota((128, 128), 1) // 8)
    lines = dot(rows, to_cells)
    x_in, x_out, y_in, y_out = [h[...] for h in halos]
    even_x, even_y = mx % 2 == 0, my % 2 == 0
    xlo, xhi = jnp.where(even_x, x_out, x_in), jnp.where(even_x, x_in, x_out)
    ylo, yhi = jnp.where(even_y, y_out, y_in), jnp.where(even_y, y_in, y_out)
    xlo = jnp.where(mx > 0, xlo + lines[64:96] + c_xlo, 0.0)
    xhi = jnp.where(mx < nx - 1, xhi + lines[96:128] + c_xhi, 0.0)
    ylo = jnp.where(my > 0, ylo + lines[128:136] + c_ylo, 0.0)
    yhi = jnp.where(my < ny - 1, yhi + lines[136:144] + c_yhi, 0.0)
    face = zhalo_ref[...]
    high = jnp.where(mz > 0, face + c_zlo, 0.0)
    low = jnp.where(mz < nz - 1, face + c_zhi, 0.0)
    face = jnp.where(lane8 >= HIGH_AT, high, low)
    diagonal = (lane32 == row32 + HIGH_AT) | (lane32 == row32 + LOW_AT)
    spots = jnp.concatenate([jnp.where(diagonal, face[x : x + 1, :], 0.0) for x in range(CX)], axis=0)
    j, k = iota((128, 128), 0), iota((128, 128), 1)
    to_ends = one_where(((j >= HIGH_AT) & (k == 0)) | ((j >= LOW_AT) & (j < HIGH_AT) & (k == CZ - 1)))
    ends = dot(spots, to_ends)

    z = [base(x) + lines[(x // 4) * 32 : (x // 4) * 32 + 32] + c_own for x in range(CX)]
    w = []
    for x in range(CX):
        here_z = z[x]
        z_ref[x] = here_z
        before = z[x - 1] if x > 0 else xlo
        after = z[x + 1] if x < CX - 1 else xhi
        y_less = jnp.where(row32 == 0, ylo[x : x + 1, :], pltpu.roll(here_z, 1, 0))
        y_more = jnp.where(row32 == CY - 1, yhi[x : x + 1, :], pltpu.roll(here_z, CY - 1, 0))
        z_less = jnp.where(lane32 == 0, 0.0, pltpu.roll(here_z, 1, 1))
        z_more = jnp.where(lane32 == CZ - 1, 0.0, pltpu.roll(here_z, CZ - 1, 1))
        twice = 2.0 * here_z
        value = (
            sigma_ref[x] * here_z
            + kappa_ref[0, x] * (twice - before - after)
            + kappa_ref[1, x] * (twice - y_less - y_more)
            + kappa_ref[2, x] * (twice - z_less - z_more - ends[x * 32 : x * 32 + 32])
        )
        w_ref[x] = value
        w.append(value)
    return z, w


def first_kernel(
    sizes, r_ref, sigma_ref, kappa_ref, xrec_ref, own_ref, zhalo_ref, h0, h1, h2, h3,
    loc_ref, spread_ref, z_ref, w_ref, zmsg_ref, alpha_ref, *planes
):
    scales = [scale(sigma_ref, kappa_ref, x) for x in range(CX)]
    base = lambda x: scales[x] * r_ref[x]
    operator(sizes, base, sigma_ref, kappa_ref, xrec_ref, own_ref, zhalo_ref, (h0, h1, h2, h3), z_ref, w_ref)
    field = w_ref[...]
    jac = jnp.stack([scales[x] * w_ref[x] for x in range(CX)], axis=0)
    write_planes(jac, planes)
    rhs = lines_of(field)
    row = lambda a, k: a[k : k + 1, :]
    cur_first, cur = row(rhs, 0), row(rhs, 1)
    zero = jnp.zeros((1, 128), F32)
    for k in (0, CELLS - 1):
        alpha_ref[k : k + 1, :] = zero
    for k in range(1, CELLS - 1):
        alpha_ref[k : k + 1, :] = cur * loc_ref[2, k : k + 1, :]
        cur_first = cur_first + loc_ref[0, k : k + 1, :] * cur
        cur = row(rhs, k + 1) + loc_ref[1, k : k + 1, :] * cur
    write_z_message(
        zmsg_ref, [cur_first, cur], faces_of(jac), spread_ref[...], jnp.sum(field), sizes
    )


def second_kernel(
    sizes, r_ref, w1_ref, sigma_ref, kappa_ref, xrec_ref, own_ref, zhalo_ref, h0, h1, h2, h3,
    z_ref, w_ref, sums_ref
):
    base = lambda x: scale(sigma_ref, kappa_ref, x) * w1_ref[x]
    operator(sizes, base, sigma_ref, kappa_ref, xrec_ref, own_ref, zhalo_ref, (h0, h1, h2, h3), z_ref, w_ref)
    w1, w2, r = w1_ref[...], w_ref[...], r_ref[...]
    lane = iota((1, 128), 1)
    out = jnp.zeros((1, 128), F32)
    for i, product in enumerate((w1 * w1, w1 * w2, w2 * w2, w1 * r, w2 * r)):
        out = jnp.where(lane == i, jnp.sum(product), out)
    sums_ref[...] = out


def end_kernel(all_ref, r_ref, z1_ref, w1_ref, z2_ref, w2_ref, field_ref, res_ref):
    sums = all_ref[0]
    for q in range(1, all_ref.shape[0]):
        sums = sums + all_ref[q]
    lane = iota((1, 128), 1)
    spread = lambda i: jnp.sum(jnp.where(lane == i, sums, 0.0), axis=1, keepdims=True)
    g11, g12, g22, h1, h2 = [spread(i) for i in range(5)]
    inv = 1.0 / (g11 * g22 - g12 * g12)
    y1 = (g22 * h1 - g12 * h2) * inv
    y2 = (g11 * h2 - g12 * h1) * inv
    for x in range(CX):
        field_ref[x] = y1 * z1_ref[x] + y2 * z2_ref[x]
        res_ref[x] = r_ref[x] - y1 * w1_ref[x] - y2 * w2_ref[x]


def call(kernel, out_shapes, scratch=(), name=None, inputs=pltpu.VMEM, semaphores=(), limit=24 << 20):
    vmem = pl.BlockSpec(memory_space=pltpu.VMEM)

    def run(*args):
        return pl.pallas_call(
            kernel,
            out_shape=[jax.ShapeDtypeStruct(s, F32) for s in out_shapes],
            in_specs=[pl.BlockSpec(memory_space=inputs)] * len(args),
            out_specs=[vmem] * len(out_shapes),
            scratch_shapes=[pltpu.VMEM(s, F32) for s in scratch] + list(semaphores),
            compiler_params=pltpu.CompilerParams(vmem_limit_bytes=limit),
            name=name,
        )(*args)

    return run


def shards(sizes, r, sigma, kappa, inverse_rows):
    nx, ny, nz = sizes
    field, plane, tile, coarse = (CX, CY, CZ), (CY, CZ), (8, 128), (CELLS, 128)
    planes = [plane, plane, tile, tile]
    to_z, to_xy = (nz, 8, 128), (nx * ny, 2, 128)

    def swaps(n, first):
        pairs = [(i, i + 1) for i in range(first, n - 1, 2)]
        return pairs + [(b, a) for a, b in pairs]

    def halo(parts):
        x_in, x_out, y_in, y_out = parts
        return (
            lax.ppermute(x_in, "gx", swaps(nx, 0)),
            lax.ppermute(x_out, "gx", swaps(nx, 1)),
            lax.ppermute(y_in, "gy", swaps(ny, 0)),
            lax.ppermute(y_out, "gy", swaps(ny, 1)),
        )

    def along_z(message):
        return lax.all_to_all(message, "gz", split_axis=0, concat_axis=0, tiled=True)

    def along_xy(message):
        return lax.all_to_all(message, ("gx", "gy"), split_axis=0, concat_axis=0, tiled=True)

    bind = lambda kernel, *a: functools.partial(kernel, sizes, *a)
    zmsg, loc, alpha, spread, *sides = call(
        bind(begin_kernel), [to_z, (3, *coarse), coarse, tile, *planes],
        [field, field, (3, *field), tile], "begin", pltpu.HBM, [pltpu.SemaphoreType.DMA((4,))], 55100 << 10,
    )(r, sigma, kappa, inverse_rows)
    zrec = along_z(zmsg)
    halos = halo(sides)
    xmsg, own, zhalo, chain, final = call(
        bind(chain_kernel, True), [to_xy, tile, tile, (4, nz, 128), tile], [coarse], "lines_first"
    )(zrec, loc, alpha, *halos)
    xrec = along_xy(xmsg)
    z1, w1, zmsg, alpha, *sides = call(
        bind(first_kernel), [field, field, to_z, coarse, *planes], name="operator_first"
    )(r, sigma, kappa, xrec, own, zhalo, *halos, loc, spread)
    zrec = along_z(zmsg)
    halos = halo(sides)
    xmsg, own, zhalo = call(
        bind(chain_kernel, False), [to_xy, tile, tile], [coarse], "lines_second"
    )(zrec, loc, alpha, *halos, chain, final)
    xrec = along_xy(xmsg)
    z2, w2, sums = call(bind(second_kernel), [field, field, (1, 128)], name="operator_second")(
        r, w1, sigma, kappa, xrec, own, zhalo, *halos
    )
    sums = jnp.sum(along_z(jnp.broadcast_to(sums[None], (nz, 1, 128))), axis=0)
    sums = along_xy(jnp.broadcast_to(sums[None], (nx * ny, 1, 128)))
    return tuple(call(end_kernel, [field, field], name="end")(sums, r, z1, w1, z2, w2))


def solution(mesh):
    sizes = (mesh.shape["gx"], mesh.shape["gy"], mesh.shape["gz"])
    spec = P("gx", "gy", "gz")

    def run(r, sigma, kappa, inverse):
        return shards(sizes, r, sigma, kappa, inverse.reshape(8, 128))

    return jax.shard_map(
        run,
        mesh=mesh,
        in_specs=(spec, spec, P(None, "gx", "gy", "gz"), P(("gx", "gy", "gz"), None)),
        out_specs=(spec, spec),
        check_vma=False,
    )
```

```python
import functools

import jax
import jax.numpy as jnp
from jax import lax
from jax.experimental import pallas as pl
from jax.experimental.pallas import tpu as pltpu
from jax.sharding import PartitionSpec as P

CX, CY, CZ = 8, 32, 128
CELLS = 16
LINES = 16
THETA = 1.0 / 128.0
WEIGHT = 0.6
PART_AT, LOW_AT, HIGH_AT = 32, 64, 96
HIGHEST = lax.Precision.HIGHEST
F32 = jnp.float32


def iota(shape, dim):
    return lax.broadcasted_iota(jnp.int32, shape, dim)


def dot(a, b):
    return lax.dot_general(
        a, b, (((1,), (0,)), ((), ())), precision=HIGHEST, preferred_element_type=F32
    )


def dot_t(a, b):
    return lax.dot_general(
        a, b, (((1,), (1,)), ((), ())), precision=HIGHEST, preferred_element_type=F32
    )


def one_where(cond):
    return jnp.where(cond, 1.0, 0.0).astype(F32)


def lines_of(field):
    low = (field[0] + field[1]) + (field[2] + field[3])
    high = (field[4] + field[5]) + (field[6] + field[7])
    stacked = jnp.concatenate([low, high], axis=0)
    by_line = one_where(iota((128, 64), 1) // 4 == iota((128, 64), 0))
    by_cell = one_where(iota((CELLS, 128), 1) // 8 == iota((CELLS, 128), 0))
    return dot_t(by_cell, dot(by_line, stacked))


def faces_of(field):
    lane, row = iota((CX, CY, 128), 2), iota((CX, CY, 128), 1)
    low = jnp.where(lane == LOW_AT + row, field[:, :, 0:1], 0.0)
    both = jnp.where(lane == HIGH_AT + row, field[:, :, CZ - 1 : CZ], low)
    return jnp.sum(both, axis=1)


def write_z_message(zmsg_ref, rows, faces, spread_inverse, total, sizes):
    lane = iota((8, 128), 1)
    zero = jnp.zeros((1, 128), F32)
    head = jnp.concatenate(rows + [zero] * (8 - len(rows)), axis=0)
    base = jnp.where(lane < LINES, head, faces)
    mine = spread_inverse * total
    inside = (lane >= PART_AT) & (lane < PART_AT + 24)
    for p in range(sizes[2]):
        moved = pltpu.roll(mine, (PART_AT + 8 - 8 * p) % 128, 1)
        zmsg_ref[p] = jnp.where(inside, moved, base)


def write_planes(field, planes):
    xlo, xhi, ylo, yhi = planes
    xlo[...] = field[0]
    xhi[...] = field[CX - 1]
    ylo[...] = field[:, 0, :]
    yhi[...] = field[:, CY - 1, :]


def begin_kernel(
    sizes, r_hbm, sigma_hbm, kappa_hbm, inv_hbm,
    zmsg_ref, loc_ref, alpha_ref, spread_ref, xlo, xhi, ylo, yhi,
    r_ref, sigma_ref, kappa_ref, inv_ref, sems
):
    pairs = ((kappa_hbm, kappa_ref), (sigma_hbm, sigma_ref), (r_hbm, r_ref), (inv_hbm, inv_ref))
    copies = [pltpu.make_async_copy(a, b, sems.at[i]) for i, (a, b) in enumerate(pairs)]
    for copy in copies:
        copy.start()
    for copy in copies:
        copy.wait()
    r, sigma = r_ref[...], sigma_ref[...]
    kx, ky, kz = kappa_ref[0], kappa_ref[1], kappa_ref[2]
    jac = r * (WEIGHT / (sigma + 2.0 * (kx + ky + kz)))
    write_planes(jac, (xlo, xhi, ylo, yhi))
    unused = iota((CELLS, 128), 1) >= LINES
    e = jnp.where(unused, 1.0, lines_of(sigma))
    g = jnp.where(unused, 1.0, lines_of(kz) * 0.125)
    rhs = lines_of(r)
    row = lambda a, k: a[k : k + 1, :]
    first, mid, last = row(e, 0), row(g, 0), row(e, 1)
    cur_first, cur = row(rhs, 0), row(rhs, 1)
    zero = jnp.zeros((1, 128), F32)
    for c in range(3):
        for k in (0, CELLS - 1):
            loc_ref[c, k : k + 1, :] = zero
    for k in (0, CELLS - 1):
        alpha_ref[k : k + 1, :] = zero
    for k in range(1, CELLS - 1):
        inv = 1.0 / (mid + last + row(g, k))
        mu, gam = mid * inv, row(g, k) * inv
        loc_ref[0, k : k + 1, :] = mu
        loc_ref[1, k : k + 1, :] = gam
        loc_ref[2, k : k + 1, :] = inv
        alpha_ref[k : k + 1, :] = cur * inv
        first = first + mu * last
        mid = mu * row(g, k)
        last = row(e, k + 1) + gam * last
        cur_first = cur_first + mu * cur
        cur = row(rhs, k + 1) + gam * cur
    move = one_where((iota((128, 128), 0) % 16) * 8 + iota((128, 128), 0) // 16 == iota((128, 128), 1))
    spread_inverse = dot(inv_ref[...], move)
    spread_ref[...] = spread_inverse
    rows = [cur_first, cur, first, mid, last, row(g, CELLS - 1)]
    write_z_message(zmsg_ref, rows, faces_of(jac), spread_inverse, jnp.sum(r), sizes)


def solve_chain(sizes, fresh, zrec_ref, loc_ref, alpha_ref, chain_ref, final_ref, sol_ref):
    nz = sizes[2]
    mz = lax.axis_index("gz")
    used = iota((8, 128), 1) < LINES
    tiles = [jnp.where(used, zrec_ref[p], 1.0) for p in range(nz)]
    part = lambda p, i: tiles[p][i : i + 1, :]
    zero = jnp.zeros((1, 128), F32)

    if fresh:
        one = zero + 1.0
        cond, cond_own, hold, ginv = zero, zero, one, one
        for p in range(nz - 1):
            a, m, b, g = part(p, 2), part(p, 3), part(p, 4), part(p, 5)
            at_first = a + cond
            s = m + at_first
            n = b * s + m * at_first
            inv = 1.0 / (n + g * s)
            chain_ref[0, p : p + 1, :] = g * m * inv
            c2 = g * s * inv
            chain_ref[1, p : p + 1, :] = c2
            cond = g * n * inv
            here = mz == p + 1
            cond_own = jnp.where(here, cond, cond_own)
            hold = jnp.where(here, c2, hold)
            ginv = jnp.where(here, g, ginv)
        left_cond, left_hold, left_ginv = cond_own, hold, 1.0 / ginv
        cond = part(nz - 1, 5)
        cond_own, hold, ginv = cond, one, one
        for p in range(nz - 1, 0, -1):
            a, m, b, g = part(p, 2), part(p, 3), part(p, 4), part(p - 1, 5)
            at_last = b + cond
            s = m + at_last
            n = a * s + m * at_last
            inv = 1.0 / (n + g * s)
            chain_ref[2, p : p + 1, :] = g * m * inv
            c2 = g * s * inv
            chain_ref[3, p : p + 1, :] = c2
            cond = g * n * inv
            here = mz == p - 1
            cond_own = jnp.where(here, cond, cond_own)
            hold = jnp.where(here, c2, hold)
            ginv = jnp.where(here, g, ginv)
        right_cond, right_hold, right_ginv = cond_own, hold, 1.0 / ginv
        for c, p in ((0, nz - 1), (1, nz - 1), (2, 0), (3, 0)):
            chain_ref[c, p : p + 1, :] = zero
        mine = jnp.where(used, zrec_ref[mz], 1.0)
        big_a = mine[2:3, :] + left_cond
        big_b = mine[4:5, :] + right_cond
        m = mine[3:4, :]
        det_inv = 1.0 / (big_a * m + big_b * m + big_a * big_b)
        f1, f2, f3 = (big_b + m) * det_inv, m * det_inv, (big_a + m) * det_inv
        final_ref[...] = jnp.concatenate(
            [f1, f2, f3, left_ginv, left_hold, right_ginv, right_hold, zero], axis=0
        )
    else:
        mine = jnp.where(used, zrec_ref[mz], 0.0)
        f1, f2, f3, left_ginv, left_hold, right_ginv, right_hold = [
            final_ref[i : i + 1, :] for i in range(7)
        ]
    chain = lambda c, p: chain_ref[c, p : p + 1, :]
    cur, cur_left = zero, zero
    for p in range(nz - 1):
        cur = chain(0, p) * (part(p, 0) + cur) + chain(1, p) * part(p, 1)
        cur_left = jnp.where(mz == p + 1, cur, cur_left)
    cur, cur_right = zero, zero
    for p in range(nz - 1, 0, -1):
        cur = chain(2, p) * (part(p, 1) + cur) + chain(3, p) * part(p, 0)
        cur_right = jnp.where(mz == p - 1, cur, cur_right)
    cur_first = mine[0:1, :] + cur_left
    cur_last = mine[1:2, :] + cur_right
    sol_first = f1 * cur_first + f2 * cur_last
    sol_last = f2 * cur_first + f3 * cur_last
    below = cur_left * left_ginv + left_hold * sol_first
    above = cur_right * right_ginv + right_hold * sol_last
    sol_ref[0:1, :] = sol_first
    sol_ref[CELLS - 1 : CELLS, :] = sol_last
    value = sol_last
    for k in range(CELLS - 2, 0, -1):
        value = alpha_ref[k : k + 1, :] + loc_ref[0, k : k + 1, :] * sol_first + loc_ref[1, k : k + 1, :] * value
        sol_ref[k : k + 1, :] = value
    lanes16 = iota((CELLS, 128), 1) < LINES
    sol = jnp.where(lanes16, sol_ref[...], 0.0) * THETA

    line, lane = iota((128, 128), 0), iota((128, 128), 1)
    picks = [
        one_where(line == lane // 16),
        one_where(line == 8 + lane // 16),
        one_where((line == (lane // 16) * 8) & (lane < 32)),
        one_where((line == (lane // 16) * 8 + 7) & (lane < 32)),
    ]
    keep = iota((CELLS, 128), 1) % 16 == iota((CELLS, 128), 0)
    x_low, x_high, y_low, y_high = [
        jnp.sum(jnp.where(keep, dot(sol, pick), 0.0), axis=0, keepdims=True) for pick in picks
    ]

    lane8, row8 = iota((8, 128), 1), iota((8, 128), 0)
    of_row = (lane8 // 8 == row8 // 4) & (lane8 < LINES)
    to_high = one_where((lane >= HIGH_AT) & ((lane - HIGH_AT) // 4 == line % 8) & (line < LINES))
    to_low = one_where(
        (lane >= LOW_AT) & (lane < HIGH_AT) & ((lane - LOW_AT) // 4 == line % 8) & (line < LINES)
    )
    lines_part = dot(jnp.where(of_row, below, 0.0), to_high) + dot(jnp.where(of_row, above, 0.0), to_low)
    from_below = zrec_ref[jnp.maximum(mz - 1, 0)]
    from_above = zrec_ref[jnp.minimum(mz + 1, nz - 1)]
    face = jnp.where(lane8 >= HIGH_AT, from_below, from_above)
    zhalo = jnp.where(lane8 >= LOW_AT, face + THETA * lines_part, 0.0)
    return x_low, x_high, y_low, y_high, zhalo


def first_lines_kernel(
    sizes, zrec_ref, loc_ref, alpha_ref, h2, h3, xmsg_ref, own_ref, zhalo_ref, chain_ref, final_ref, sol_ref
):
    nx, ny, nz = sizes
    mx, my = lax.axis_index("gx"), lax.axis_index("gy")
    x_low, x_high, y_low, y_high, zhalo = solve_chain(
        sizes, True, zrec_ref, loc_ref, alpha_ref, chain_ref, final_ref, sol_ref
    )
    zero = jnp.zeros((1, 128), F32)
    lane8 = iota((8, 128), 1)
    own_ref[...] = jnp.concatenate([x_low, x_high] + [zero] * 6, axis=0)
    zhalo_ref[...] = zhalo

    total = zrec_ref[0]
    for p in range(1, nz):
        total = total + zrec_ref[p]
    at = lambda lo: (lane8 >= lo) & (lane8 < lo + 8)
    x_less = pltpu.roll(pltpu.roll(total, 1, 0), 16, 1)
    x_more = pltpu.roll(pltpu.roll(total, 7, 0), 24, 1)
    sums = jnp.where((lane8 >= PART_AT) & (lane8 < PART_AT + 24), total, 0.0)
    sums = jnp.where(at(PART_AT + 24), x_less, sums)
    sums = jnp.where(at(PART_AT + 32), x_more, sums)
    second = iota((2, 128), 0) == 1
    for i in range(nx):
        both = jnp.where(second, sums[i : i + 1, :], 0.0)
        for j in range(ny):
            xmsg_ref[i * ny + j] = both
    here = mx * ny + my

    @pl.when(mx > 0)
    def _():
        xmsg_ref[here - ny, 0:1, :] = x_low

    @pl.when(mx < nx - 1)
    def _():
        xmsg_ref[here + ny, 0:1, :] = x_high

    @pl.when(my > 0)
    def _():
        xmsg_ref[here - 1, 0:1, :] = y_low

    @pl.when(my < ny - 1)
    def _():
        xmsg_ref[here + 1, 0:1, :] = y_high


def scale(sigma_ref, kappa_ref, x):
    return WEIGHT / (sigma_ref[x] + 2.0 * (kappa_ref[0, x] + kappa_ref[1, x] + kappa_ref[2, x]))


def ends_of(face):
    lane32, row32 = iota((CY, 128), 1), iota((CY, 128), 0)
    diagonal = (lane32 == row32 + HIGH_AT) | (lane32 == row32 + LOW_AT)
    spots = jnp.concatenate([jnp.where(diagonal, face[x : x + 1, :], 0.0) for x in range(CX)], axis=0)
    j, k = iota((128, 128), 0), iota((128, 128), 1)
    to_ends = one_where(((j >= HIGH_AT) & (k == 0)) | ((j >= LOW_AT) & (j < HIGH_AT) & (k == CZ - 1)))
    return dot(spots, to_ends)


def apply_operator(z, xlo, xhi, ylo, yhi, ends, sigma_ref, kappa_ref, w_ref):
    lane32, row32 = iota((CY, 128), 1), iota((CY, 128), 0)
    for x in range(CX):
        here_z = z[x]
        before = z[x - 1] if x > 0 else xlo
        after = z[x + 1] if x < CX - 1 else xhi
        y_less = jnp.where(row32 == 0, ylo[x : x + 1, :], pltpu.roll(here_z, 1, 0))
        y_more = jnp.where(row32 == CY - 1, yhi[x : x + 1, :], pltpu.roll(here_z, CY - 1, 0))
        z_less = jnp.where(lane32 == 0, 0.0, pltpu.roll(here_z, 1, 1))
        z_more = jnp.where(lane32 == CZ - 1, 0.0, pltpu.roll(here_z, CZ - 1, 1))
        twice = 2.0 * here_z
        w_ref[x] = (
            sigma_ref[x] * here_z
            + kappa_ref[0, x] * (twice - before - after)
            + kappa_ref[1, x] * (twice - y_less - y_more)
            + kappa_ref[2, x] * (twice - z_less - z_more - ends[x * 32 : x * 32 + 32])
        )


def wide(row):
    return jnp.where(iota((CY, 128), 1) // 16 == iota((CY, 128), 0) // 4, row, 0.0)


def thin(row):
    return jnp.where(iota((CX, 128), 1) // 16 == iota((CX, 128), 0) // 4, row, 0.0)


def to_cells():
    return one_where(iota((128, 128), 0) % 16 == iota((128, 128), 1) // 8)


def full_direction(sizes, base, xrec_ref, own_ref, zhalo_ref, halos, z_ref):
    nx, ny, nz = sizes
    mx, my, mz = lax.axis_index("gx"), lax.axis_index("gy"), lax.axis_index("gz")
    here = mx * ny + my
    sums = xrec_ref[0, 1:2, :]
    for q in range(1, nx * ny):
        sums = sums + xrec_ref[q, 1:2, :]
    lane1 = iota((1, 128), 1)
    coarse = lambda at: jnp.sum(jnp.where(lane1 == at + my, sums, 0.0))
    c_own = coarse(PART_AT + 8)
    c_zlo, c_zhi = coarse(PART_AT), coarse(PART_AT + 16)
    c_ylo, c_yhi = coarse(PART_AT + 7), coarse(PART_AT + 9)
    c_xlo, c_xhi = coarse(PART_AT + 24), coarse(PART_AT + 32)

    left = xrec_ref[jnp.maximum(here - ny, 0), 0:1, :]
    right = xrec_ref[jnp.minimum(here + ny, nx * ny - 1), 0:1, :]
    front = xrec_ref[jnp.maximum(here - 1, 0), 0:1, :]
    back = xrec_ref[jnp.minimum(here + 1, nx * ny - 1), 0:1, :]
    rows = jnp.concatenate(
        [wide(own_ref[0:1, :]), wide(own_ref[1:2, :]), wide(left), wide(right), thin(front), thin(back)],
        axis=0,
    )
    lines = dot(rows, to_cells())
    xlo, xhi, ylo, yhi = [h[...] for h in halos]
    xlo = jnp.where(mx > 0, xlo + lines[64:96] + c_xlo, 0.0)
    xhi = jnp.where(mx < nx - 1, xhi + lines[96:128] + c_xhi, 0.0)
    ylo = jnp.where(my > 0, ylo + lines[128:136] + c_ylo, 0.0)
    yhi = jnp.where(my < ny - 1, yhi + lines[136:144] + c_yhi, 0.0)
    face = zhalo_ref[...]
    high = jnp.where(mz > 0, face + c_zlo, 0.0)
    low = jnp.where(mz < nz - 1, face + c_zhi, 0.0)
    ends = ends_of(jnp.where(iota((8, 128), 1) >= HIGH_AT, high, low))
    z = [base(x) + lines[(x // 4) * 32 : (x // 4) * 32 + 32] + c_own for x in range(CX)]
    for x in range(CX):
        z_ref[x] = z[x]
    return z, xlo, xhi, ylo, yhi, ends


def first_kernel(
    sizes, r_ref, sigma_ref, kappa_ref, xrec_ref, own_ref, zhalo_ref, h0, h1, h2, h3,
    loc_ref, spread_ref, z_ref, w_ref, jac_ref, zmsg_ref, alpha_ref
):
    scales = [scale(sigma_ref, kappa_ref, x) for x in range(CX)]
    base = lambda x: scales[x] * r_ref[x]
    parts = full_direction(sizes, base, xrec_ref, own_ref, zhalo_ref, (h0, h1, h2, h3), z_ref)
    apply_operator(*parts, sigma_ref, kappa_ref, w_ref)
    field = w_ref[...]
    for x in range(CX):
        jac_ref[x] = scales[x] * w_ref[x]
    rhs = lines_of(field)
    row = lambda a, k: a[k : k + 1, :]
    cur_first, cur = row(rhs, 0), row(rhs, 1)
    zero = jnp.zeros((1, 128), F32)
    for k in (0, CELLS - 1):
        alpha_ref[k : k + 1, :] = zero
    for k in range(1, CELLS - 1):
        alpha_ref[k : k + 1, :] = cur * loc_ref[2, k : k + 1, :]
        cur_first = cur_first + loc_ref[0, k : k + 1, :] * cur
        cur = row(rhs, k + 1) + loc_ref[1, k : k + 1, :] * cur
    write_z_message(
        zmsg_ref, [cur_first, cur], faces_of(jac_ref[...]), spread_ref[...], jnp.sum(field), sizes
    )


def second_lines_kernel(
    sizes, zrec_ref, loc_ref, alpha_ref, chain_ref, final_ref, jac_ref,
    part_ref, zhalo_ref, z_ref, xlo, xhi, ylo, yhi, sol_ref
):
    x_low, x_high, _, _, zhalo = solve_chain(
        sizes, False, zrec_ref, loc_ref, alpha_ref, chain_ref, final_ref, sol_ref
    )
    zhalo_ref[...] = zhalo
    lines = dot(jnp.concatenate([wide(x_low), wide(x_high)], axis=0), to_cells())
    for x in range(CX):
        z_ref[x] = jac_ref[x] + lines[(x // 4) * 32 : (x // 4) * 32 + 32]
    write_planes(z_ref[...], (xlo, xhi, ylo, yhi))
    total = zrec_ref[0]
    for p in range(1, sizes[2]):
        total = total + zrec_ref[p]
    part_ref[...] = total


FACES = range(1, 7)
TERMS = (
    [("g11", -1, -1), ("g12", -1, -1), ("g22", -1, -1), ("h1", -1, -1), ("h2", -1, -1)]
    + [(name, j, -1) for name in ("h2", "g12", "g22") for j in range(7)]
    + [("g22", 0, j) for j in range(7)]
    + [("g22", j, j) for j in FACES]
    + [("g22", j, k) for j in FACES for k in FACES if j < k and (j - 1) // 2 != (k - 1) // 2]
)
NAMES = ("g11", "g12", "g22", "h1", "h2")
TERMS_AT = 72


def second_kernel(
    sizes, r_ref, w1_ref, sigma_ref, kappa_ref, z_ref, zhalo_ref, part_ref, h0, h1, h2, h3,
    w_ref, xmsg_ref, terms_ref
):
    nx, ny, nz = sizes
    mx, my, mz = lax.axis_index("gx"), lax.axis_index("gy"), lax.axis_index("gz")
    xlo = jnp.where(mx > 0, h0[...], 0.0)
    xhi = jnp.where(mx < nx - 1, h1[...], 0.0)
    ylo = jnp.where(my > 0, h2[...], 0.0)
    yhi = jnp.where(my < ny - 1, h3[...], 0.0)
    face = zhalo_ref[...]
    high, low = jnp.where(mz > 0, face, 0.0), jnp.where(mz < nz - 1, face, 0.0)
    ends = ends_of(jnp.where(iota((8, 128), 1) >= HIGH_AT, high, low))
    apply_operator([z_ref[x] for x in range(CX)], xlo, xhi, ylo, yhi, ends, sigma_ref, kappa_ref, w_ref)

    r, w1, w2, sigma = r_ref[...], w1_ref[...], w_ref[...], sigma_ref[...]
    kz = kappa_ref[2]
    rows = lambda a: jnp.sum(jnp.sum(a, axis=0), axis=0, keepdims=True)
    lane1 = iota((1, 128), 1)
    pick = lambda profile, face: jnp.where(lane1 == (0 if face == 5 else CZ - 1), profile, 0.0)
    low_row = lambda a: jnp.sum(a, axis=0, keepdims=True)
    partner = {"h2": r, "g12": w1, "g22": w2}
    partner_ref = {"h2": r_ref, "g12": w1_ref, "g22": w_ref}
    z_profiles = {name: rows(kz * f) for name, f in partner.items()}
    z_sigma, z_self = rows(kz * sigma), rows(kz * kz)

    def plane(ref, f):
        if f < 3:
            return ref[0 if f == 1 else CX - 1]
        return ref[:, 0 if f == 3 else CY - 1, :]

    face_weight = {f: plane(kappa_ref.at[(f - 1) // 2], f) for f in range(1, 5)}

    def on_face(f, other):
        return low_row(face_weight[f] * plane(other, f))

    def term(name, j, k):
        if j == -1:
            a, b = {"g11": (w1, w1), "g12": (w1, w2), "g22": (w2, w2), "h1": (w1, r), "h2": (w2, r)}[name]
            return rows(a * b)
        if k == -1:
            twice = 2.0 if name == "g22" else 1.0
            if j == 0:
                return twice * rows(sigma * partner[name])
            if j > 4:
                return twice * pick(z_profiles[name], j)
            return twice * on_face(j, partner_ref[name])
        if j == 0:
            if k == 0:
                return rows(sigma * sigma)
            return 2.0 * (pick(z_sigma, k) if k > 4 else on_face(k, sigma_ref))
        if j == k:
            return pick(z_self, j) if j > 4 else on_face(j, kappa_ref.at[(j - 1) // 2])
        if k > 4:
            return 2.0 * pick(on_face(j, kappa_ref.at[2]), k)
        x, y = 0 if j == 1 else CX - 1, 0 if k == 3 else CY - 1
        return 2.0 * kappa_ref[0, x, y : y + 1, :] * kappa_ref[1, x, y : y + 1, :]

    for i, (name, j, k) in enumerate(TERMS):
        terms_ref[i : i + 1, :] = term(name, j, k)
    for i in range(len(TERMS), 128):
        if i % 8 == 0:
            terms_ref[i : i + 8, :] = jnp.zeros((8, 128), F32)
        elif i == len(TERMS):
            stop = -(-i // 8) * 8
            terms_ref[i:stop, :] = jnp.zeros((stop - i, 128), F32)
    poly = dot_t(jnp.full((8, 128), 1.0, F32), terms_ref[...])[0:1, :]
    part = part_ref[...]
    lane8 = iota((8, 128), 1)
    part = jnp.where((lane8 >= PART_AT) & (lane8 < PART_AT + 24), part, 0.0)
    at = lambda i, lane: pltpu.roll(part, (lane - PART_AT) % 128, 1)[i : i + 1, :]
    upper = at(0, 0) + at(1, 24) + at(2, 48) + at(3, 72) + at(4, 96)
    lower = at(5, 0) + at(6, 24) + at(7, 48) + pltpu.roll(poly, TERMS_AT, 1)
    both = jnp.concatenate([upper, lower], axis=0)
    for q in range(nx * ny):
        xmsg_ref[q] = both


def plane_kernel(sizes, xrec_ref, sums_ref, own_ref, flat_ref):
    nx, ny, nz = sizes
    mx, my, mz = lax.axis_index("gx"), lax.axis_index("gy"), lax.axis_index("gz")
    count = nx * ny
    total = xrec_ref[0]
    for q in range(count):
        flat_ref[q : q + 1, :] = xrec_ref[q, 1:2, :]
        if q > 0:
            total = total + xrec_ref[q]
    lane, row = iota((count, 128), 1), iota((count, 128), 0)
    tx, ty = row // ny, row % ny

    def value(qx, qy, dz, valid):
        at = jnp.where(qx < 5, qx * 24, (qx - 5) * 24) + 8 + 8 * dz + qy
        chosen = jnp.where(qx < 5, total[0:1, :], total[1:2, :])
        return jnp.sum(jnp.where((lane == at) & valid, chosen, 0.0), axis=1, keepdims=True)

    always = row >= 0
    c = value(tx, ty, 0, always)
    near = [
        value(tx - 1, ty, 0, tx > 0),
        value(tx + 1, ty, 0, tx < nx - 1),
        value(tx, ty - 1, 0, ty > 0),
        value(tx, ty + 1, 0, ty < ny - 1),
        value(tx, ty, -1, always & (mz > 0)),
        value(tx, ty, 1, always & (mz < nz - 1)),
    ]
    v = [c] + [c - n for n in near]
    first = jnp.where(lane < 0, 1.0, 0.0)
    second = first
    for j in range(-1, 7):
        amount = 1.0 if j == -1 else v[j]
        is_first = lane < 0
        is_second = is_first
        for i, (_, a, b) in enumerate(TERMS):
            if a == j:
                is_first = is_first | (lane == TERMS_AT + i)
            if b == j:
                is_second = is_second | (lane == TERMS_AT + i)
        first = jnp.where(is_first, amount, first)
        second = jnp.where(is_second, amount, second)
    terms = jnp.where(lane >= TERMS_AT, flat_ref[...], 0.0)
    added = jnp.sum(terms * first * second, axis=0, keepdims=True)
    lane1 = iota((1, 128), 1)
    out = jnp.zeros((1, 128), F32)
    for n, name in enumerate(NAMES):
        mask = lane1 < 0
        for i, (of, _, _) in enumerate(TERMS):
            if of == name:
                mask = mask | (lane1 == TERMS_AT + i)
        out = jnp.where(lane1 == n, jnp.sum(jnp.where(mask, added, 0.0), axis=1, keepdims=True), out)
    sums_ref[...] = out
    mine = row == mx * ny + my
    for j in range(7):
        own = jnp.sum(jnp.where(mine & (lane == 0), v[j], 0.0))
        own_ref[j : j + 1, :] = jnp.full((1, 128), own, F32)
    own_ref[7:8, :] = jnp.zeros((1, 128), F32)


def end_kernel(all_ref, own_ref, r_ref, sigma_ref, kappa_ref, z1_ref, w1_ref, z2_ref, w2_ref, field_ref, res_ref):
    sums = all_ref[0]
    for q in range(1, all_ref.shape[0]):
        sums = sums + all_ref[q]
    lane = iota((1, 128), 1)
    spread = lambda i: jnp.sum(jnp.where(lane == i, sums, 0.0), axis=1, keepdims=True)
    g11, g12, g22, h1, h2 = [spread(i) for i in range(5)]
    inv = 1.0 / (g11 * g22 - g12 * g12)
    y1 = (g22 * h1 - g12 * h2) * inv
    y2 = (g11 * h2 - g12 * h1) * inv
    c, xlo, xhi, ylo, yhi, zlo, zhi = [own_ref[j : j + 1, :] for j in range(7)]
    lane32, row32 = iota((CY, 128), 1), iota((CY, 128), 0)
    on_y = jnp.where(row32 == 0, ylo, jnp.where(row32 == CY - 1, yhi, 0.0))
    on_z = jnp.where(lane32 == 0, zlo, jnp.where(lane32 == CZ - 1, zhi, 0.0))
    for x in range(CX):
        w2 = w2_ref[x] + sigma_ref[x] * c + kappa_ref[1, x] * on_y + kappa_ref[2, x] * on_z
        if x == 0:
            w2 = w2 + kappa_ref[0, x] * xlo
        if x == CX - 1:
            w2 = w2 + kappa_ref[0, x] * xhi
        field_ref[x] = y1 * z1_ref[x] + y2 * (z2_ref[x] + c)
        res_ref[x] = r_ref[x] - y1 * w1_ref[x] - y2 * w2


def call(kernel, out_shapes, scratch=(), name=None, inputs=pltpu.VMEM, semaphores=(), limit=24 << 20):
    vmem = pl.BlockSpec(memory_space=pltpu.VMEM)

    def run(*args):
        return pl.pallas_call(
            kernel,
            out_shape=[jax.ShapeDtypeStruct(s, F32) for s in out_shapes],
            in_specs=[pl.BlockSpec(memory_space=inputs)] * len(args),
            out_specs=[vmem] * len(out_shapes),
            scratch_shapes=[pltpu.VMEM(s, F32) for s in scratch] + list(semaphores),
            compiler_params=pltpu.CompilerParams(vmem_limit_bytes=limit),
            name=name,
        )(*args)

    return run


def shards(sizes, r, sigma, kappa, inverse_rows):
    nx, ny, nz = sizes
    field, plane, tile, coarse = (CX, CY, CZ), (CY, CZ), (8, 128), (CELLS, 128)
    planes = [plane, plane, tile, tile]
    to_z, to_xy = (nz, 8, 128), (nx * ny, 2, 128)

    def halo(parts):
        xlo, xhi, ylo, yhi = parts
        up = lambda n: [(i, (i + 1) % n) for i in range(n)]
        down = lambda n: [((i + 1) % n, i) for i in range(n)]
        return (
            lax.ppermute(xhi, "gx", up(nx)),
            lax.ppermute(xlo, "gx", down(nx)),
            lax.ppermute(yhi, "gy", up(ny)),
            lax.ppermute(ylo, "gy", down(ny)),
        )

    def along_z(message):
        return lax.all_to_all(message, "gz", split_axis=0, concat_axis=0, tiled=True)

    def along_xy(message):
        return lax.all_to_all(message, ("gx", "gy"), split_axis=0, concat_axis=0, tiled=True)

    bind = lambda kernel, *a: functools.partial(kernel, sizes, *a)
    zmsg, loc, alpha, spread, *sides = call(
        bind(begin_kernel), [to_z, (3, *coarse), coarse, tile, *planes],
        [field, field, (3, *field), tile], "begin", pltpu.HBM, [pltpu.SemaphoreType.DMA((4,))], 55100 << 10,
    )(r, sigma, kappa, inverse_rows)
    zrec = along_z(zmsg)
    halos = halo(sides)
    xmsg, own, zhalo, chain, final = call(
        bind(first_lines_kernel), [to_xy, tile, tile, (4, nz, 128), tile], [coarse], "lines_first"
    )(zrec, loc, alpha, *halos[2:])
    xrec = along_xy(xmsg)
    z1, w1, jac, zmsg, alpha = call(
        bind(first_kernel), [field, field, field, to_z, coarse], name="operator_first"
    )(r, sigma, kappa, xrec, own, zhalo, *halos, loc, spread)
    zrec = along_z(zmsg)
    part, zhalo, z2, *sides = call(
        bind(second_lines_kernel), [tile, tile, field, *planes], [coarse], "lines_second"
    )(zrec, loc, alpha, chain, final, jac)
    halos = halo(sides)
    w2, xmsg = call(bind(second_kernel), [field, to_xy], [(128, 128)], "operator_second")(
        r, w1, sigma, kappa, z2, zhalo, part, *halos
    )
    xrec = along_xy(xmsg)
    sums, values = call(bind(plane_kernel), [(1, 128), tile], [(nx * ny, 128)], "plane")(xrec)
    sums = along_z(jnp.broadcast_to(sums[None], (nz, 1, 128)))
    return tuple(
        call(end_kernel, [field, field], name="end")(sums, values, r, sigma, kappa, z1, w1, z2, w2)
    )


def solution(mesh):
    sizes = (mesh.shape["gx"], mesh.shape["gy"], mesh.shape["gz"])
    spec = P("gx", "gy", "gz")

    def run(r, sigma, kappa, inverse):
        return shards(sizes, r, sigma, kappa, inverse.reshape(8, 128))

    return jax.shard_map(
        run,
        mesh=mesh,
        in_specs=(spec, spec, P(None, "gx", "gy", "gz"), P(("gx", "gy", "gz"), None)),
        out_specs=(spec, spec),
        check_vma=False,
    )
```

```python
import functools

import jax
import jax.numpy as jnp
from jax import lax
from jax.experimental import pallas as pl
from jax.experimental.pallas import tpu as pltpu
from jax.sharding import PartitionSpec as P

CX, CY, CZ = 8, 32, 128
CELLS = 16
LINES = 16
THETA = 1.0 / 128.0
WEIGHT = 0.6
PART_AT, LOW_AT, HIGH_AT = 32, 64, 96
HIGHEST = lax.Precision.HIGHEST
F32 = jnp.float32


def iota(shape, dim):
    return lax.broadcasted_iota(jnp.int32, shape, dim)


def dot(a, b):
    return lax.dot_general(
        a, b, (((1,), (0,)), ((), ())), precision=HIGHEST, preferred_element_type=F32
    )


def dot_t(a, b):
    return lax.dot_general(
        a, b, (((1,), (1,)), ((), ())), precision=HIGHEST, preferred_element_type=F32
    )


def one_where(cond):
    return jnp.where(cond, 1.0, 0.0).astype(F32)


def lines_of(field):
    low = (field[0] + field[1]) + (field[2] + field[3])
    high = (field[4] + field[5]) + (field[6] + field[7])
    stacked = jnp.concatenate([low, high], axis=0)
    by_line = one_where(iota((128, 64), 1) // 4 == iota((128, 64), 0))
    by_cell = one_where(iota((CELLS, 128), 1) // 8 == iota((CELLS, 128), 0))
    return dot_t(by_cell, dot(by_line, stacked))


def faces_of(field):
    shape = (CX, CY, 128)
    here = iota(shape, 2) == (iota(shape, 0) % 4) * 32 + iota(shape, 1)

    def packed(z):
        rows = jnp.sum(jnp.where(here, field[:, :, z : z + 1], 0.0), axis=1)
        halves = [jnp.sum(rows[i : i + 4], axis=0, keepdims=True) for i in (0, 4)]
        return jnp.concatenate(halves, axis=0)

    return packed(0), packed(CZ - 1)


def write_z_message(zmsg_ref, pairs, faces, spread_inverse, total, sizes):
    nz, count = sizes[2], 2 + len(pairs)
    mz = lax.axis_index("gz")
    lane1, lane8, row8 = iota((1, 128), 1), iota((8, 128), 1), iota((8, 128), 0)
    only = lambda v: jnp.where(lane1 < LINES, v, 0.0)
    tails = [pltpu.roll(only(a), 96, 1) + pltpu.roll(only(b), 112, 1) if a is not None else None for a, b in pairs]
    mine = spread_inverse * total
    inside = lane8 // 24 == row8 % 4
    zero = jnp.zeros((1, 128), F32)
    for p in range(nz):
        moved = jnp.where(inside, pltpu.roll(mine, (8 - 8 * p) % 128, 1), 0.0)
        zmsg_ref[p * count] = zero
        zmsg_ref[p * count + 1] = zero
        for h, tail in enumerate(tails):
            row = jnp.sum(moved[4 * h : 4 * h + 4], axis=0, keepdims=True) if h < 2 else zero
            zmsg_ref[p * count + 2 + h] = row if tail is None else row + tail

    @pl.when(mz > 0)
    def _():
        zmsg_ref[(mz - 1) * count] = faces[0][0:1]
        zmsg_ref[(mz - 1) * count + 1] = faces[0][1:2]

    @pl.when(mz < nz - 1)
    def _():
        zmsg_ref[(mz + 1) * count] = faces[1][0:1]
        zmsg_ref[(mz + 1) * count + 1] = faces[1][1:2]


def write_planes(field, planes):
    xlo, xhi, ylo, yhi = planes
    xlo[...] = field[0]
    xhi[...] = field[CX - 1]
    ylo[...] = field[:, 0, :]
    yhi[...] = field[:, CY - 1, :]


def begin_kernel(
    sizes, r_hbm, sigma_hbm, kappa_hbm, inv_hbm,
    zmsg_ref, loc_ref, alpha_ref, spread_ref, xlo, xhi, ylo, yhi,
    r_ref, sigma_ref, kappa_ref, inv_ref, sems
):
    pairs = ((kappa_hbm, kappa_ref), (sigma_hbm, sigma_ref), (r_hbm, r_ref), (inv_hbm, inv_ref))
    copies = [pltpu.make_async_copy(a, b, sems.at[i]) for i, (a, b) in enumerate(pairs)]
    for copy in copies:
        copy.start()
    for copy in copies:
        copy.wait()
    r, sigma = r_ref[...], sigma_ref[...]
    kx, ky, kz = kappa_ref[0], kappa_ref[1], kappa_ref[2]
    jac = r * (WEIGHT / (sigma + 2.0 * (kx + ky + kz)))
    write_planes(jac, (xlo, xhi, ylo, yhi))
    unused = iota((CELLS, 128), 1) >= LINES
    e = jnp.where(unused, 1.0, lines_of(sigma))
    g = jnp.where(unused, 1.0, lines_of(kz) * 0.125)
    rhs = lines_of(r)
    row = lambda a, k: a[k : k + 1, :]
    first, mid, last = row(e, 0), row(g, 0), row(e, 1)
    cur_first, cur = row(rhs, 0), row(rhs, 1)
    zero = jnp.zeros((1, 128), F32)
    for c in range(3):
        for k in (0, CELLS - 1):
            loc_ref[c, k : k + 1, :] = zero
    for k in (0, CELLS - 1):
        alpha_ref[k : k + 1, :] = zero
    for k in range(1, CELLS - 1):
        inv = 1.0 / (mid + last + row(g, k))
        mu, gam = mid * inv, row(g, k) * inv
        loc_ref[0, k : k + 1, :] = mu
        loc_ref[1, k : k + 1, :] = gam
        loc_ref[2, k : k + 1, :] = inv
        alpha_ref[k : k + 1, :] = cur * inv
        first = first + mu * last
        mid = mu * row(g, k)
        last = row(e, k + 1) + gam * last
        cur_first = cur_first + mu * cur
        cur = row(rhs, k + 1) + gam * cur
    move = one_where((iota((128, 128), 0) % 16) * 8 + iota((128, 128), 0) // 16 == iota((128, 128), 1))
    plain = dot(inv_ref[...], move)
    step = iota((8, 128), 0) % 4
    spread_inverse = plain
    for k in range(1, 4):
        spread_inverse = jnp.where(step == k, pltpu.roll(plain, 24 * k, 1), spread_inverse)
    spread_ref[...] = spread_inverse
    pairs = [(cur_first, cur), (first, mid), (last, row(g, CELLS - 1))]
    write_z_message(zmsg_ref, pairs, faces_of(jac), spread_inverse, jnp.sum(r), sizes)


def solve_chain(sizes, fresh, zrec_ref, loc_ref, alpha_ref, chain_ref, final_ref, sol_ref):
    nz = sizes[2]
    mz = lax.axis_index("gz")
    count = 5 if fresh else 4
    zero = jnp.zeros((1, 128), F32)
    columns = []
    for h in range(count - 2 if fresh else 1):
        rows = jnp.concatenate([zrec_ref[p * count + 2 + h] for p in range(nz)], axis=0)
        used = iota(rows.shape, 1) < LINES
        for shift in (32, 16):
            columns.append(jnp.where(used, pltpu.roll(rows, shift, 1), 1.0))
    part = lambda p, i: columns[i][p : p + 1, :]

    def mine(i):
        row = pltpu.roll(zrec_ref[mz * count + 2 + i // 2], 32 - 16 * (i % 2), 1)
        return jnp.where(iota((1, 128), 1) < LINES, row, 1.0)

    if fresh:
        one = zero + 1.0
        cond, cond_own, hold, ginv = zero, zero, one, one
        for p in range(nz - 1):
            a, m, b, g = part(p, 2), part(p, 3), part(p, 4), part(p, 5)
            at_first = a + cond
            s = m + at_first
            n = b * s + m * at_first
            inv = 1.0 / (n + g * s)
            chain_ref[0, p : p + 1, :] = g * m * inv
            c2 = g * s * inv
            chain_ref[1, p : p + 1, :] = c2
            cond = g * n * inv
            here = mz == p + 1
            cond_own = jnp.where(here, cond, cond_own)
            hold = jnp.where(here, c2, hold)
            ginv = jnp.where(here, g, ginv)
        left_cond, left_hold, left_ginv = cond_own, hold, 1.0 / ginv
        cond = part(nz - 1, 5)
        cond_own, hold, ginv = cond, one, one
        for p in range(nz - 1, 0, -1):
            a, m, b, g = part(p, 2), part(p, 3), part(p, 4), part(p - 1, 5)
            at_last = b + cond
            s = m + at_last
            n = a * s + m * at_last
            inv = 1.0 / (n + g * s)
            chain_ref[2, p : p + 1, :] = g * m * inv
            c2 = g * s * inv
            chain_ref[3, p : p + 1, :] = c2
            cond = g * n * inv
            here = mz == p - 1
            cond_own = jnp.where(here, cond, cond_own)
            hold = jnp.where(here, c2, hold)
            ginv = jnp.where(here, g, ginv)
        right_cond, right_hold, right_ginv = cond_own, hold, 1.0 / ginv
        for c, p in ((0, nz - 1), (1, nz - 1), (2, 0), (3, 0)):
            chain_ref[c, p : p + 1, :] = zero
        big_a = mine(2) + left_cond
        big_b = mine(4) + right_cond
        m = mine(3)
        det_inv = 1.0 / (big_a * m + big_b * m + big_a * big_b)
        f1, f2, f3 = (big_b + m) * det_inv, m * det_inv, (big_a + m) * det_inv
        final_ref[...] = jnp.concatenate(
            [f1, f2, f3, left_ginv, left_hold, right_ginv, right_hold, zero], axis=0
        )
    else:
        f1, f2, f3, left_ginv, left_hold, right_ginv, right_hold = [
            final_ref[i : i + 1, :] for i in range(7)
        ]
    chain = lambda c, p: chain_ref[c, p : p + 1, :]
    cur, cur_left = zero, zero
    for p in range(nz - 1):
        cur = chain(0, p) * (part(p, 0) + cur) + chain(1, p) * part(p, 1)
        cur_left = jnp.where(mz == p + 1, cur, cur_left)
    cur, cur_right = zero, zero
    for p in range(nz - 1, 0, -1):
        cur = chain(2, p) * (part(p, 1) + cur) + chain(3, p) * part(p, 0)
        cur_right = jnp.where(mz == p - 1, cur, cur_right)
    cur_first = mine(0) + cur_left
    cur_last = mine(1) + cur_right
    sol_first = f1 * cur_first + f2 * cur_last
    sol_last = f2 * cur_first + f3 * cur_last
    below = cur_left * left_ginv + left_hold * sol_first
    above = cur_right * right_ginv + right_hold * sol_last
    sol_ref[0:1, :] = sol_first
    sol_ref[CELLS - 1 : CELLS, :] = sol_last
    value = sol_last
    for k in range(CELLS - 2, 0, -1):
        value = alpha_ref[k : k + 1, :] + loc_ref[0, k : k + 1, :] * sol_first + loc_ref[1, k : k + 1, :] * value
        sol_ref[k : k + 1, :] = value
    lanes16 = iota((CELLS, 128), 1) < LINES
    sol = jnp.where(lanes16, sol_ref[...], 0.0) * THETA

    line, lane = iota((128, 128), 0), iota((128, 128), 1)
    picks = [
        one_where(line == lane // 16),
        one_where(line == 8 + lane // 16),
        one_where((line == (lane // 16) * 8) & (lane < 32)),
        one_where((line == (lane // 16) * 8 + 7) & (lane < 32)),
    ]
    keep = iota((CELLS, 128), 1) % 16 == iota((CELLS, 128), 0)
    x_low, x_high, y_low, y_high = [
        jnp.sum(jnp.where(keep, dot(sol, pick), 0.0), axis=0, keepdims=True) for pick in picks
    ]

    lane8, row8 = iota((8, 128), 1), iota((8, 128), 0)
    of_row = (lane8 // 8 == row8 // 4) & (lane8 < LINES)
    to_high = one_where((lane >= HIGH_AT) & ((lane - HIGH_AT) // 4 == line % 8) & (line < LINES))
    to_low = one_where(
        (lane >= LOW_AT) & (lane < HIGH_AT) & ((lane - LOW_AT) // 4 == line % 8) & (line < LINES)
    )
    lines_part = dot(jnp.where(of_row, below, 0.0), to_high) + dot(jnp.where(of_row, above, 0.0), to_low)
    face = jnp.zeros((8, 128), F32)
    for peer, at in ((jnp.maximum(mz - 1, 0), HIGH_AT), (jnp.minimum(mz + 1, nz - 1), LOW_AT)):
        packed = jnp.where(row8 < 4, zrec_ref[peer * count], zrec_ref[peer * count + 1])
        for k in range(4):
            here = (lane8 // 32 == at // 32) & (row8 % 4 == k)
            face = jnp.where(here, pltpu.roll(packed, (at - 32 * k) % 128, 1), face)
    zhalo = jnp.where(lane8 >= LOW_AT, face + THETA * lines_part, 0.0)
    return x_low, x_high, y_low, y_high, zhalo


def coarse_totals(zrec_ref, count, nz):
    totals = [zrec_ref[2], zrec_ref[3]]
    for p in range(1, nz):
        for h in range(2):
            totals[h] = totals[h] + zrec_ref[p * count + 2 + h]
    return totals


def first_lines_kernel(
    sizes, zrec_ref, loc_ref, alpha_ref, h2, h3, xmsg_ref, own_ref, zhalo_ref, chain_ref, final_ref, sol_ref
):
    nx, ny, nz = sizes
    mx, my = lax.axis_index("gx"), lax.axis_index("gy")
    x_low, x_high, y_low, y_high, zhalo = solve_chain(
        sizes, True, zrec_ref, loc_ref, alpha_ref, chain_ref, final_ref, sol_ref
    )
    zero = jnp.zeros((1, 128), F32)
    own_ref[...] = jnp.concatenate([x_low, x_high] + [zero] * 6, axis=0)
    zhalo_ref[...] = zhalo

    totals = coarse_totals(zrec_ref, 5, nz)
    lane1 = iota((1, 128), 1)

    def block(i, width, at, offset):
        moved = pltpu.roll(totals[i // 4], (at - 24 * (i % 4) - offset) % 128, 1)
        return jnp.where((lane1 >= at) & (lane1 < at + width), moved, 0.0)

    second = iota((2, 128), 0) == 1
    for i in range(nx):
        sums = block(i, 24, PART_AT, 0)
        if i > 0:
            sums = sums + block(i - 1, 8, PART_AT + 24, 8)
        if i < nx - 1:
            sums = sums + block(i + 1, 8, PART_AT + 32, 8)
        both = jnp.where(second, sums, 0.0)
        for j in range(ny):
            xmsg_ref[i * ny + j] = both
    here = mx * ny + my

    @pl.when(mx > 0)
    def _():
        xmsg_ref[here - ny, 0:1, :] = x_low

    @pl.when(mx < nx - 1)
    def _():
        xmsg_ref[here + ny, 0:1, :] = x_high

    @pl.when(my > 0)
    def _():
        xmsg_ref[here - 1, 0:1, :] = y_low

    @pl.when(my < ny - 1)
    def _():
        xmsg_ref[here + 1, 0:1, :] = y_high


def scale(sigma_ref, kappa_ref, x):
    return WEIGHT / (sigma_ref[x] + 2.0 * (kappa_ref[0, x] + kappa_ref[1, x] + kappa_ref[2, x]))


def ends_of(face):
    lane32, row32 = iota((CY, 128), 1), iota((CY, 128), 0)
    diagonal = (lane32 == row32 + HIGH_AT) | (lane32 == row32 + LOW_AT)
    spots = jnp.concatenate([jnp.where(diagonal, face[x : x + 1, :], 0.0) for x in range(CX)], axis=0)
    j, k = iota((128, 128), 0), iota((128, 128), 1)
    to_ends = one_where(((j >= HIGH_AT) & (k == 0)) | ((j >= LOW_AT) & (j < HIGH_AT) & (k == CZ - 1)))
    return dot(spots, to_ends)


def apply_operator(z, xlo, xhi, ylo, yhi, ends, sigma_ref, kappa_ref, w_ref):
    lane32, row32 = iota((CY, 128), 1), iota((CY, 128), 0)
    for x in range(CX):
        here_z = z[x]
        before = z[x - 1] if x > 0 else xlo
        after = z[x + 1] if x < CX - 1 else xhi
        y_less = jnp.where(row32 == 0, ylo[x : x + 1, :], pltpu.roll(here_z, 1, 0))
        y_more = jnp.where(row32 == CY - 1, yhi[x : x + 1, :], pltpu.roll(here_z, CY - 1, 0))
        z_less = jnp.where(lane32 == 0, 0.0, pltpu.roll(here_z, 1, 1))
        z_more = jnp.where(lane32 == CZ - 1, 0.0, pltpu.roll(here_z, CZ - 1, 1))
        twice = 2.0 * here_z
        w_ref[x] = (
            sigma_ref[x] * here_z
            + kappa_ref[0, x] * (twice - before - after)
            + kappa_ref[1, x] * (twice - y_less - y_more)
            + kappa_ref[2, x] * (twice - z_less - z_more - ends[x * 32 : x * 32 + 32])
        )


def wide(row):
    return jnp.where(iota((CY, 128), 1) // 16 == iota((CY, 128), 0) // 4, row, 0.0)


def thin(row):
    return jnp.where(iota((CX, 128), 1) // 16 == iota((CX, 128), 0) // 4, row, 0.0)


def to_cells():
    return one_where(iota((128, 128), 0) % 16 == iota((128, 128), 1) // 8)


def full_direction(sizes, base, xrec_ref, own_ref, zhalo_ref, halos, z_ref):
    nx, ny, nz = sizes
    mx, my, mz = lax.axis_index("gx"), lax.axis_index("gy"), lax.axis_index("gz")
    here = mx * ny + my
    sums = xrec_ref[0, 1:2, :]
    for q in range(1, nx * ny):
        sums = sums + xrec_ref[q, 1:2, :]
    lane1 = iota((1, 128), 1)
    coarse = lambda at: jnp.sum(jnp.where(lane1 == at + my, sums, 0.0))
    c_own = coarse(PART_AT + 8)
    c_zlo, c_zhi = coarse(PART_AT), coarse(PART_AT + 16)
    c_ylo, c_yhi = coarse(PART_AT + 7), coarse(PART_AT + 9)
    c_xlo, c_xhi = coarse(PART_AT + 24), coarse(PART_AT + 32)

    left = xrec_ref[jnp.maximum(here - ny, 0), 0:1, :]
    right = xrec_ref[jnp.minimum(here + ny, nx * ny - 1), 0:1, :]
    front = xrec_ref[jnp.maximum(here - 1, 0), 0:1, :]
    back = xrec_ref[jnp.minimum(here + 1, nx * ny - 1), 0:1, :]
    rows = jnp.concatenate(
        [wide(own_ref[0:1, :]), wide(own_ref[1:2, :]), wide(left), wide(right), thin(front), thin(back)],
        axis=0,
    )
    lines = dot(rows, to_cells())
    xlo, xhi, ylo, yhi = [h[...] for h in halos]
    xlo = jnp.where(mx > 0, xlo + lines[64:96] + c_xlo, 0.0)
    xhi = jnp.where(mx < nx - 1, xhi + lines[96:128] + c_xhi, 0.0)
    ylo = jnp.where(my > 0, ylo + lines[128:136] + c_ylo, 0.0)
    yhi = jnp.where(my < ny - 1, yhi + lines[136:144] + c_yhi, 0.0)
    face = zhalo_ref[...]
    high = jnp.where(mz > 0, face + c_zlo, 0.0)
    low = jnp.where(mz < nz - 1, face + c_zhi, 0.0)
    ends = ends_of(jnp.where(iota((8, 128), 1) >= HIGH_AT, high, low))
    z = [base(x) + lines[(x // 4) * 32 : (x // 4) * 32 + 32] + c_own for x in range(CX)]
    for x in range(CX):
        z_ref[x] = z[x]
    return z, xlo, xhi, ylo, yhi, ends


def first_kernel(
    sizes, r_ref, sigma_ref, kappa_ref, xrec_ref, own_ref, zhalo_ref, h0, h1, h2, h3,
    loc_ref, spread_ref, z_ref, w_ref, jac_ref, zmsg_ref, alpha_ref
):
    scales = [scale(sigma_ref, kappa_ref, x) for x in range(CX)]
    base = lambda x: scales[x] * r_ref[x]
    parts = full_direction(sizes, base, xrec_ref, own_ref, zhalo_ref, (h0, h1, h2, h3), z_ref)
    apply_operator(*parts, sigma_ref, kappa_ref, w_ref)
    field = w_ref[...]
    for x in range(CX):
        jac_ref[x] = scales[x] * w_ref[x]
    rhs = lines_of(field)
    row = lambda a, k: a[k : k + 1, :]
    cur_first, cur = row(rhs, 0), row(rhs, 1)
    zero = jnp.zeros((1, 128), F32)
    for k in (0, CELLS - 1):
        alpha_ref[k : k + 1, :] = zero
    for k in range(1, CELLS - 1):
        alpha_ref[k : k + 1, :] = cur * loc_ref[2, k : k + 1, :]
        cur_first = cur_first + loc_ref[0, k : k + 1, :] * cur
        cur = row(rhs, k + 1) + loc_ref[1, k : k + 1, :] * cur
    write_z_message(
        zmsg_ref, [(cur_first, cur), (None, None)], faces_of(jac_ref[...]), spread_ref[...], jnp.sum(field), sizes
    )


def second_lines_kernel(
    sizes, zrec_ref, loc_ref, alpha_ref, chain_ref, final_ref, jac_ref,
    part_ref, zhalo_ref, z_ref, xlo, xhi, ylo, yhi, sol_ref
):
    x_low, x_high, _, _, zhalo = solve_chain(
        sizes, False, zrec_ref, loc_ref, alpha_ref, chain_ref, final_ref, sol_ref
    )
    zhalo_ref[...] = zhalo
    lines = dot(jnp.concatenate([wide(x_low), wide(x_high)], axis=0), to_cells())
    for x in range(CX):
        z_ref[x] = jac_ref[x] + lines[(x // 4) * 32 : (x // 4) * 32 + 32]
    write_planes(z_ref[...], (xlo, xhi, ylo, yhi))
    zero = jnp.zeros((1, 128), F32)
    part_ref[...] = jnp.concatenate(coarse_totals(zrec_ref, 4, sizes[2]) + [zero] * 6, axis=0)


FACES = range(1, 7)
TERMS = (
    [("g11", -1, -1), ("g12", -1, -1), ("g22", -1, -1), ("h1", -1, -1), ("h2", -1, -1)]
    + [(name, j, -1) for name in ("h2", "g12", "g22") for j in range(7)]
    + [("g22", 0, j) for j in range(7)]
    + [("g22", j, j) for j in FACES]
    + [("g22", j, k) for j in FACES for k in FACES if j < k and (j - 1) // 2 != (k - 1) // 2]
)
NAMES = ("g11", "g12", "g22", "h1", "h2")
TERMS_AT, TERMS_ROW = 96, 32


def second_kernel(
    sizes, r_ref, w1_ref, sigma_ref, kappa_ref, z_ref, zhalo_ref, part_ref, h0, h1, h2, h3,
    w_ref, xmsg_ref, terms_ref
):
    nx, ny, nz = sizes
    mx, my, mz = lax.axis_index("gx"), lax.axis_index("gy"), lax.axis_index("gz")
    xlo = jnp.where(mx > 0, h0[...], 0.0)
    xhi = jnp.where(mx < nx - 1, h1[...], 0.0)
    ylo = jnp.where(my > 0, h2[...], 0.0)
    yhi = jnp.where(my < ny - 1, h3[...], 0.0)
    face = zhalo_ref[...]
    high, low = jnp.where(mz > 0, face, 0.0), jnp.where(mz < nz - 1, face, 0.0)
    ends = ends_of(jnp.where(iota((8, 128), 1) >= HIGH_AT, high, low))
    apply_operator([z_ref[x] for x in range(CX)], xlo, xhi, ylo, yhi, ends, sigma_ref, kappa_ref, w_ref)

    r, w1, w2, sigma = r_ref[...], w1_ref[...], w_ref[...], sigma_ref[...]
    kz = kappa_ref[2]
    rows = lambda a: jnp.sum(jnp.sum(a, axis=0), axis=0, keepdims=True)
    lane1 = iota((1, 128), 1)
    pick = lambda profile, face: jnp.where(lane1 == (0 if face == 5 else CZ - 1), profile, 0.0)
    low_row = lambda a: jnp.sum(a, axis=0, keepdims=True)
    partner = {"h2": r, "g12": w1, "g22": w2}
    partner_ref = {"h2": r_ref, "g12": w1_ref, "g22": w_ref}
    z_profiles = {name: rows(kz * f) for name, f in partner.items()}
    z_sigma, z_self = rows(kz * sigma), rows(kz * kz)

    def plane(ref, f):
        if f < 3:
            return ref[0 if f == 1 else CX - 1]
        return ref[:, 0 if f == 3 else CY - 1, :]

    face_weight = {f: plane(kappa_ref.at[(f - 1) // 2], f) for f in range(1, 5)}

    def on_face(f, other):
        return low_row(face_weight[f] * plane(other, f))

    def term(name, j, k):
        if j == -1:
            a, b = {"g11": (w1, w1), "g12": (w1, w2), "g22": (w2, w2), "h1": (w1, r), "h2": (w2, r)}[name]
            return rows(a * b)
        if k == -1:
            twice = 2.0 if name == "g22" else 1.0
            if j == 0:
                return twice * rows(sigma * partner[name])
            if j > 4:
                return twice * pick(z_profiles[name], j)
            return twice * on_face(j, partner_ref[name])
        if j == 0:
            if k == 0:
                return rows(sigma * sigma)
            return 2.0 * (pick(z_sigma, k) if k > 4 else on_face(k, sigma_ref))
        if j == k:
            return pick(z_self, j) if j > 4 else on_face(j, kappa_ref.at[(j - 1) // 2])
        if k > 4:
            return 2.0 * pick(on_face(j, kappa_ref.at[2]), k)
        x, y = 0 if j == 1 else CX - 1, 0 if k == 3 else CY - 1
        return 2.0 * kappa_ref[0, x, y : y + 1, :] * kappa_ref[1, x, y : y + 1, :]

    for i, (name, j, k) in enumerate(TERMS):
        terms_ref[i : i + 1, :] = term(name, j, k)
    for i in range(len(TERMS), 128):
        if i % 8 == 0:
            terms_ref[i : i + 8, :] = jnp.zeros((8, 128), F32)
        elif i == len(TERMS):
            stop = -(-i // 8) * 8
            terms_ref[i:stop, :] = jnp.zeros((stop - i, 128), F32)
    poly = dot_t(jnp.full((8, 128), 1.0, F32), terms_ref[...])[0:1, :]
    halves = [
        jnp.where(lane1 < TERMS_AT, part_ref[h : h + 1, :], pltpu.roll(poly, TERMS_AT - TERMS_ROW * h, 1))
        for h in range(2)
    ]
    both = jnp.concatenate(halves, axis=0)
    for q in range(nx * ny):
        xmsg_ref[q] = both


def plane_kernel(sizes, xrec_ref, sums_ref, own_ref, flat_ref):
    nx, ny, nz = sizes
    mx, my, mz = lax.axis_index("gx"), lax.axis_index("gy"), lax.axis_index("gz")
    count = nx * ny
    total = xrec_ref[0]
    for q in range(count):
        for h in range(2):
            flat_ref[h, q : q + 1, :] = xrec_ref[q, h : h + 1, :]
        if q > 0:
            total = total + xrec_ref[q]
    lane, row = iota((count, 128), 1), iota((count, 128), 0)
    tx, ty = row // ny, row % ny

    def value(qx, qy, dz, valid):
        at = (qx & 3) * 24 + 8 + 8 * dz + qy
        chosen = jnp.where(qx < 4, total[0:1, :], total[1:2, :])
        return jnp.sum(jnp.where((lane == at) & valid, chosen, 0.0), axis=1, keepdims=True)

    always = row >= 0
    c = value(tx, ty, 0, always)
    near = [
        value(tx - 1, ty, 0, tx > 0),
        value(tx + 1, ty, 0, tx < nx - 1),
        value(tx, ty - 1, 0, ty > 0),
        value(tx, ty + 1, 0, ty < ny - 1),
        value(tx, ty, -1, always & (mz > 0)),
        value(tx, ty, 1, always & (mz < nz - 1)),
    ]
    v = [c] + [c - n for n in near]
    lane1 = iota((1, 128), 1)
    out = jnp.zeros((1, 128), F32)
    for h in range(2):
        terms = list(enumerate(TERMS[TERMS_ROW * h : TERMS_ROW * (h + 1)], TERMS_AT))
        first = jnp.where(lane < 0, 1.0, 0.0)
        second = first
        for j in range(-1, 7):
            amount = 1.0 if j == -1 else v[j]
            is_first = lane < 0
            is_second = is_first
            for i, (_, a, b) in terms:
                if a == j:
                    is_first = is_first | (lane == i)
                if b == j:
                    is_second = is_second | (lane == i)
            first = jnp.where(is_first, amount, first)
            second = jnp.where(is_second, amount, second)
        weights = jnp.where(lane >= TERMS_AT, flat_ref[h], 0.0)
        added = jnp.sum(weights * first * second, axis=0, keepdims=True)
        for n, name in enumerate(NAMES):
            mask = lane1 < 0
            for i, (of, _, _) in terms:
                if of == name:
                    mask = mask | (lane1 == i)
            add = jnp.sum(jnp.where(mask, added, 0.0), axis=1, keepdims=True)
            out = jnp.where(lane1 == n, out + add, out)
    sums_ref[...] = out
    mine = row == mx * ny + my
    for j in range(7):
        own = jnp.sum(jnp.where(mine & (lane == 0), v[j], 0.0))
        own_ref[j : j + 1, :] = jnp.full((1, 128), own, F32)
    own_ref[7:8, :] = jnp.zeros((1, 128), F32)


def end_kernel(all_ref, own_ref, r_ref, sigma_ref, kappa_ref, z1_ref, w1_ref, z2_ref, w2_ref, field_ref, res_ref):
    sums = all_ref[0]
    for q in range(1, all_ref.shape[0]):
        sums = sums + all_ref[q]
    lane = iota((1, 128), 1)
    spread = lambda i: jnp.sum(jnp.where(lane == i, sums, 0.0), axis=1, keepdims=True)
    g11, g12, g22, h1, h2 = [spread(i) for i in range(5)]
    inv = 1.0 / (g11 * g22 - g12 * g12)
    y1 = (g22 * h1 - g12 * h2) * inv
    y2 = (g11 * h2 - g12 * h1) * inv
    c, xlo, xhi, ylo, yhi, zlo, zhi = [own_ref[j : j + 1, :] for j in range(7)]
    lane32, row32 = iota((CY, 128), 1), iota((CY, 128), 0)
    on_y = jnp.where(row32 == 0, ylo, jnp.where(row32 == CY - 1, yhi, 0.0))
    on_z = jnp.where(lane32 == 0, zlo, jnp.where(lane32 == CZ - 1, zhi, 0.0))
    for x in range(CX):
        w2 = w2_ref[x] + sigma_ref[x] * c + kappa_ref[1, x] * on_y + kappa_ref[2, x] * on_z
        if x == 0:
            w2 = w2 + kappa_ref[0, x] * xlo
        if x == CX - 1:
            w2 = w2 + kappa_ref[0, x] * xhi
        field_ref[x] = y1 * z1_ref[x] + y2 * (z2_ref[x] + c)
        res_ref[x] = r_ref[x] - y1 * w1_ref[x] - y2 * w2


def call(kernel, out_shapes, scratch=(), name=None, inputs=pltpu.VMEM, semaphores=(), limit=24 << 20):
    vmem = pl.BlockSpec(memory_space=pltpu.VMEM)

    def run(*args):
        return pl.pallas_call(
            kernel,
            out_shape=[jax.ShapeDtypeStruct(s, F32) for s in out_shapes],
            in_specs=[pl.BlockSpec(memory_space=inputs)] * len(args),
            out_specs=[vmem] * len(out_shapes),
            scratch_shapes=[pltpu.VMEM(s, F32) for s in scratch] + list(semaphores),
            compiler_params=pltpu.CompilerParams(vmem_limit_bytes=limit),
            name=name,
        )(*args)

    return run


def shards(sizes, r, sigma, kappa, inverse_rows):
    nx, ny, nz = sizes
    field, plane, tile, coarse = (CX, CY, CZ), (CY, CZ), (8, 128), (CELLS, 128)
    planes = [plane, plane, tile, tile]
    to_xy = (nx * ny, 2, 128)

    def halo(parts):
        xlo, xhi, ylo, yhi = parts
        up = lambda n: [(i, (i + 1) % n) for i in range(n)]
        down = lambda n: [((i + 1) % n, i) for i in range(n)]
        return (
            lax.ppermute(xhi, "gx", up(nx)),
            lax.ppermute(xlo, "gx", down(nx)),
            lax.ppermute(yhi, "gy", up(ny)),
            lax.ppermute(ylo, "gy", down(ny)),
        )

    def along_z(message):
        return lax.all_to_all(message, "gz", split_axis=0, concat_axis=0, tiled=True)

    def along_xy(message):
        return lax.all_to_all(message, ("gx", "gy"), split_axis=0, concat_axis=0, tiled=True)

    bind = lambda kernel, *a: functools.partial(kernel, sizes, *a)
    zmsg, loc, alpha, spread, *sides = call(
        bind(begin_kernel), [(nz * 5, 1, 128), (3, *coarse), coarse, tile, *planes],
        [field, field, (3, *field), tile], "begin", pltpu.HBM, [pltpu.SemaphoreType.DMA((4,))], 55100 << 10,
    )(r, sigma, kappa, inverse_rows)
    zrec = along_z(zmsg)
    halos = halo(sides)
    xmsg, own, zhalo, chain, final = call(
        bind(first_lines_kernel), [to_xy, tile, tile, (4, nz, 128), tile], [coarse], "lines_first"
    )(zrec, loc, alpha, *halos[2:])
    xrec = along_xy(xmsg)
    z1, w1, jac, zmsg, alpha = call(
        bind(first_kernel), [field, field, field, (nz * 4, 1, 128), coarse], name="operator_first"
    )(r, sigma, kappa, xrec, own, zhalo, *halos, loc, spread)
    zrec = along_z(zmsg)
    part, zhalo, z2, *sides = call(
        bind(second_lines_kernel), [tile, tile, field, *planes], [coarse], "lines_second"
    )(zrec, loc, alpha, chain, final, jac)
    halos = halo(sides)
    w2, xmsg = call(bind(second_kernel), [field, to_xy], [(128, 128)], "operator_second")(
        r, w1, sigma, kappa, z2, zhalo, part, *halos
    )
    xrec = along_xy(xmsg)
    sums, values = call(bind(plane_kernel), [(1, 128), tile], [(2, nx * ny, 128)], "plane")(xrec)
    sums = along_z(jnp.broadcast_to(sums[None], (nz, 1, 128)))
    return tuple(
        call(end_kernel, [field, field], name="end")(sums, values, r, sigma, kappa, z1, w1, z2, w2)
    )


def solution(mesh):
    sizes = (mesh.shape["gx"], mesh.shape["gy"], mesh.shape["gz"])
    spec = P("gx", "gy", "gz")

    def run(r, sigma, kappa, inverse):
        return shards(sizes, r, sigma, kappa, inverse.reshape(8, 128))

    return jax.shard_map(
        run,
        mesh=mesh,
        in_specs=(spec, spec, P(None, "gx", "gy", "gz"), P(("gx", "gy", "gz"), None)),
        out_specs=(spec, spec),
        check_vma=False,
    )
```

```python
import functools

import jax
import jax.numpy as jnp
from jax import lax
from jax.experimental import pallas as pl
from jax.experimental.pallas import tpu as pltpu
from jax.sharding import PartitionSpec as P

CX, CY, CZ = 8, 32, 128
CELLS = 16
LINES = 16
THETA = 1.0 / 128.0
WEIGHT = 0.6
PART_AT, LOW_AT, HIGH_AT = 32, 64, 96
HIGHEST = lax.Precision.HIGHEST
F32 = jnp.float32


def iota(shape, dim):
    return lax.broadcasted_iota(jnp.int32, shape, dim)


def dot(a, b):
    return lax.dot_general(
        a, b, (((1,), (0,)), ((), ())), precision=HIGHEST, preferred_element_type=F32
    )


def dot_t(a, b):
    return lax.dot_general(
        a, b, (((1,), (1,)), ((), ())), precision=HIGHEST, preferred_element_type=F32
    )


def one_where(cond):
    return jnp.where(cond, 1.0, 0.0).astype(F32)


def lines_of(field):
    low = (field[0] + field[1]) + (field[2] + field[3])
    high = (field[4] + field[5]) + (field[6] + field[7])
    stacked = jnp.concatenate([low, high], axis=0)
    by_line = one_where(iota((128, 64), 1) // 4 == iota((128, 64), 0))
    by_cell = one_where(iota((CELLS, 128), 1) // 8 == iota((CELLS, 128), 0))
    return dot_t(by_cell, dot(by_line, stacked))


def faces_of(field):
    shape = (CX, CY, 128)
    here = iota(shape, 2) == (iota(shape, 0) % 4) * 32 + iota(shape, 1)

    def packed(z):
        rows = jnp.sum(jnp.where(here, field[:, :, z : z + 1], 0.0), axis=1)
        halves = [jnp.sum(rows[i : i + 4], axis=0, keepdims=True) for i in (0, 4)]
        return jnp.concatenate(halves, axis=0)

    return packed(0), packed(CZ - 1)


def write_z_message(zmsg_ref, pairs, faces, spread_inverse, total, sizes):
    nz, count = sizes[2], 2 + len(pairs)
    mz = lax.axis_index("gz")
    lane1, lane8, row8 = iota((1, 128), 1), iota((8, 128), 1), iota((8, 128), 0)
    only = lambda v: jnp.where(lane1 < LINES, v, 0.0)
    tails = [pltpu.roll(only(a), 96, 1) + pltpu.roll(only(b), 112, 1) if a is not None else None for a, b in pairs]
    mine = spread_inverse * total
    inside = lane8 // 24 == row8 % 4
    zero = jnp.zeros((1, 128), F32)
    for p in range(nz):
        moved = jnp.where(inside, pltpu.roll(mine, (8 - 8 * p) % 128, 1), 0.0)
        zmsg_ref[p * count] = zero
        zmsg_ref[p * count + 1] = zero
        for h, tail in enumerate(tails):
            row = jnp.sum(moved[4 * h : 4 * h + 4], axis=0, keepdims=True) if h < 2 else zero
            zmsg_ref[p * count + 2 + h] = row if tail is None else row + tail

    @pl.when(mz > 0)
    def _():
        zmsg_ref[(mz - 1) * count] = faces[0][0:1]
        zmsg_ref[(mz - 1) * count + 1] = faces[0][1:2]

    @pl.when(mz < nz - 1)
    def _():
        zmsg_ref[(mz + 1) * count] = faces[1][0:1]
        zmsg_ref[(mz + 1) * count + 1] = faces[1][1:2]


def write_planes(field, planes):
    xlo, xhi, ylo, yhi = planes
    xlo[...] = field[0]
    xhi[...] = field[CX - 1]
    ylo[...] = field[:, 0, :]
    yhi[...] = field[:, CY - 1, :]


def begin_kernel(
    sizes, r_hbm, sigma_hbm, kappa_hbm, inv_hbm,
    zmsg_ref, loc_ref, alpha_ref, spread_ref, xlo, xhi, ylo, yhi,
    r_ref, sigma_ref, kappa_ref, inv_ref, sems
):
    pairs = ((kappa_hbm, kappa_ref), (sigma_hbm, sigma_ref), (r_hbm, r_ref), (inv_hbm, inv_ref))
    copies = [pltpu.make_async_copy(a, b, sems.at[i]) for i, (a, b) in enumerate(pairs)]
    for i in (2, 1, 3, 0):
        copies[i].start()
    unused = iota((CELLS, 128), 1) >= LINES
    copies[2].wait()
    r = r_ref[...]
    rhs = lines_of(r)
    copies[1].wait()
    sigma = sigma_ref[...]
    e = jnp.where(unused, 1.0, lines_of(sigma))
    copies[3].wait()
    move = one_where((iota((128, 128), 0) % 16) * 8 + iota((128, 128), 0) // 16 == iota((128, 128), 1))
    plain = dot(inv_ref[...], move)
    copies[0].wait()
    kx, ky, kz = kappa_ref[0], kappa_ref[1], kappa_ref[2]
    jac = r * (WEIGHT / (sigma + 2.0 * (kx + ky + kz)))
    write_planes(jac, (xlo, xhi, ylo, yhi))
    g = jnp.where(unused, 1.0, lines_of(kz) * 0.125)
    row = lambda a, k: a[k : k + 1, :]
    first, mid, last = row(e, 0), row(g, 0), row(e, 1)
    cur_first, cur = row(rhs, 0), row(rhs, 1)
    zero = jnp.zeros((1, 128), F32)
    for c in range(3):
        for k in (0, CELLS - 1):
            loc_ref[c, k : k + 1, :] = zero
    for k in (0, CELLS - 1):
        alpha_ref[k : k + 1, :] = zero
    for k in range(1, CELLS - 1):
        inv = 1.0 / (mid + last + row(g, k))
        mu, gam = mid * inv, row(g, k) * inv
        loc_ref[0, k : k + 1, :] = mu
        loc_ref[1, k : k + 1, :] = gam
        loc_ref[2, k : k + 1, :] = inv
        alpha_ref[k : k + 1, :] = cur * inv
        first = first + mu * last
        mid = mu * row(g, k)
        last = row(e, k + 1) + gam * last
        cur_first = cur_first + mu * cur
        cur = row(rhs, k + 1) + gam * cur
    step = iota((8, 128), 0) % 4
    spread_inverse = plain
    for k in range(1, 4):
        spread_inverse = jnp.where(step == k, pltpu.roll(plain, 24 * k, 1), spread_inverse)
    spread_ref[...] = spread_inverse
    pairs = [(cur_first, cur), (first, mid), (last, row(g, CELLS - 1))]
    write_z_message(zmsg_ref, pairs, faces_of(jac), spread_inverse, jnp.sum(r), sizes)


def solve_chain(sizes, fresh, zrec_ref, loc_ref, alpha_ref, chain_ref, final_ref, sol_ref):
    nz = sizes[2]
    mz = lax.axis_index("gz")
    count = 5 if fresh else 4
    zero = jnp.zeros((1, 128), F32)
    columns = []
    for h in range(count - 2 if fresh else 1):
        rows = jnp.concatenate([zrec_ref[p * count + 2 + h] for p in range(nz)], axis=0)
        used = iota(rows.shape, 1) < LINES
        for shift in (32, 16):
            columns.append(jnp.where(used, pltpu.roll(rows, shift, 1), 1.0))
    part = lambda p, i: columns[i][p : p + 1, :]

    def mine(i):
        row = pltpu.roll(zrec_ref[mz * count + 2 + i // 2], 32 - 16 * (i % 2), 1)
        return jnp.where(iota((1, 128), 1) < LINES, row, 1.0)

    if fresh:
        one = zero + 1.0
        cond, cond_own, hold, ginv = zero, zero, one, one
        for p in range(nz - 1):
            a, m, b, g = part(p, 2), part(p, 3), part(p, 4), part(p, 5)
            at_first = a + cond
            s = m + at_first
            n = b * s + m * at_first
            inv = 1.0 / (n + g * s)
            chain_ref[0, p : p + 1, :] = g * m * inv
            c2 = g * s * inv
            chain_ref[1, p : p + 1, :] = c2
            cond = g * n * inv
            here = mz == p + 1
            cond_own = jnp.where(here, cond, cond_own)
            hold = jnp.where(here, c2, hold)
            ginv = jnp.where(here, g, ginv)
        left_cond, left_hold, left_ginv = cond_own, hold, 1.0 / ginv
        cond = part(nz - 1, 5)
        cond_own, hold, ginv = cond, one, one
        for p in range(nz - 1, 0, -1):
            a, m, b, g = part(p, 2), part(p, 3), part(p, 4), part(p - 1, 5)
            at_last = b + cond
            s = m + at_last
            n = a * s + m * at_last
            inv = 1.0 / (n + g * s)
            chain_ref[2, p : p + 1, :] = g * m * inv
            c2 = g * s * inv
            chain_ref[3, p : p + 1, :] = c2
            cond = g * n * inv
            here = mz == p - 1
            cond_own = jnp.where(here, cond, cond_own)
            hold = jnp.where(here, c2, hold)
            ginv = jnp.where(here, g, ginv)
        right_cond, right_hold, right_ginv = cond_own, hold, 1.0 / ginv
        for c, p in ((0, nz - 1), (1, nz - 1), (2, 0), (3, 0)):
            chain_ref[c, p : p + 1, :] = zero
        big_a = mine(2) + left_cond
        big_b = mine(4) + right_cond
        m = mine(3)
        det_inv = 1.0 / (big_a * m + big_b * m + big_a * big_b)
        f1, f2, f3 = (big_b + m) * det_inv, m * det_inv, (big_a + m) * det_inv
        final_ref[...] = jnp.concatenate(
            [f1, f2, f3, left_ginv, left_hold, right_ginv, right_hold, zero], axis=0
        )
    else:
        f1, f2, f3, left_ginv, left_hold, right_ginv, right_hold = [
            final_ref[i : i + 1, :] for i in range(7)
        ]
    chain = lambda c, p: chain_ref[c, p : p + 1, :]
    cur, cur_left = zero, zero
    for p in range(nz - 1):
        cur = chain(0, p) * (part(p, 0) + cur) + chain(1, p) * part(p, 1)
        cur_left = jnp.where(mz == p + 1, cur, cur_left)
    cur, cur_right = zero, zero
    for p in range(nz - 1, 0, -1):
        cur = chain(2, p) * (part(p, 1) + cur) + chain(3, p) * part(p, 0)
        cur_right = jnp.where(mz == p - 1, cur, cur_right)
    cur_first = mine(0) + cur_left
    cur_last = mine(1) + cur_right
    sol_first = f1 * cur_first + f2 * cur_last
    sol_last = f2 * cur_first + f3 * cur_last
    below = cur_left * left_ginv + left_hold * sol_first
    above = cur_right * right_ginv + right_hold * sol_last
    sol_ref[0:1, :] = sol_first
    sol_ref[CELLS - 1 : CELLS, :] = sol_last
    value = sol_last
    for k in range(CELLS - 2, 0, -1):
        value = alpha_ref[k : k + 1, :] + loc_ref[0, k : k + 1, :] * sol_first + loc_ref[1, k : k + 1, :] * value
        sol_ref[k : k + 1, :] = value
    lanes16 = iota((CELLS, 128), 1) < LINES
    sol = jnp.where(lanes16, sol_ref[...], 0.0) * THETA

    line, lane = iota((128, 128), 0), iota((128, 128), 1)
    picks = [
        one_where(line == lane // 16),
        one_where(line == 8 + lane // 16),
        one_where((line == (lane // 16) * 8) & (lane < 32)),
        one_where((line == (lane // 16) * 8 + 7) & (lane < 32)),
    ]
    keep = iota((CELLS, 128), 1) % 16 == iota((CELLS, 128), 0)
    x_low, x_high, y_low, y_high = [
        jnp.sum(jnp.where(keep, dot(sol, pick), 0.0), axis=0, keepdims=True) for pick in picks
    ]

    lane8, row8 = iota((8, 128), 1), iota((8, 128), 0)
    of_row = (lane8 // 8 == row8 // 4) & (lane8 < LINES)
    to_high = one_where((lane >= HIGH_AT) & ((lane - HIGH_AT) // 4 == line % 8) & (line < LINES))
    to_low = one_where(
        (lane >= LOW_AT) & (lane < HIGH_AT) & ((lane - LOW_AT) // 4 == line % 8) & (line < LINES)
    )
    lines_part = dot(jnp.where(of_row, below, 0.0), to_high) + dot(jnp.where(of_row, above, 0.0), to_low)
    face = jnp.zeros((8, 128), F32)
    for peer, at in ((jnp.maximum(mz - 1, 0), HIGH_AT), (jnp.minimum(mz + 1, nz - 1), LOW_AT)):
        packed = jnp.where(row8 < 4, zrec_ref[peer * count], zrec_ref[peer * count + 1])
        for k in range(4):
            here = (lane8 // 32 == at // 32) & (row8 % 4 == k)
            face = jnp.where(here, pltpu.roll(packed, (at - 32 * k) % 128, 1), face)
    zhalo = jnp.where(lane8 >= LOW_AT, face + THETA * lines_part, 0.0)
    return x_low, x_high, y_low, y_high, zhalo


def coarse_totals(zrec_ref, count, nz):
    totals = [zrec_ref[2], zrec_ref[3]]
    for p in range(1, nz):
        for h in range(2):
            totals[h] = totals[h] + zrec_ref[p * count + 2 + h]
    return totals


def first_lines_kernel(
    sizes, zrec_ref, loc_ref, alpha_ref, h2, h3, xmsg_ref, own_ref, zhalo_ref, chain_ref, final_ref, sol_ref
):
    nx, ny, nz = sizes
    mx, my = lax.axis_index("gx"), lax.axis_index("gy")
    x_low, x_high, y_low, y_high, zhalo = solve_chain(
        sizes, True, zrec_ref, loc_ref, alpha_ref, chain_ref, final_ref, sol_ref
    )
    zero = jnp.zeros((1, 128), F32)
    own_ref[...] = jnp.concatenate([x_low, x_high] + [zero] * 6, axis=0)
    zhalo_ref[...] = zhalo

    totals = coarse_totals(zrec_ref, 5, nz)
    lane1 = iota((1, 128), 1)

    def block(i, width, at, offset):
        moved = pltpu.roll(totals[i // 4], (at - 24 * (i % 4) - offset) % 128, 1)
        return jnp.where((lane1 >= at) & (lane1 < at + width), moved, 0.0)

    second = iota((2, 128), 0) == 1
    for i in range(nx):
        sums = block(i, 24, PART_AT, 0)
        if i > 0:
            sums = sums + block(i - 1, 8, PART_AT + 24, 8)
        if i < nx - 1:
            sums = sums + block(i + 1, 8, PART_AT + 32, 8)
        both = jnp.where(second, sums, 0.0)
        for j in range(ny):
            xmsg_ref[i * ny + j] = both
    here = mx * ny + my

    @pl.when(mx > 0)
    def _():
        xmsg_ref[here - ny, 0:1, :] = x_low

    @pl.when(mx < nx - 1)
    def _():
        xmsg_ref[here + ny, 0:1, :] = x_high

    @pl.when(my > 0)
    def _():
        xmsg_ref[here - 1, 0:1, :] = y_low

    @pl.when(my < ny - 1)
    def _():
        xmsg_ref[here + 1, 0:1, :] = y_high


def scale(sigma_ref, kappa_ref, x):
    return WEIGHT / (sigma_ref[x] + 2.0 * (kappa_ref[0, x] + kappa_ref[1, x] + kappa_ref[2, x]))


def ends_of(face):
    lane32, row32 = iota((CY, 128), 1), iota((CY, 128), 0)
    diagonal = (lane32 == row32 + HIGH_AT) | (lane32 == row32 + LOW_AT)
    spots = jnp.concatenate([jnp.where(diagonal, face[x : x + 1, :], 0.0) for x in range(CX)], axis=0)
    j, k = iota((128, 128), 0), iota((128, 128), 1)
    to_ends = one_where(((j >= HIGH_AT) & (k == 0)) | ((j >= LOW_AT) & (j < HIGH_AT) & (k == CZ - 1)))
    return dot(spots, to_ends)


def apply_operator(z, xlo, xhi, ylo, yhi, ends, sigma_ref, kappa_ref, w_ref):
    lane32, row32 = iota((CY, 128), 1), iota((CY, 128), 0)
    for x in range(CX):
        here_z = z[x]
        before = z[x - 1] if x > 0 else xlo
        after = z[x + 1] if x < CX - 1 else xhi
        y_less = jnp.where(row32 == 0, ylo[x : x + 1, :], pltpu.roll(here_z, 1, 0))
        y_more = jnp.where(row32 == CY - 1, yhi[x : x + 1, :], pltpu.roll(here_z, CY - 1, 0))
        z_less = jnp.where(lane32 == 0, 0.0, pltpu.roll(here_z, 1, 1))
        z_more = jnp.where(lane32 == CZ - 1, 0.0, pltpu.roll(here_z, CZ - 1, 1))
        twice = 2.0 * here_z
        w_ref[x] = (
            sigma_ref[x] * here_z
            + kappa_ref[0, x] * (twice - before - after)
            + kappa_ref[1, x] * (twice - y_less - y_more)
            + kappa_ref[2, x] * (twice - z_less - z_more - ends[x * 32 : x * 32 + 32])
        )


def wide(row):
    return jnp.where(iota((CY, 128), 1) // 16 == iota((CY, 128), 0) // 4, row, 0.0)


def thin(row):
    return jnp.where(iota((CX, 128), 1) // 16 == iota((CX, 128), 0) // 4, row, 0.0)


def to_cells():
    return one_where(iota((128, 128), 0) % 16 == iota((128, 128), 1) // 8)


def full_direction(sizes, base, xrec_ref, own_ref, zhalo_ref, halos, z_ref):
    nx, ny, nz = sizes
    mx, my, mz = lax.axis_index("gx"), lax.axis_index("gy"), lax.axis_index("gz")
    here = mx * ny + my
    sums = xrec_ref[0, 1:2, :]
    for q in range(1, nx * ny):
        sums = sums + xrec_ref[q, 1:2, :]
    lane1 = iota((1, 128), 1)
    coarse = lambda at: jnp.sum(jnp.where(lane1 == at + my, sums, 0.0))
    c_own = coarse(PART_AT + 8)
    c_zlo, c_zhi = coarse(PART_AT), coarse(PART_AT + 16)
    c_ylo, c_yhi = coarse(PART_AT + 7), coarse(PART_AT + 9)
    c_xlo, c_xhi = coarse(PART_AT + 24), coarse(PART_AT + 32)

    left = xrec_ref[jnp.maximum(here - ny, 0), 0:1, :]
    right = xrec_ref[jnp.minimum(here + ny, nx * ny - 1), 0:1, :]
    front = xrec_ref[jnp.maximum(here - 1, 0), 0:1, :]
    back = xrec_ref[jnp.minimum(here + 1, nx * ny - 1), 0:1, :]
    rows = jnp.concatenate(
        [wide(own_ref[0:1, :]), wide(own_ref[1:2, :]), wide(left), wide(right), thin(front), thin(back)],
        axis=0,
    )
    lines = dot(rows, to_cells())
    xlo, xhi, ylo, yhi = [h[...] for h in halos]
    xlo = jnp.where(mx > 0, xlo + lines[64:96] + c_xlo, 0.0)
    xhi = jnp.where(mx < nx - 1, xhi + lines[96:128] + c_xhi, 0.0)
    ylo = jnp.where(my > 0, ylo + lines[128:136] + c_ylo, 0.0)
    yhi = jnp.where(my < ny - 1, yhi + lines[136:144] + c_yhi, 0.0)
    face = zhalo_ref[...]
    high = jnp.where(mz > 0, face + c_zlo, 0.0)
    low = jnp.where(mz < nz - 1, face + c_zhi, 0.0)
    ends = ends_of(jnp.where(iota((8, 128), 1) >= HIGH_AT, high, low))
    z = [base(x) + lines[(x // 4) * 32 : (x // 4) * 32 + 32] + c_own for x in range(CX)]
    for x in range(CX):
        z_ref[x] = z[x]
    return z, xlo, xhi, ylo, yhi, ends


def first_kernel(
    sizes, r_ref, sigma_ref, kappa_ref, xrec_ref, own_ref, zhalo_ref, h0, h1, h2, h3,
    loc_ref, spread_ref, z_ref, w_ref, jac_ref, zmsg_ref, alpha_ref
):
    scales = [scale(sigma_ref, kappa_ref, x) for x in range(CX)]
    base = lambda x: scales[x] * r_ref[x]
    parts = full_direction(sizes, base, xrec_ref, own_ref, zhalo_ref, (h0, h1, h2, h3), z_ref)
    apply_operator(*parts, sigma_ref, kappa_ref, w_ref)
    field = w_ref[...]
    for x in range(CX):
        jac_ref[x] = scales[x] * w_ref[x]
    rhs = lines_of(field)
    row = lambda a, k: a[k : k + 1, :]
    cur_first, cur = row(rhs, 0), row(rhs, 1)
    zero = jnp.zeros((1, 128), F32)
    for k in (0, CELLS - 1):
        alpha_ref[k : k + 1, :] = zero
    for k in range(1, CELLS - 1):
        alpha_ref[k : k + 1, :] = cur * loc_ref[2, k : k + 1, :]
        cur_first = cur_first + loc_ref[0, k : k + 1, :] * cur
        cur = row(rhs, k + 1) + loc_ref[1, k : k + 1, :] * cur
    write_z_message(
        zmsg_ref, [(cur_first, cur), (None, None)], faces_of(jac_ref[...]), spread_ref[...], jnp.sum(field), sizes
    )


def second_lines_kernel(
    sizes, zrec_ref, loc_ref, alpha_ref, chain_ref, final_ref, jac_ref,
    part_ref, zhalo_ref, z_ref, xlo, xhi, ylo, yhi, sol_ref
):
    x_low, x_high, _, _, zhalo = solve_chain(
        sizes, False, zrec_ref, loc_ref, alpha_ref, chain_ref, final_ref, sol_ref
    )
    zhalo_ref[...] = zhalo
    lines = dot(jnp.concatenate([wide(x_low), wide(x_high)], axis=0), to_cells())
    for x in range(CX):
        z_ref[x] = jac_ref[x] + lines[(x // 4) * 32 : (x // 4) * 32 + 32]
    write_planes(z_ref[...], (xlo, xhi, ylo, yhi))
    zero = jnp.zeros((1, 128), F32)
    part_ref[...] = jnp.concatenate(coarse_totals(zrec_ref, 4, sizes[2]) + [zero] * 6, axis=0)


FACES = range(1, 7)
TERMS = (
    [("g11", -1, -1), ("g12", -1, -1), ("g22", -1, -1), ("h1", -1, -1), ("h2", -1, -1)]
    + [(name, j, -1) for name in ("h2", "g12", "g22") for j in range(7)]
    + [("g22", 0, j) for j in range(7)]
    + [("g22", j, j) for j in FACES]
    + [("g22", j, k) for j in FACES for k in FACES if j < k and (j - 1) // 2 != (k - 1) // 2]
)
NAMES = ("g11", "g12", "g22", "h1", "h2")
TERMS_AT, TERMS_ROW = 96, 32


def second_kernel(
    sizes, r_ref, w1_ref, sigma_ref, kappa_ref, z_ref, zhalo_ref, part_ref, h0, h1, h2, h3,
    w_ref, xmsg_ref, terms_ref
):
    nx, ny, nz = sizes
    mx, my, mz = lax.axis_index("gx"), lax.axis_index("gy"), lax.axis_index("gz")
    xlo = jnp.where(mx > 0, h0[...], 0.0)
    xhi = jnp.where(mx < nx - 1, h1[...], 0.0)
    ylo = jnp.where(my > 0, h2[...], 0.0)
    yhi = jnp.where(my < ny - 1, h3[...], 0.0)
    face = zhalo_ref[...]
    high, low = jnp.where(mz > 0, face, 0.0), jnp.where(mz < nz - 1, face, 0.0)
    ends = ends_of(jnp.where(iota((8, 128), 1) >= HIGH_AT, high, low))
    apply_operator([z_ref[x] for x in range(CX)], xlo, xhi, ylo, yhi, ends, sigma_ref, kappa_ref, w_ref)

    r, w1, w2, sigma = r_ref[...], w1_ref[...], w_ref[...], sigma_ref[...]
    kz = kappa_ref[2]
    rows = lambda a: jnp.sum(jnp.sum(a, axis=0), axis=0, keepdims=True)
    lane1 = iota((1, 128), 1)
    pick = lambda profile, face: jnp.where(lane1 == (0 if face == 5 else CZ - 1), profile, 0.0)
    low_row = lambda a: jnp.sum(a, axis=0, keepdims=True)
    partner = {"h2": r, "g12": w1, "g22": w2}
    partner_ref = {"h2": r_ref, "g12": w1_ref, "g22": w_ref}
    z_profiles = {name: rows(kz * f) for name, f in partner.items()}
    z_sigma, z_self = rows(kz * sigma), rows(kz * kz)

    def plane(ref, f):
        if f < 3:
            return ref[0 if f == 1 else CX - 1]
        return ref[:, 0 if f == 3 else CY - 1, :]

    face_weight = {f: plane(kappa_ref.at[(f - 1) // 2], f) for f in range(1, 5)}

    def on_face(f, other):
        return low_row(face_weight[f] * plane(other, f))

    def term(name, j, k):
        if j == -1:
            a, b = {"g11": (w1, w1), "g12": (w1, w2), "g22": (w2, w2), "h1": (w1, r), "h2": (w2, r)}[name]
            return rows(a * b)
        if k == -1:
            twice = 2.0 if name == "g22" else 1.0
            if j == 0:
                return twice * rows(sigma * partner[name])
            if j > 4:
                return twice * pick(z_profiles[name], j)
            return twice * on_face(j, partner_ref[name])
        if j == 0:
            if k == 0:
                return rows(sigma * sigma)
            return 2.0 * (pick(z_sigma, k) if k > 4 else on_face(k, sigma_ref))
        if j == k:
            return pick(z_self, j) if j > 4 else on_face(j, kappa_ref.at[(j - 1) // 2])
        if k > 4:
            return 2.0 * pick(on_face(j, kappa_ref.at[2]), k)
        x, y = 0 if j == 1 else CX - 1, 0 if k == 3 else CY - 1
        return 2.0 * kappa_ref[0, x, y : y + 1, :] * kappa_ref[1, x, y : y + 1, :]

    for i, (name, j, k) in enumerate(TERMS):
        terms_ref[i : i + 1, :] = term(name, j, k)
    for i in range(len(TERMS), 128):
        if i % 8 == 0:
            terms_ref[i : i + 8, :] = jnp.zeros((8, 128), F32)
        elif i == len(TERMS):
            stop = -(-i // 8) * 8
            terms_ref[i:stop, :] = jnp.zeros((stop - i, 128), F32)
    poly = dot_t(jnp.full((8, 128), 1.0, F32), terms_ref[...])[0:1, :]
    halves = [
        jnp.where(lane1 < TERMS_AT, part_ref[h : h + 1, :], pltpu.roll(poly, TERMS_AT - TERMS_ROW * h, 1))
        for h in range(2)
    ]
    both = jnp.concatenate(halves, axis=0)
    for q in range(nx * ny):
        xmsg_ref[q] = both


def plane_kernel(sizes, xrec_ref, sums_ref, own_ref, flat_ref):
    nx, ny, nz = sizes
    mx, my, mz = lax.axis_index("gx"), lax.axis_index("gy"), lax.axis_index("gz")
    count = nx * ny
    total = xrec_ref[0]
    for q in range(count):
        for h in range(2):
            flat_ref[h, q : q + 1, :] = xrec_ref[q, h : h + 1, :]
        if q > 0:
            total = total + xrec_ref[q]
    lane, row = iota((count, 128), 1), iota((count, 128), 0)
    tx, ty = row // ny, row % ny

    def value(qx, qy, dz, valid):
        at = (qx & 3) * 24 + 8 + 8 * dz + qy
        chosen = jnp.where(qx < 4, total[0:1, :], total[1:2, :])
        return jnp.sum(jnp.where((lane == at) & valid, chosen, 0.0), axis=1, keepdims=True)

    always = row >= 0
    c = value(tx, ty, 0, always)
    near = [
        value(tx - 1, ty, 0, tx > 0),
        value(tx + 1, ty, 0, tx < nx - 1),
        value(tx, ty - 1, 0, ty > 0),
        value(tx, ty + 1, 0, ty < ny - 1),
        value(tx, ty, -1, always & (mz > 0)),
        value(tx, ty, 1, always & (mz < nz - 1)),
    ]
    v = [c] + [c - n for n in near]
    lane1 = iota((1, 128), 1)
    out = jnp.zeros((1, 128), F32)
    for h in range(2):
        terms = list(enumerate(TERMS[TERMS_ROW * h : TERMS_ROW * (h + 1)], TERMS_AT))
        first = jnp.where(lane < 0, 1.0, 0.0)
        second = first
        for j in range(-1, 7):
            amount = 1.0 if j == -1 else v[j]
            is_first = lane < 0
            is_second = is_first
            for i, (_, a, b) in terms:
                if a == j:
                    is_first = is_first | (lane == i)
                if b == j:
                    is_second = is_second | (lane == i)
            first = jnp.where(is_first, amount, first)
            second = jnp.where(is_second, amount, second)
        weights = jnp.where(lane >= TERMS_AT, flat_ref[h], 0.0)
        added = jnp.sum(weights * first * second, axis=0, keepdims=True)
        for n, name in enumerate(NAMES):
            mask = lane1 < 0
            for i, (of, _, _) in terms:
                if of == name:
                    mask = mask | (lane1 == i)
            add = jnp.sum(jnp.where(mask, added, 0.0), axis=1, keepdims=True)
            out = jnp.where(lane1 == n, out + add, out)
    sums_ref[...] = out
    mine = row == mx * ny + my
    for j in range(7):
        own = jnp.sum(jnp.where(mine & (lane == 0), v[j], 0.0))
        own_ref[j : j + 1, :] = jnp.full((1, 128), own, F32)
    own_ref[7:8, :] = jnp.zeros((1, 128), F32)


def end_kernel(all_ref, own_ref, r_ref, sigma_ref, kappa_ref, z1_ref, w1_ref, z2_ref, w2_ref, field_ref, res_ref):
    sums = all_ref[0]
    for q in range(1, all_ref.shape[0]):
        sums = sums + all_ref[q]
    lane = iota((1, 128), 1)
    spread = lambda i: jnp.sum(jnp.where(lane == i, sums, 0.0), axis=1, keepdims=True)
    g11, g12, g22, h1, h2 = [spread(i) for i in range(5)]
    inv = 1.0 / (g11 * g22 - g12 * g12)
    y1 = (g22 * h1 - g12 * h2) * inv
    y2 = (g11 * h2 - g12 * h1) * inv
    c, xlo, xhi, ylo, yhi, zlo, zhi = [own_ref[j : j + 1, :] for j in range(7)]
    lane32, row32 = iota((CY, 128), 1), iota((CY, 128), 0)
    on_y = jnp.where(row32 == 0, ylo, jnp.where(row32 == CY - 1, yhi, 0.0))
    on_z = jnp.where(lane32 == 0, zlo, jnp.where(lane32 == CZ - 1, zhi, 0.0))
    for x in range(CX):
        w2 = w2_ref[x] + sigma_ref[x] * c + kappa_ref[1, x] * on_y + kappa_ref[2, x] * on_z
        if x == 0:
            w2 = w2 + kappa_ref[0, x] * xlo
        if x == CX - 1:
            w2 = w2 + kappa_ref[0, x] * xhi
        field_ref[x] = y1 * z1_ref[x] + y2 * (z2_ref[x] + c)
        res_ref[x] = r_ref[x] - y1 * w1_ref[x] - y2 * w2


def call(kernel, out_shapes, scratch=(), name=None, inputs=pltpu.VMEM, semaphores=(), limit=24 << 20):
    vmem = pl.BlockSpec(memory_space=pltpu.VMEM)

    def run(*args):
        return pl.pallas_call(
            kernel,
            out_shape=[jax.ShapeDtypeStruct(s, F32) for s in out_shapes],
            in_specs=[pl.BlockSpec(memory_space=inputs)] * len(args),
            out_specs=[vmem] * len(out_shapes),
            scratch_shapes=[pltpu.VMEM(s, F32) for s in scratch] + list(semaphores),
            compiler_params=pltpu.CompilerParams(vmem_limit_bytes=limit),
            name=name,
        )(*args)

    return run


def shards(sizes, r, sigma, kappa, inverse_rows):
    nx, ny, nz = sizes
    field, plane, tile, coarse = (CX, CY, CZ), (CY, CZ), (8, 128), (CELLS, 128)
    planes = [plane, plane, tile, tile]
    to_xy = (nx * ny, 2, 128)

    def halo(parts):
        xlo, xhi, ylo, yhi = parts
        up = lambda n: [(i, i + 1) for i in range(n - 1)]
        down = lambda n: [(i + 1, i) for i in range(n - 1)]
        return (
            lax.ppermute(xhi, "gx", up(nx)),
            lax.ppermute(xlo, "gx", down(nx)),
            lax.ppermute(yhi, "gy", up(ny)),
            lax.ppermute(ylo, "gy", down(ny)),
        )

    def along_z(message):
        return lax.all_to_all(message, "gz", split_axis=0, concat_axis=0, tiled=True)

    def along_xy(message):
        return lax.all_to_all(message, ("gx", "gy"), split_axis=0, concat_axis=0, tiled=True)

    bind = lambda kernel, *a: functools.partial(kernel, sizes, *a)
    zmsg, loc, alpha, spread, *sides = call(
        bind(begin_kernel), [(nz * 5, 1, 128), (3, *coarse), coarse, tile, *planes],
        [field, field, (3, *field), tile], "begin", pltpu.HBM, [pltpu.SemaphoreType.DMA((4,))], 55100 << 10,
    )(r, sigma, kappa, inverse_rows)
    zrec = along_z(zmsg)
    halos = halo(sides)
    xmsg, own, zhalo, chain, final = call(
        bind(first_lines_kernel), [to_xy, tile, tile, (4, nz, 128), tile], [coarse], "lines_first"
    )(zrec, loc, alpha, *halos[2:])
    xrec = along_xy(xmsg)
    z1, w1, jac, zmsg, alpha = call(
        bind(first_kernel), [field, field, field, (nz * 4, 1, 128), coarse], name="operator_first"
    )(r, sigma, kappa, xrec, own, zhalo, *halos, loc, spread)
    zrec = along_z(zmsg)
    part, zhalo, z2, *sides = call(
        bind(second_lines_kernel), [tile, tile, field, *planes], [coarse], "lines_second"
    )(zrec, loc, alpha, chain, final, jac)
    halos = halo(sides)
    w2, xmsg = call(bind(second_kernel), [field, to_xy], [(128, 128)], "operator_second")(
        r, w1, sigma, kappa, z2, zhalo, part, *halos
    )
    xrec = along_xy(xmsg)
    sums, values = call(bind(plane_kernel), [(1, 128), tile], [(2, nx * ny, 128)], "plane")(xrec)
    sums = along_z(jnp.broadcast_to(sums[None], (nz, 1, 128)))
    return tuple(
        call(end_kernel, [field, field], name="end")(sums, values, r, sigma, kappa, z1, w1, z2, w2)
    )


def solution(mesh):
    sizes = (mesh.shape["gx"], mesh.shape["gy"], mesh.shape["gz"])
    spec = P("gx", "gy", "gz")

    def run(r, sigma, kappa, inverse):
        return shards(sizes, r, sigma, kappa, inverse.reshape(8, 128))

    return jax.shard_map(
        run,
        mesh=mesh,
        in_specs=(spec, spec, P(None, "gx", "gy", "gz"), P(("gx", "gy", "gz"), None)),
        out_specs=(spec, spec),
        check_vma=False,
    )
```

```python
import functools

import jax
import jax.numpy as jnp
from jax import lax
from jax.experimental import pallas as pl
from jax.experimental.pallas import tpu as pltpu
from jax.sharding import PartitionSpec as P

CX, CY, CZ = 8, 32, 128
CELLS = 16
LINES = 16
THETA = 1.0 / 128.0
WEIGHT = 0.6
PART_AT, LOW_AT, HIGH_AT = 32, 64, 96
HIGHEST = lax.Precision.HIGHEST
F32 = jnp.float32


def iota(shape, dim):
    return lax.broadcasted_iota(jnp.int32, shape, dim)


def dot(a, b):
    return lax.dot_general(
        a, b, (((1,), (0,)), ((), ())), precision=HIGHEST, preferred_element_type=F32
    )


def dot_t(a, b):
    return lax.dot_general(
        a, b, (((1,), (1,)), ((), ())), precision=HIGHEST, preferred_element_type=F32
    )


def one_where(cond):
    return jnp.where(cond, 1.0, 0.0).astype(F32)


def lines_of(field):
    low = (field[0] + field[1]) + (field[2] + field[3])
    high = (field[4] + field[5]) + (field[6] + field[7])
    stacked = jnp.concatenate([low, high], axis=0)
    by_line = one_where(iota((128, 64), 1) // 4 == iota((128, 64), 0))
    by_cell = one_where(iota((CELLS, 128), 1) // 8 == iota((CELLS, 128), 0))
    return dot_t(by_cell, dot(by_line, stacked))


def faces_of(field):
    shape = (CX, CY, 128)
    here = iota(shape, 2) == (iota(shape, 0) % 4) * 32 + iota(shape, 1)

    def packed(z):
        rows = jnp.sum(jnp.where(here, field[:, :, z : z + 1], 0.0), axis=1)
        halves = [jnp.sum(rows[i : i + 4], axis=0, keepdims=True) for i in (0, 4)]
        return jnp.concatenate(halves, axis=0)

    return packed(0), packed(CZ - 1)


def write_z_message(zmsg_ref, pairs, faces, spread_inverse, total, sizes):
    nz, count = sizes[2], 2 + len(pairs)
    mz = lax.axis_index("gz")
    lane1, lane8, row8 = iota((1, 128), 1), iota((8, 128), 1), iota((8, 128), 0)
    only = lambda v: jnp.where(lane1 < LINES, v, 0.0)
    tails = [pltpu.roll(only(a), 96, 1) + pltpu.roll(only(b), 112, 1) if a is not None else None for a, b in pairs]
    mine = spread_inverse * total
    inside = lane8 // 24 == row8 % 4
    zero = jnp.zeros((1, 128), F32)
    for p in range(nz):
        moved = jnp.where(inside, pltpu.roll(mine, (8 - 8 * p) % 128, 1), 0.0)
        zmsg_ref[p * count] = zero
        zmsg_ref[p * count + 1] = zero
        for h, tail in enumerate(tails):
            row = jnp.sum(moved[4 * h : 4 * h + 4], axis=0, keepdims=True) if h < 2 else zero
            zmsg_ref[p * count + 2 + h] = row if tail is None else row + tail

    @pl.when(mz > 0)
    def _():
        zmsg_ref[(mz - 1) * count] = faces[0][0:1]
        zmsg_ref[(mz - 1) * count + 1] = faces[0][1:2]

    @pl.when(mz < nz - 1)
    def _():
        zmsg_ref[(mz + 1) * count] = faces[1][0:1]
        zmsg_ref[(mz + 1) * count + 1] = faces[1][1:2]


def write_planes(field, planes):
    xlo, xhi, y_one, y_two = planes
    xlo[...] = field[0]
    xhi[...] = field[CX - 1]
    core = lax.axis_index("gx") % 2
    low, high = field[:, 0, :], field[:, CY - 1, :]
    y_one[...] = jnp.where(core == 0, high, low)
    y_two[...] = jnp.where(core == 0, low, high)


def y_halos(y_one, y_two):
    core = lax.axis_index("gx") % 2
    return jnp.where(core == 0, y_one, y_two), jnp.where(core == 0, y_two, y_one)


def begin_kernel(
    sizes, r_hbm, sigma_hbm, kappa_hbm, inv_hbm,
    zmsg_ref, loc_ref, alpha_ref, spread_ref, xlo, xhi, ylo, yhi,
    r_ref, sigma_ref, kappa_ref, inv_ref, sems
):
    pairs = ((kappa_hbm, kappa_ref), (sigma_hbm, sigma_ref), (r_hbm, r_ref), (inv_hbm, inv_ref))
    copies = [pltpu.make_async_copy(a, b, sems.at[i]) for i, (a, b) in enumerate(pairs)]
    for copy in copies:
        copy.start()
    for copy in copies:
        copy.wait()
    r, sigma = r_ref[...], sigma_ref[...]
    kx, ky, kz = kappa_ref[0], kappa_ref[1], kappa_ref[2]
    jac = r * (WEIGHT / (sigma + 2.0 * (kx + ky + kz)))
    write_planes(jac, (xlo, xhi, ylo, yhi))
    unused = iota((CELLS, 128), 1) >= LINES
    e = jnp.where(unused, 1.0, lines_of(sigma))
    g = jnp.where(unused, 1.0, lines_of(kz) * 0.125)
    rhs = lines_of(r)
    row = lambda a, k: a[k : k + 1, :]
    first, mid, last = row(e, 0), row(g, 0), row(e, 1)
    cur_first, cur = row(rhs, 0), row(rhs, 1)
    zero = jnp.zeros((1, 128), F32)
    for c in range(3):
        for k in (0, CELLS - 1):
            loc_ref[c, k : k + 1, :] = zero
    for k in (0, CELLS - 1):
        alpha_ref[k : k + 1, :] = zero
    for k in range(1, CELLS - 1):
        inv = 1.0 / (mid + last + row(g, k))
        mu, gam = mid * inv, row(g, k) * inv
        loc_ref[0, k : k + 1, :] = mu
        loc_ref[1, k : k + 1, :] = gam
        loc_ref[2, k : k + 1, :] = inv
        alpha_ref[k : k + 1, :] = cur * inv
        first = first + mu * last
        mid = mu * row(g, k)
        last = row(e, k + 1) + gam * last
        cur_first = cur_first + mu * cur
        cur = row(rhs, k + 1) + gam * cur
    move = one_where((iota((128, 128), 0) % 16) * 8 + iota((128, 128), 0) // 16 == iota((128, 128), 1))
    plain = dot(inv_ref[...], move)
    step = iota((8, 128), 0) % 4
    spread_inverse = plain
    for k in range(1, 4):
        spread_inverse = jnp.where(step == k, pltpu.roll(plain, 24 * k, 1), spread_inverse)
    spread_ref[...] = spread_inverse
    pairs = [(cur_first, cur), (first, mid), (last, row(g, CELLS - 1))]
    write_z_message(zmsg_ref, pairs, faces_of(jac), spread_inverse, jnp.sum(r), sizes)


def solve_chain(sizes, fresh, zrec_ref, loc_ref, alpha_ref, chain_ref, final_ref, sol_ref):
    nz = sizes[2]
    mz = lax.axis_index("gz")
    count = 5 if fresh else 4
    zero = jnp.zeros((1, 128), F32)
    columns = []
    for h in range(count - 2 if fresh else 1):
        rows = jnp.concatenate([zrec_ref[p * count + 2 + h] for p in range(nz)], axis=0)
        used = iota(rows.shape, 1) < LINES
        for shift in (32, 16):
            columns.append(jnp.where(used, pltpu.roll(rows, shift, 1), 1.0))
    part = lambda p, i: columns[i][p : p + 1, :]

    def mine(i):
        row = pltpu.roll(zrec_ref[mz * count + 2 + i // 2], 32 - 16 * (i % 2), 1)
        return jnp.where(iota((1, 128), 1) < LINES, row, 1.0)

    if fresh:
        one = zero + 1.0
        cond, cond_own, hold, ginv = zero, zero, one, one
        for p in range(nz - 1):
            a, m, b, g = part(p, 2), part(p, 3), part(p, 4), part(p, 5)
            at_first = a + cond
            s = m + at_first
            n = b * s + m * at_first
            inv = 1.0 / (n + g * s)
            chain_ref[0, p : p + 1, :] = g * m * inv
            c2 = g * s * inv
            chain_ref[1, p : p + 1, :] = c2
            cond = g * n * inv
            here = mz == p + 1
            cond_own = jnp.where(here, cond, cond_own)
            hold = jnp.where(here, c2, hold)
            ginv = jnp.where(here, g, ginv)
        left_cond, left_hold, left_ginv = cond_own, hold, 1.0 / ginv
        cond = part(nz - 1, 5)
        cond_own, hold, ginv = cond, one, one
        for p in range(nz - 1, 0, -1):
            a, m, b, g = part(p, 2), part(p, 3), part(p, 4), part(p - 1, 5)
            at_last = b + cond
            s = m + at_last
            n = a * s + m * at_last
            inv = 1.0 / (n + g * s)
            chain_ref[2, p : p + 1, :] = g * m * inv
            c2 = g * s * inv
            chain_ref[3, p : p + 1, :] = c2
            cond = g * n * inv
            here = mz == p - 1
            cond_own = jnp.where(here, cond, cond_own)
            hold = jnp.where(here, c2, hold)
            ginv = jnp.where(here, g, ginv)
        right_cond, right_hold, right_ginv = cond_own, hold, 1.0 / ginv
        for c, p in ((0, nz - 1), (1, nz - 1), (2, 0), (3, 0)):
            chain_ref[c, p : p + 1, :] = zero
        big_a = mine(2) + left_cond
        big_b = mine(4) + right_cond
        m = mine(3)
        det_inv = 1.0 / (big_a * m + big_b * m + big_a * big_b)
        f1, f2, f3 = (big_b + m) * det_inv, m * det_inv, (big_a + m) * det_inv
        final_ref[...] = jnp.concatenate(
            [f1, f2, f3, left_ginv, left_hold, right_ginv, right_hold, zero], axis=0
        )
    else:
        f1, f2, f3, left_ginv, left_hold, right_ginv, right_hold = [
            final_ref[i : i + 1, :] for i in range(7)
        ]
    chain = lambda c, p: chain_ref[c, p : p + 1, :]
    cur, cur_left = zero, zero
    for p in range(nz - 1):
        cur = chain(0, p) * (part(p, 0) + cur) + chain(1, p) * part(p, 1)
        cur_left = jnp.where(mz == p + 1, cur, cur_left)
    cur, cur_right = zero, zero
    for p in range(nz - 1, 0, -1):
        cur = chain(2, p) * (part(p, 1) + cur) + chain(3, p) * part(p, 0)
        cur_right = jnp.where(mz == p - 1, cur, cur_right)
    cur_first = mine(0) + cur_left
    cur_last = mine(1) + cur_right
    sol_first = f1 * cur_first + f2 * cur_last
    sol_last = f2 * cur_first + f3 * cur_last
    below = cur_left * left_ginv + left_hold * sol_first
    above = cur_right * right_ginv + right_hold * sol_last
    sol_ref[0:1, :] = sol_first
    sol_ref[CELLS - 1 : CELLS, :] = sol_last
    value = sol_last
    for k in range(CELLS - 2, 0, -1):
        value = alpha_ref[k : k + 1, :] + loc_ref[0, k : k + 1, :] * sol_first + loc_ref[1, k : k + 1, :] * value
        sol_ref[k : k + 1, :] = value
    lanes16 = iota((CELLS, 128), 1) < LINES
    sol = jnp.where(lanes16, sol_ref[...], 0.0) * THETA

    line, lane = iota((128, 128), 0), iota((128, 128), 1)
    picks = [
        one_where(line == lane // 16),
        one_where(line == 8 + lane // 16),
        one_where((line == (lane // 16) * 8) & (lane < 32)),
        one_where((line == (lane // 16) * 8 + 7) & (lane < 32)),
    ]
    keep = iota((CELLS, 128), 1) % 16 == iota((CELLS, 128), 0)
    x_low, x_high, y_low, y_high = [
        jnp.sum(jnp.where(keep, dot(sol, pick), 0.0), axis=0, keepdims=True) for pick in picks
    ]

    lane8, row8 = iota((8, 128), 1), iota((8, 128), 0)
    of_row = (lane8 // 8 == row8 // 4) & (lane8 < LINES)
    to_high = one_where((lane >= HIGH_AT) & ((lane - HIGH_AT) // 4 == line % 8) & (line < LINES))
    to_low = one_where(
        (lane >= LOW_AT) & (lane < HIGH_AT) & ((lane - LOW_AT) // 4 == line % 8) & (line < LINES)
    )
    lines_part = dot(jnp.where(of_row, below, 0.0), to_high) + dot(jnp.where(of_row, above, 0.0), to_low)
    face = jnp.zeros((8, 128), F32)
    for peer, at in ((jnp.maximum(mz - 1, 0), HIGH_AT), (jnp.minimum(mz + 1, nz - 1), LOW_AT)):
        packed = jnp.where(row8 < 4, zrec_ref[peer * count], zrec_ref[peer * count + 1])
        for k in range(4):
            here = (lane8 // 32 == at // 32) & (row8 % 4 == k)
            face = jnp.where(here, pltpu.roll(packed, (at - 32 * k) % 128, 1), face)
    zhalo = jnp.where(lane8 >= LOW_AT, face + THETA * lines_part, 0.0)
    return x_low, x_high, y_low, y_high, zhalo


def coarse_totals(zrec_ref, count, nz):
    totals = [zrec_ref[2], zrec_ref[3]]
    for p in range(1, nz):
        for h in range(2):
            totals[h] = totals[h] + zrec_ref[p * count + 2 + h]
    return totals


def first_lines_kernel(
    sizes, zrec_ref, loc_ref, alpha_ref, h2, h3, xmsg_ref, own_ref, zhalo_ref, chain_ref, final_ref, sol_ref
):
    nx, ny, nz = sizes
    mx, my = lax.axis_index("gx"), lax.axis_index("gy")
    x_low, x_high, y_low, y_high, zhalo = solve_chain(
        sizes, True, zrec_ref, loc_ref, alpha_ref, chain_ref, final_ref, sol_ref
    )
    zero = jnp.zeros((1, 128), F32)
    own_ref[...] = jnp.concatenate([x_low, x_high] + [zero] * 6, axis=0)
    zhalo_ref[...] = zhalo

    totals = coarse_totals(zrec_ref, 5, nz)
    lane1 = iota((1, 128), 1)

    def block(i, width, at, offset):
        moved = pltpu.roll(totals[i // 4], (at - 24 * (i % 4) - offset) % 128, 1)
        return jnp.where((lane1 >= at) & (lane1 < at + width), moved, 0.0)

    second = iota((2, 128), 0) == 1
    for i in range(nx):
        sums = block(i, 24, PART_AT, 0)
        if i > 0:
            sums = sums + block(i - 1, 8, PART_AT + 24, 8)
        if i < nx - 1:
            sums = sums + block(i + 1, 8, PART_AT + 32, 8)
        both = jnp.where(second, sums, 0.0)
        for j in range(ny):
            xmsg_ref[i * ny + j] = both
    here = mx * ny + my

    @pl.when(mx > 0)
    def _():
        xmsg_ref[here - ny, 0:1, :] = x_low

    @pl.when(mx < nx - 1)
    def _():
        xmsg_ref[here + ny, 0:1, :] = x_high

    @pl.when(my > 0)
    def _():
        xmsg_ref[here - 1, 0:1, :] = y_low

    @pl.when(my < ny - 1)
    def _():
        xmsg_ref[here + 1, 0:1, :] = y_high


def scale(sigma_ref, kappa_ref, x):
    return WEIGHT / (sigma_ref[x] + 2.0 * (kappa_ref[0, x] + kappa_ref[1, x] + kappa_ref[2, x]))


def ends_of(face):
    lane32, row32 = iota((CY, 128), 1), iota((CY, 128), 0)
    diagonal = (lane32 == row32 + HIGH_AT) | (lane32 == row32 + LOW_AT)
    spots = jnp.concatenate([jnp.where(diagonal, face[x : x + 1, :], 0.0) for x in range(CX)], axis=0)
    j, k = iota((128, 128), 0), iota((128, 128), 1)
    to_ends = one_where(((j >= HIGH_AT) & (k == 0)) | ((j >= LOW_AT) & (j < HIGH_AT) & (k == CZ - 1)))
    return dot(spots, to_ends)


def apply_operator(z, xlo, xhi, ylo, yhi, ends, sigma_ref, kappa_ref, w_ref):
    lane32, row32 = iota((CY, 128), 1), iota((CY, 128), 0)
    for x in range(CX):
        here_z = z[x]
        before = z[x - 1] if x > 0 else xlo
        after = z[x + 1] if x < CX - 1 else xhi
        y_less = jnp.where(row32 == 0, ylo[x : x + 1, :], pltpu.roll(here_z, 1, 0))
        y_more = jnp.where(row32 == CY - 1, yhi[x : x + 1, :], pltpu.roll(here_z, CY - 1, 0))
        z_less = jnp.where(lane32 == 0, 0.0, pltpu.roll(here_z, 1, 1))
        z_more = jnp.where(lane32 == CZ - 1, 0.0, pltpu.roll(here_z, CZ - 1, 1))
        twice = 2.0 * here_z
        w_ref[x] = (
            sigma_ref[x] * here_z
            + kappa_ref[0, x] * (twice - before - after)
            + kappa_ref[1, x] * (twice - y_less - y_more)
            + kappa_ref[2, x] * (twice - z_less - z_more - ends[x * 32 : x * 32 + 32])
        )


def wide(row):
    return jnp.where(iota((CY, 128), 1) // 16 == iota((CY, 128), 0) // 4, row, 0.0)


def thin(row):
    return jnp.where(iota((CX, 128), 1) // 16 == iota((CX, 128), 0) // 4, row, 0.0)


def to_cells():
    return one_where(iota((128, 128), 0) % 16 == iota((128, 128), 1) // 8)


def full_direction(sizes, base, xrec_ref, own_ref, zhalo_ref, halos, z_ref):
    nx, ny, nz = sizes
    mx, my, mz = lax.axis_index("gx"), lax.axis_index("gy"), lax.axis_index("gz")
    here = mx * ny + my
    sums = xrec_ref[0, 1:2, :]
    for q in range(1, nx * ny):
        sums = sums + xrec_ref[q, 1:2, :]
    lane1 = iota((1, 128), 1)
    coarse = lambda at: jnp.sum(jnp.where(lane1 == at + my, sums, 0.0))
    c_own = coarse(PART_AT + 8)
    c_zlo, c_zhi = coarse(PART_AT), coarse(PART_AT + 16)
    c_ylo, c_yhi = coarse(PART_AT + 7), coarse(PART_AT + 9)
    c_xlo, c_xhi = coarse(PART_AT + 24), coarse(PART_AT + 32)

    left = xrec_ref[jnp.maximum(here - ny, 0), 0:1, :]
    right = xrec_ref[jnp.minimum(here + ny, nx * ny - 1), 0:1, :]
    front = xrec_ref[jnp.maximum(here - 1, 0), 0:1, :]
    back = xrec_ref[jnp.minimum(here + 1, nx * ny - 1), 0:1, :]
    rows = jnp.concatenate(
        [wide(own_ref[0:1, :]), wide(own_ref[1:2, :]), wide(left), wide(right), thin(front), thin(back)],
        axis=0,
    )
    lines = dot(rows, to_cells())
    xlo, xhi = halos[0][...], halos[1][...]
    ylo, yhi = y_halos(halos[2][...], halos[3][...])
    xlo = jnp.where(mx > 0, xlo + lines[64:96] + c_xlo, 0.0)
    xhi = jnp.where(mx < nx - 1, xhi + lines[96:128] + c_xhi, 0.0)
    ylo = jnp.where(my > 0, ylo + lines[128:136] + c_ylo, 0.0)
    yhi = jnp.where(my < ny - 1, yhi + lines[136:144] + c_yhi, 0.0)
    face = zhalo_ref[...]
    high = jnp.where(mz > 0, face + c_zlo, 0.0)
    low = jnp.where(mz < nz - 1, face + c_zhi, 0.0)
    ends = ends_of(jnp.where(iota((8, 128), 1) >= HIGH_AT, high, low))
    z = [base(x) + lines[(x // 4) * 32 : (x // 4) * 32 + 32] + c_own for x in range(CX)]
    for x in range(CX):
        z_ref[x] = z[x]
    return z, xlo, xhi, ylo, yhi, ends


def first_kernel(
    sizes, r_ref, sigma_ref, kappa_ref, xrec_ref, own_ref, zhalo_ref, h0, h1, h2, h3,
    loc_ref, spread_ref, z_ref, w_ref, jac_ref, zmsg_ref, alpha_ref
):
    scales = [scale(sigma_ref, kappa_ref, x) for x in range(CX)]
    base = lambda x: scales[x] * r_ref[x]
    parts = full_direction(sizes, base, xrec_ref, own_ref, zhalo_ref, (h0, h1, h2, h3), z_ref)
    apply_operator(*parts, sigma_ref, kappa_ref, w_ref)
    field = w_ref[...]
    for x in range(CX):
        jac_ref[x] = scales[x] * w_ref[x]
    rhs = lines_of(field)
    row = lambda a, k: a[k : k + 1, :]
    cur_first, cur = row(rhs, 0), row(rhs, 1)
    zero = jnp.zeros((1, 128), F32)
    for k in (0, CELLS - 1):
        alpha_ref[k : k + 1, :] = zero
    for k in range(1, CELLS - 1):
        alpha_ref[k : k + 1, :] = cur * loc_ref[2, k : k + 1, :]
        cur_first = cur_first + loc_ref[0, k : k + 1, :] * cur
        cur = row(rhs, k + 1) + loc_ref[1, k : k + 1, :] * cur
    write_z_message(
        zmsg_ref, [(cur_first, cur), (None, None)], faces_of(jac_ref[...]), spread_ref[...], jnp.sum(field), sizes
    )


def second_lines_kernel(
    sizes, zrec_ref, loc_ref, alpha_ref, chain_ref, final_ref, jac_ref,
    part_ref, zhalo_ref, z_ref, xlo, xhi, ylo, yhi, sol_ref
):
    x_low, x_high, _, _, zhalo = solve_chain(
        sizes, False, zrec_ref, loc_ref, alpha_ref, chain_ref, final_ref, sol_ref
    )
    zhalo_ref[...] = zhalo
    lines = dot(jnp.concatenate([wide(x_low), wide(x_high)], axis=0), to_cells())
    for x in range(CX):
        z_ref[x] = jac_ref[x] + lines[(x // 4) * 32 : (x // 4) * 32 + 32]
    write_planes(z_ref[...], (xlo, xhi, ylo, yhi))
    zero = jnp.zeros((1, 128), F32)
    part_ref[...] = jnp.concatenate(coarse_totals(zrec_ref, 4, sizes[2]) + [zero] * 6, axis=0)


FACES = range(1, 7)
TERMS = (
    [("g11", -1, -1), ("g12", -1, -1), ("g22", -1, -1), ("h1", -1, -1), ("h2", -1, -1)]
    + [(name, j, -1) for name in ("h2", "g12", "g22") for j in range(7)]
    + [("g22", 0, j) for j in range(7)]
    + [("g22", j, j) for j in FACES]
    + [("g22", j, k) for j in FACES for k in FACES if j < k and (j - 1) // 2 != (k - 1) // 2]
)
NAMES = ("g11", "g12", "g22", "h1", "h2")
TERMS_AT, TERMS_ROW = 96, 32


def second_kernel(
    sizes, r_ref, w1_ref, sigma_ref, kappa_ref, z_ref, zhalo_ref, part_ref, h0, h1, h2, h3,
    w_ref, xmsg_ref, terms_ref
):
    nx, ny, nz = sizes
    mx, my, mz = lax.axis_index("gx"), lax.axis_index("gy"), lax.axis_index("gz")
    xlo = jnp.where(mx > 0, h0[...], 0.0)
    xhi = jnp.where(mx < nx - 1, h1[...], 0.0)
    ylo, yhi = y_halos(h2[...], h3[...])
    ylo = jnp.where(my > 0, ylo, 0.0)
    yhi = jnp.where(my < ny - 1, yhi, 0.0)
    face = zhalo_ref[...]
    high, low = jnp.where(mz > 0, face, 0.0), jnp.where(mz < nz - 1, face, 0.0)
    ends = ends_of(jnp.where(iota((8, 128), 1) >= HIGH_AT, high, low))
    apply_operator([z_ref[x] for x in range(CX)], xlo, xhi, ylo, yhi, ends, sigma_ref, kappa_ref, w_ref)

    r, w1, w2, sigma = r_ref[...], w1_ref[...], w_ref[...], sigma_ref[...]
    kz = kappa_ref[2]
    rows = lambda a: jnp.sum(jnp.sum(a, axis=0), axis=0, keepdims=True)
    lane1 = iota((1, 128), 1)
    pick = lambda profile, face: jnp.where(lane1 == (0 if face == 5 else CZ - 1), profile, 0.0)
    low_row = lambda a: jnp.sum(a, axis=0, keepdims=True)
    partner = {"h2": r, "g12": w1, "g22": w2}
    partner_ref = {"h2": r_ref, "g12": w1_ref, "g22": w_ref}
    z_profiles = {name: rows(kz * f) for name, f in partner.items()}
    z_sigma, z_self = rows(kz * sigma), rows(kz * kz)

    def plane(ref, f):
        if f < 3:
            return ref[0 if f == 1 else CX - 1]
        return ref[:, 0 if f == 3 else CY - 1, :]

    face_weight = {f: plane(kappa_ref.at[(f - 1) // 2], f) for f in range(1, 5)}

    def on_face(f, other):
        return low_row(face_weight[f] * plane(other, f))

    def term(name, j, k):
        if j == -1:
            a, b = {"g11": (w1, w1), "g12": (w1, w2), "g22": (w2, w2), "h1": (w1, r), "h2": (w2, r)}[name]
            return rows(a * b)
        if k == -1:
            twice = 2.0 if name == "g22" else 1.0
            if j == 0:
                return twice * rows(sigma * partner[name])
            if j > 4:
                return twice * pick(z_profiles[name], j)
            return twice * on_face(j, partner_ref[name])
        if j == 0:
            if k == 0:
                return rows(sigma * sigma)
            return 2.0 * (pick(z_sigma, k) if k > 4 else on_face(k, sigma_ref))
        if j == k:
            return pick(z_self, j) if j > 4 else on_face(j, kappa_ref.at[(j - 1) // 2])
        if k > 4:
            return 2.0 * pick(on_face(j, kappa_ref.at[2]), k)
        x, y = 0 if j == 1 else CX - 1, 0 if k == 3 else CY - 1
        return 2.0 * kappa_ref[0, x, y : y + 1, :] * kappa_ref[1, x, y : y + 1, :]

    for i, (name, j, k) in enumerate(TERMS):
        terms_ref[i : i + 1, :] = term(name, j, k)
    for i in range(len(TERMS), 128):
        if i % 8 == 0:
            terms_ref[i : i + 8, :] = jnp.zeros((8, 128), F32)
        elif i == len(TERMS):
            stop = -(-i // 8) * 8
            terms_ref[i:stop, :] = jnp.zeros((stop - i, 128), F32)
    poly = dot_t(jnp.full((8, 128), 1.0, F32), terms_ref[...])[0:1, :]
    halves = [
        jnp.where(lane1 < TERMS_AT, part_ref[h : h + 1, :], pltpu.roll(poly, TERMS_AT - TERMS_ROW * h, 1))
        for h in range(2)
    ]
    both = jnp.concatenate(halves, axis=0)
    for q in range(nx * ny):
        xmsg_ref[q] = both


def plane_kernel(sizes, xrec_ref, sums_ref, own_ref, flat_ref):
    nx, ny, nz = sizes
    mx, my, mz = lax.axis_index("gx"), lax.axis_index("gy"), lax.axis_index("gz")
    count = nx * ny
    total = xrec_ref[0]
    for q in range(count):
        for h in range(2):
            flat_ref[h, q : q + 1, :] = xrec_ref[q, h : h + 1, :]
        if q > 0:
            total = total + xrec_ref[q]
    lane, row = iota((count, 128), 1), iota((count, 128), 0)
    tx, ty = row // ny, row % ny

    def value(qx, qy, dz, valid):
        at = (qx & 3) * 24 + 8 + 8 * dz + qy
        chosen = jnp.where(qx < 4, total[0:1, :], total[1:2, :])
        return jnp.sum(jnp.where((lane == at) & valid, chosen, 0.0), axis=1, keepdims=True)

    always = row >= 0
    c = value(tx, ty, 0, always)
    near = [
        value(tx - 1, ty, 0, tx > 0),
        value(tx + 1, ty, 0, tx < nx - 1),
        value(tx, ty - 1, 0, ty > 0),
        value(tx, ty + 1, 0, ty < ny - 1),
        value(tx, ty, -1, always & (mz > 0)),
        value(tx, ty, 1, always & (mz < nz - 1)),
    ]
    v = [c] + [c - n for n in near]
    lane1 = iota((1, 128), 1)
    out = jnp.zeros((1, 128), F32)
    for h in range(2):
        terms = list(enumerate(TERMS[TERMS_ROW * h : TERMS_ROW * (h + 1)], TERMS_AT))
        first = jnp.where(lane < 0, 1.0, 0.0)
        second = first
        for j in range(-1, 7):
            amount = 1.0 if j == -1 else v[j]
            is_first = lane < 0
            is_second = is_first
            for i, (_, a, b) in terms:
                if a == j:
                    is_first = is_first | (lane == i)
                if b == j:
                    is_second = is_second | (lane == i)
            first = jnp.where(is_first, amount, first)
            second = jnp.where(is_second, amount, second)
        weights = jnp.where(lane >= TERMS_AT, flat_ref[h], 0.0)
        added = jnp.sum(weights * first * second, axis=0, keepdims=True)
        for n, name in enumerate(NAMES):
            mask = lane1 < 0
            for i, (of, _, _) in terms:
                if of == name:
                    mask = mask | (lane1 == i)
            add = jnp.sum(jnp.where(mask, added, 0.0), axis=1, keepdims=True)
            out = jnp.where(lane1 == n, out + add, out)
    sums_ref[...] = out
    mine = row == mx * ny + my
    for j in range(7):
        own = jnp.sum(jnp.where(mine & (lane == 0), v[j], 0.0))
        own_ref[j : j + 1, :] = jnp.full((1, 128), own, F32)
    own_ref[7:8, :] = jnp.zeros((1, 128), F32)


def end_kernel(all_ref, own_ref, r_ref, sigma_ref, kappa_ref, z1_ref, w1_ref, z2_ref, w2_ref, field_ref, res_ref):
    sums = all_ref[0]
    for q in range(1, all_ref.shape[0]):
        sums = sums + all_ref[q]
    lane = iota((1, 128), 1)
    spread = lambda i: jnp.sum(jnp.where(lane == i, sums, 0.0), axis=1, keepdims=True)
    g11, g12, g22, h1, h2 = [spread(i) for i in range(5)]
    inv = 1.0 / (g11 * g22 - g12 * g12)
    y1 = (g22 * h1 - g12 * h2) * inv
    y2 = (g11 * h2 - g12 * h1) * inv
    c, xlo, xhi, ylo, yhi, zlo, zhi = [own_ref[j : j + 1, :] for j in range(7)]
    lane32, row32 = iota((CY, 128), 1), iota((CY, 128), 0)
    on_y = jnp.where(row32 == 0, ylo, jnp.where(row32 == CY - 1, yhi, 0.0))
    on_z = jnp.where(lane32 == 0, zlo, jnp.where(lane32 == CZ - 1, zhi, 0.0))
    for x in range(CX):
        w2 = w2_ref[x] + sigma_ref[x] * c + kappa_ref[1, x] * on_y + kappa_ref[2, x] * on_z
        if x == 0:
            w2 = w2 + kappa_ref[0, x] * xlo
        if x == CX - 1:
            w2 = w2 + kappa_ref[0, x] * xhi
        field_ref[x] = y1 * z1_ref[x] + y2 * (z2_ref[x] + c)
        res_ref[x] = r_ref[x] - y1 * w1_ref[x] - y2 * w2


def call(kernel, out_shapes, scratch=(), name=None, inputs=pltpu.VMEM, semaphores=(), limit=24 << 20):
    vmem = pl.BlockSpec(memory_space=pltpu.VMEM)

    def run(*args):
        return pl.pallas_call(
            kernel,
            out_shape=[jax.ShapeDtypeStruct(s, F32) for s in out_shapes],
            in_specs=[pl.BlockSpec(memory_space=inputs)] * len(args),
            out_specs=[vmem] * len(out_shapes),
            scratch_shapes=[pltpu.VMEM(s, F32) for s in scratch] + list(semaphores),
            compiler_params=pltpu.CompilerParams(vmem_limit_bytes=limit),
            name=name,
        )(*args)

    return run


def shards(sizes, r, sigma, kappa, inverse_rows):
    nx, ny, nz = sizes
    field, plane, tile, coarse = (CX, CY, CZ), (CY, CZ), (8, 128), (CELLS, 128)
    planes = [plane, plane, tile, tile]
    to_xy = (nx * ny, 2, 128)

    fold = []
    for x in range(0, nx, 2):
        ring = [x * ny + y for y in range(ny)] + [(x + 1) * ny + y for y in reversed(range(ny))]
        fold += list(zip(ring, ring[1:] + ring[:1]))
    unfold = [(b, a) for a, b in fold]

    def halo(parts):
        xlo, xhi, y_one, y_two = parts
        return (
            lax.ppermute(xhi, "gx", [(i, (i + 1) % nx) for i in range(nx)]),
            lax.ppermute(xlo, "gx", [((i + 1) % nx, i) for i in range(nx)]),
            lax.ppermute(y_one, ("gx", "gy"), fold),
            lax.ppermute(y_two, ("gx", "gy"), unfold),
        )

    def along_z(message):
        return lax.all_to_all(message, "gz", split_axis=0, concat_axis=0, tiled=True)

    def along_xy(message):
        return lax.all_to_all(message, ("gx", "gy"), split_axis=0, concat_axis=0, tiled=True)

    bind = lambda kernel, *a: functools.partial(kernel, sizes, *a)
    zmsg, loc, alpha, spread, *sides = call(
        bind(begin_kernel), [(nz * 5, 1, 128), (3, *coarse), coarse, tile, *planes],
        [field, field, (3, *field), tile], "begin", pltpu.HBM, [pltpu.SemaphoreType.DMA((4,))], 55100 << 10,
    )(r, sigma, kappa, inverse_rows)
    zrec = along_z(zmsg)
    halos = halo(sides)
    xmsg, own, zhalo, chain, final = call(
        bind(first_lines_kernel), [to_xy, tile, tile, (4, nz, 128), tile], [coarse], "lines_first"
    )(zrec, loc, alpha, *halos[2:])
    xrec = along_xy(xmsg)
    z1, w1, jac, zmsg, alpha = call(
        bind(first_kernel), [field, field, field, (nz * 4, 1, 128), coarse], name="operator_first"
    )(r, sigma, kappa, xrec, own, zhalo, *halos, loc, spread)
    zrec = along_z(zmsg)
    part, zhalo, z2, *sides = call(
        bind(second_lines_kernel), [tile, tile, field, *planes], [coarse], "lines_second"
    )(zrec, loc, alpha, chain, final, jac)
    halos = halo(sides)
    w2, xmsg = call(bind(second_kernel), [field, to_xy], [(128, 128)], "operator_second")(
        r, w1, sigma, kappa, z2, zhalo, part, *halos
    )
    xrec = along_xy(xmsg)
    sums, values = call(bind(plane_kernel), [(1, 128), tile], [(2, nx * ny, 128)], "plane")(xrec)
    sums = along_z(jnp.broadcast_to(sums[None], (nz, 1, 128)))
    return tuple(
        call(end_kernel, [field, field], name="end")(sums, values, r, sigma, kappa, z1, w1, z2, w2)
    )


def solution(mesh):
    sizes = (mesh.shape["gx"], mesh.shape["gy"], mesh.shape["gz"])
    spec = P("gx", "gy", "gz")

    def run(r, sigma, kappa, inverse):
        return shards(sizes, r, sigma, kappa, inverse.reshape(8, 128))

    return jax.shard_map(
        run,
        mesh=mesh,
        in_specs=(spec, spec, P(None, "gx", "gy", "gz"), P(("gx", "gy", "gz"), None)),
        out_specs=(spec, spec),
        check_vma=False,
    )
```

```python
import functools

import jax
import jax.numpy as jnp
from jax import lax
from jax.experimental import pallas as pl
from jax.experimental.pallas import tpu as pltpu
from jax.sharding import PartitionSpec as P

CX, CY, CZ = 8, 32, 128
CELLS = 16
LINES = 16
THETA = 1.0 / 128.0
WEIGHT = 0.6
PART_AT, LOW_AT, HIGH_AT = 32, 64, 96
HIGHEST = lax.Precision.HIGHEST
F32 = jnp.float32


def iota(shape, dim):
    return lax.broadcasted_iota(jnp.int32, shape, dim)


def dot(a, b):
    return lax.dot_general(
        a, b, (((1,), (0,)), ((), ())), precision=HIGHEST, preferred_element_type=F32
    )


def dot_t(a, b):
    return lax.dot_general(
        a, b, (((1,), (1,)), ((), ())), precision=HIGHEST, preferred_element_type=F32
    )


def one_where(cond):
    return jnp.where(cond, 1.0, 0.0).astype(F32)


def lines_of(field):
    low = (field[0] + field[1]) + (field[2] + field[3])
    high = (field[4] + field[5]) + (field[6] + field[7])
    stacked = jnp.concatenate([low, high], axis=0)
    by_line = one_where(iota((128, 64), 1) // 4 == iota((128, 64), 0))
    by_cell = one_where(iota((CELLS, 128), 1) // 8 == iota((CELLS, 128), 0))
    return dot_t(by_cell, dot(by_line, stacked))


def faces_of(field):
    shape = (CX, CY, 128)
    here = iota(shape, 2) == (iota(shape, 0) % 4) * 32 + iota(shape, 1)

    def packed(z):
        rows = jnp.sum(jnp.where(here, field[:, :, z : z + 1], 0.0), axis=1)
        halves = [jnp.sum(rows[i : i + 4], axis=0, keepdims=True) for i in (0, 4)]
        return jnp.concatenate(halves, axis=0)

    return packed(0), packed(CZ - 1)


def write_z_message(zmsg_ref, pairs, faces, spread_inverse, total, sizes):
    nz, count = sizes[2], 2 + len(pairs)
    mz = lax.axis_index("gz")
    lane1, lane8, row8 = iota((1, 128), 1), iota((8, 128), 1), iota((8, 128), 0)
    only = lambda v: jnp.where(lane1 < LINES, v, 0.0)
    tails = [pltpu.roll(only(a), 96, 1) + pltpu.roll(only(b), 112, 1) if a is not None else None for a, b in pairs]
    mine = spread_inverse * total
    inside = lane8 // 24 == row8 % 4
    zero = jnp.zeros((1, 128), F32)
    for p in range(nz):
        moved = jnp.where(inside, pltpu.roll(mine, (8 - 8 * p) % 128, 1), 0.0)
        zmsg_ref[p * count] = zero
        zmsg_ref[p * count + 1] = zero
        for h, tail in enumerate(tails):
            row = jnp.sum(moved[4 * h : 4 * h + 4], axis=0, keepdims=True) if h < 2 else zero
            zmsg_ref[p * count + 2 + h] = row if tail is None else row + tail

    @pl.when(mz > 0)
    def _():
        zmsg_ref[(mz - 1) * count] = faces[0][0:1]
        zmsg_ref[(mz - 1) * count + 1] = faces[0][1:2]

    @pl.when(mz < nz - 1)
    def _():
        zmsg_ref[(mz + 1) * count] = faces[1][0:1]
        zmsg_ref[(mz + 1) * count + 1] = faces[1][1:2]


def write_planes(field, planes):
    x_one, x_two, y_one, y_two = planes
    even = lax.axis_index("gy") % 2 == 0
    low, high = field[0], field[CX - 1]
    x_one[...] = jnp.where(even, high, low)
    x_two[...] = jnp.where(even, low, high)
    even = lax.axis_index("gx") % 2 == 0
    low, high = field[:, 0, :], field[:, CY - 1, :]
    y_one[...] = jnp.where(even, high, low)
    y_two[...] = jnp.where(even, low, high)


def low_and_high(halos):
    x_one, x_two, y_one, y_two = [h[...] for h in halos]
    even_y, even_x = lax.axis_index("gy") % 2 == 0, lax.axis_index("gx") % 2 == 0
    xlo, xhi = jnp.where(even_y, x_one, x_two), jnp.where(even_y, x_two, x_one)
    ylo, yhi = jnp.where(even_x, y_one, y_two), jnp.where(even_x, y_two, y_one)
    return xlo, xhi, ylo, yhi


def begin_kernel(
    sizes, r_hbm, sigma_hbm, kappa_hbm, inv_hbm,
    zmsg_ref, loc_ref, alpha_ref, spread_ref, xlo, xhi, ylo, yhi,
    r_ref, sigma_ref, kappa_ref, inv_ref, sems
):
    pairs = ((kappa_hbm, kappa_ref), (sigma_hbm, sigma_ref), (r_hbm, r_ref), (inv_hbm, inv_ref))
    copies = [pltpu.make_async_copy(a, b, sems.at[i]) for i, (a, b) in enumerate(pairs)]
    for copy in copies:
        copy.start()
    for copy in copies:
        copy.wait()
    r, sigma = r_ref[...], sigma_ref[...]
    kx, ky, kz = kappa_ref[0], kappa_ref[1], kappa_ref[2]
    jac = r * (WEIGHT / (sigma + 2.0 * (kx + ky + kz)))
    write_planes(jac, (xlo, xhi, ylo, yhi))
    unused = iota((CELLS, 128), 1) >= LINES
    e = jnp.where(unused, 1.0, lines_of(sigma))
    g = jnp.where(unused, 1.0, lines_of(kz) * 0.125)
    rhs = lines_of(r)
    row = lambda a, k: a[k : k + 1, :]
    first, mid, last = row(e, 0), row(g, 0), row(e, 1)
    cur_first, cur = row(rhs, 0), row(rhs, 1)
    zero = jnp.zeros((1, 128), F32)
    for c in range(3):
        for k in (0, CELLS - 1):
            loc_ref[c, k : k + 1, :] = zero
    for k in (0, CELLS - 1):
        alpha_ref[k : k + 1, :] = zero
    for k in range(1, CELLS - 1):
        inv = 1.0 / (mid + last + row(g, k))
        mu, gam = mid * inv, row(g, k) * inv
        loc_ref[0, k : k + 1, :] = mu
        loc_ref[1, k : k + 1, :] = gam
        loc_ref[2, k : k + 1, :] = inv
        alpha_ref[k : k + 1, :] = cur * inv
        first = first + mu * last
        mid = mu * row(g, k)
        last = row(e, k + 1) + gam * last
        cur_first = cur_first + mu * cur
        cur = row(rhs, k + 1) + gam * cur
    move = one_where((iota((128, 128), 0) % 16) * 8 + iota((128, 128), 0) // 16 == iota((128, 128), 1))
    plain = dot(inv_ref[...], move)
    step = iota((8, 128), 0) % 4
    spread_inverse = plain
    for k in range(1, 4):
        spread_inverse = jnp.where(step == k, pltpu.roll(plain, 24 * k, 1), spread_inverse)
    spread_ref[...] = spread_inverse
    pairs = [(cur_first, cur), (first, mid), (last, row(g, CELLS - 1))]
    write_z_message(zmsg_ref, pairs, faces_of(jac), spread_inverse, jnp.sum(r), sizes)


def solve_chain(sizes, fresh, zrec_ref, loc_ref, alpha_ref, chain_ref, final_ref, sol_ref):
    nz = sizes[2]
    mz = lax.axis_index("gz")
    count = 5 if fresh else 4
    zero = jnp.zeros((1, 128), F32)
    columns = []
    for h in range(count - 2 if fresh else 1):
        rows = jnp.concatenate([zrec_ref[p * count + 2 + h] for p in range(nz)], axis=0)
        used = iota(rows.shape, 1) < LINES
        for shift in (32, 16):
            columns.append(jnp.where(used, pltpu.roll(rows, shift, 1), 1.0))
    part = lambda p, i: columns[i][p : p + 1, :]

    def mine(i):
        row = pltpu.roll(zrec_ref[mz * count + 2 + i // 2], 32 - 16 * (i % 2), 1)
        return jnp.where(iota((1, 128), 1) < LINES, row, 1.0)

    if fresh:
        one = zero + 1.0
        cond, cond_own, hold, ginv = zero, zero, one, one
        for p in range(nz - 1):
            a, m, b, g = part(p, 2), part(p, 3), part(p, 4), part(p, 5)
            at_first = a + cond
            s = m + at_first
            n = b * s + m * at_first
            inv = 1.0 / (n + g * s)
            chain_ref[0, p : p + 1, :] = g * m * inv
            c2 = g * s * inv
            chain_ref[1, p : p + 1, :] = c2
            cond = g * n * inv
            here = mz == p + 1
            cond_own = jnp.where(here, cond, cond_own)
            hold = jnp.where(here, c2, hold)
            ginv = jnp.where(here, g, ginv)
        left_cond, left_hold, left_ginv = cond_own, hold, 1.0 / ginv
        cond = part(nz - 1, 5)
        cond_own, hold, ginv = cond, one, one
        for p in range(nz - 1, 0, -1):
            a, m, b, g = part(p, 2), part(p, 3), part(p, 4), part(p - 1, 5)
            at_last = b + cond
            s = m + at_last
            n = a * s + m * at_last
            inv = 1.0 / (n + g * s)
            chain_ref[2, p : p + 1, :] = g * m * inv
            c2 = g * s * inv
            chain_ref[3, p : p + 1, :] = c2
            cond = g * n * inv
            here = mz == p - 1
            cond_own = jnp.where(here, cond, cond_own)
            hold = jnp.where(here, c2, hold)
            ginv = jnp.where(here, g, ginv)
        right_cond, right_hold, right_ginv = cond_own, hold, 1.0 / ginv
        for c, p in ((0, nz - 1), (1, nz - 1), (2, 0), (3, 0)):
            chain_ref[c, p : p + 1, :] = zero
        big_a = mine(2) + left_cond
        big_b = mine(4) + right_cond
        m = mine(3)
        det_inv = 1.0 / (big_a * m + big_b * m + big_a * big_b)
        f1, f2, f3 = (big_b + m) * det_inv, m * det_inv, (big_a + m) * det_inv
        final_ref[...] = jnp.concatenate(
            [f1, f2, f3, left_ginv, left_hold, right_ginv, right_hold, zero], axis=0
        )
    else:
        f1, f2, f3, left_ginv, left_hold, right_ginv, right_hold = [
            final_ref[i : i + 1, :] for i in range(7)
        ]
    chain = lambda c, p: chain_ref[c, p : p + 1, :]
    cur, cur_left = zero, zero
    for p in range(nz - 1):
        cur = chain(0, p) * (part(p, 0) + cur) + chain(1, p) * part(p, 1)
        cur_left = jnp.where(mz == p + 1, cur, cur_left)
    cur, cur_right = zero, zero
    for p in range(nz - 1, 0, -1):
        cur = chain(2, p) * (part(p, 1) + cur) + chain(3, p) * part(p, 0)
        cur_right = jnp.where(mz == p - 1, cur, cur_right)
    cur_first = mine(0) + cur_left
    cur_last = mine(1) + cur_right
    sol_first = f1 * cur_first + f2 * cur_last
    sol_last = f2 * cur_first + f3 * cur_last
    below = cur_left * left_ginv + left_hold * sol_first
    above = cur_right * right_ginv + right_hold * sol_last
    sol_ref[0:1, :] = sol_first
    sol_ref[CELLS - 1 : CELLS, :] = sol_last
    value = sol_last
    for k in range(CELLS - 2, 0, -1):
        value = alpha_ref[k : k + 1, :] + loc_ref[0, k : k + 1, :] * sol_first + loc_ref[1, k : k + 1, :] * value
        sol_ref[k : k + 1, :] = value
    lanes16 = iota((CELLS, 128), 1) < LINES
    sol = jnp.where(lanes16, sol_ref[...], 0.0) * THETA

    line, lane = iota((128, 128), 0), iota((128, 128), 1)
    picks = [
        one_where(line == lane // 16),
        one_where(line == 8 + lane // 16),
        one_where((line == (lane // 16) * 8) & (lane < 32)),
        one_where((line == (lane // 16) * 8 + 7) & (lane < 32)),
    ]
    keep = iota((CELLS, 128), 1) % 16 == iota((CELLS, 128), 0)
    x_low, x_high, y_low, y_high = [
        jnp.sum(jnp.where(keep, dot(sol, pick), 0.0), axis=0, keepdims=True) for pick in picks
    ]

    lane8, row8 = iota((8, 128), 1), iota((8, 128), 0)
    of_row = (lane8 // 8 == row8 // 4) & (lane8 < LINES)
    to_high = one_where((lane >= HIGH_AT) & ((lane - HIGH_AT) // 4 == line % 8) & (line < LINES))
    to_low = one_where(
        (lane >= LOW_AT) & (lane < HIGH_AT) & ((lane - LOW_AT) // 4 == line % 8) & (line < LINES)
    )
    lines_part = dot(jnp.where(of_row, below, 0.0), to_high) + dot(jnp.where(of_row, above, 0.0), to_low)
    face = jnp.zeros((8, 128), F32)
    for peer, at in ((jnp.maximum(mz - 1, 0), HIGH_AT), (jnp.minimum(mz + 1, nz - 1), LOW_AT)):
        packed = jnp.where(row8 < 4, zrec_ref[peer * count], zrec_ref[peer * count + 1])
        for k in range(4):
            here = (lane8 // 32 == at // 32) & (row8 % 4 == k)
            face = jnp.where(here, pltpu.roll(packed, (at - 32 * k) % 128, 1), face)
    zhalo = jnp.where(lane8 >= LOW_AT, face + THETA * lines_part, 0.0)
    return x_low, x_high, y_low, y_high, zhalo


def coarse_totals(zrec_ref, count, nz):
    totals = [zrec_ref[2], zrec_ref[3]]
    for p in range(1, nz):
        for h in range(2):
            totals[h] = totals[h] + zrec_ref[p * count + 2 + h]
    return totals


def first_lines_kernel(
    sizes, zrec_ref, loc_ref, alpha_ref, h2, h3, xmsg_ref, own_ref, zhalo_ref, chain_ref, final_ref, sol_ref
):
    nx, ny, nz = sizes
    mx, my = lax.axis_index("gx"), lax.axis_index("gy")
    x_low, x_high, y_low, y_high, zhalo = solve_chain(
        sizes, True, zrec_ref, loc_ref, alpha_ref, chain_ref, final_ref, sol_ref
    )
    zero = jnp.zeros((1, 128), F32)
    own_ref[...] = jnp.concatenate([x_low, x_high] + [zero] * 6, axis=0)
    zhalo_ref[...] = zhalo

    totals = coarse_totals(zrec_ref, 5, nz)
    lane1 = iota((1, 128), 1)

    def block(i, width, at, offset):
        moved = pltpu.roll(totals[i // 4], (at - 24 * (i % 4) - offset) % 128, 1)
        return jnp.where((lane1 >= at) & (lane1 < at + width), moved, 0.0)

    second = iota((2, 128), 0) == 1
    for i in range(nx):
        sums = block(i, 24, PART_AT, 0)
        if i > 0:
            sums = sums + block(i - 1, 8, PART_AT + 24, 8)
        if i < nx - 1:
            sums = sums + block(i + 1, 8, PART_AT + 32, 8)
        both = jnp.where(second, sums, 0.0)
        for j in range(ny):
            xmsg_ref[i * ny + j] = both
    here = mx * ny + my

    @pl.when(mx > 0)
    def _():
        xmsg_ref[here - ny, 0:1, :] = x_low

    @pl.when(mx < nx - 1)
    def _():
        xmsg_ref[here + ny, 0:1, :] = x_high

    @pl.when(my > 0)
    def _():
        xmsg_ref[here - 1, 0:1, :] = y_low

    @pl.when(my < ny - 1)
    def _():
        xmsg_ref[here + 1, 0:1, :] = y_high


def scale(sigma_ref, kappa_ref, x):
    return WEIGHT / (sigma_ref[x] + 2.0 * (kappa_ref[0, x] + kappa_ref[1, x] + kappa_ref[2, x]))


def ends_of(face):
    lane32, row32 = iota((CY, 128), 1), iota((CY, 128), 0)
    diagonal = (lane32 == row32 + HIGH_AT) | (lane32 == row32 + LOW_AT)
    spots = jnp.concatenate([jnp.where(diagonal, face[x : x + 1, :], 0.0) for x in range(CX)], axis=0)
    j, k = iota((128, 128), 0), iota((128, 128), 1)
    to_ends = one_where(((j >= HIGH_AT) & (k == 0)) | ((j >= LOW_AT) & (j < HIGH_AT) & (k == CZ - 1)))
    return dot(spots, to_ends)


def apply_operator(z, xlo, xhi, ylo, yhi, ends, sigma_ref, kappa_ref, w_ref):
    lane32, row32 = iota((CY, 128), 1), iota((CY, 128), 0)
    for x in range(CX):
        here_z = z[x]
        before = z[x - 1] if x > 0 else xlo
        after = z[x + 1] if x < CX - 1 else xhi
        y_less = jnp.where(row32 == 0, ylo[x : x + 1, :], pltpu.roll(here_z, 1, 0))
        y_more = jnp.where(row32 == CY - 1, yhi[x : x + 1, :], pltpu.roll(here_z, CY - 1, 0))
        z_less = jnp.where(lane32 == 0, 0.0, pltpu.roll(here_z, 1, 1))
        z_more = jnp.where(lane32 == CZ - 1, 0.0, pltpu.roll(here_z, CZ - 1, 1))
        twice = 2.0 * here_z
        w_ref[x] = (
            sigma_ref[x] * here_z
            + kappa_ref[0, x] * (twice - before - after)
            + kappa_ref[1, x] * (twice - y_less - y_more)
            + kappa_ref[2, x] * (twice - z_less - z_more - ends[x * 32 : x * 32 + 32])
        )


def wide(row):
    return jnp.where(iota((CY, 128), 1) // 16 == iota((CY, 128), 0) // 4, row, 0.0)


def thin(row):
    return jnp.where(iota((CX, 128), 1) // 16 == iota((CX, 128), 0) // 4, row, 0.0)


def to_cells():
    return one_where(iota((128, 128), 0) % 16 == iota((128, 128), 1) // 8)


def full_direction(sizes, base, xrec_ref, own_ref, zhalo_ref, halos, z_ref):
    nx, ny, nz = sizes
    mx, my, mz = lax.axis_index("gx"), lax.axis_index("gy"), lax.axis_index("gz")
    here = mx * ny + my
    sums = xrec_ref[0, 1:2, :]
    for q in range(1, nx * ny):
        sums = sums + xrec_ref[q, 1:2, :]
    lane1 = iota((1, 128), 1)
    coarse = lambda at: jnp.sum(jnp.where(lane1 == at + my, sums, 0.0))
    c_own = coarse(PART_AT + 8)
    c_zlo, c_zhi = coarse(PART_AT), coarse(PART_AT + 16)
    c_ylo, c_yhi = coarse(PART_AT + 7), coarse(PART_AT + 9)
    c_xlo, c_xhi = coarse(PART_AT + 24), coarse(PART_AT + 32)

    left = xrec_ref[jnp.maximum(here - ny, 0), 0:1, :]
    right = xrec_ref[jnp.minimum(here + ny, nx * ny - 1), 0:1, :]
    front = xrec_ref[jnp.maximum(here - 1, 0), 0:1, :]
    back = xrec_ref[jnp.minimum(here + 1, nx * ny - 1), 0:1, :]
    rows = jnp.concatenate(
        [wide(own_ref[0:1, :]), wide(own_ref[1:2, :]), wide(left), wide(right), thin(front), thin(back)],
        axis=0,
    )
    lines = dot(rows, to_cells())
    xlo, xhi, ylo, yhi = low_and_high(halos)
    xlo = jnp.where(mx > 0, xlo + lines[64:96] + c_xlo, 0.0)
    xhi = jnp.where(mx < nx - 1, xhi + lines[96:128] + c_xhi, 0.0)
    ylo = jnp.where(my > 0, ylo + lines[128:136] + c_ylo, 0.0)
    yhi = jnp.where(my < ny - 1, yhi + lines[136:144] + c_yhi, 0.0)
    face = zhalo_ref[...]
    high = jnp.where(mz > 0, face + c_zlo, 0.0)
    low = jnp.where(mz < nz - 1, face + c_zhi, 0.0)
    ends = ends_of(jnp.where(iota((8, 128), 1) >= HIGH_AT, high, low))
    z = [base(x) + lines[(x // 4) * 32 : (x // 4) * 32 + 32] + c_own for x in range(CX)]
    for x in range(CX):
        z_ref[x] = z[x]
    return z, xlo, xhi, ylo, yhi, ends


def first_kernel(
    sizes, r_ref, sigma_ref, kappa_ref, xrec_ref, own_ref, zhalo_ref, h0, h1, h2, h3,
    loc_ref, spread_ref, z_ref, w_ref, jac_ref, zmsg_ref, alpha_ref
):
    scales = [scale(sigma_ref, kappa_ref, x) for x in range(CX)]
    base = lambda x: scales[x] * r_ref[x]
    parts = full_direction(sizes, base, xrec_ref, own_ref, zhalo_ref, (h0, h1, h2, h3), z_ref)
    apply_operator(*parts, sigma_ref, kappa_ref, w_ref)
    field = w_ref[...]
    for x in range(CX):
        jac_ref[x] = scales[x] * w_ref[x]
    rhs = lines_of(field)
    row = lambda a, k: a[k : k + 1, :]
    cur_first, cur = row(rhs, 0), row(rhs, 1)
    zero = jnp.zeros((1, 128), F32)
    for k in (0, CELLS - 1):
        alpha_ref[k : k + 1, :] = zero
    for k in range(1, CELLS - 1):
        alpha_ref[k : k + 1, :] = cur * loc_ref[2, k : k + 1, :]
        cur_first = cur_first + loc_ref[0, k : k + 1, :] * cur
        cur = row(rhs, k + 1) + loc_ref[1, k : k + 1, :] * cur
    write_z_message(
        zmsg_ref, [(cur_first, cur), (None, None)], faces_of(jac_ref[...]), spread_ref[...], jnp.sum(field), sizes
    )


def second_lines_kernel(
    sizes, zrec_ref, loc_ref, alpha_ref, chain_ref, final_ref, jac_ref,
    part_ref, zhalo_ref, z_ref, xlo, xhi, ylo, yhi, sol_ref
):
    x_low, x_high, _, _, zhalo = solve_chain(
        sizes, False, zrec_ref, loc_ref, alpha_ref, chain_ref, final_ref, sol_ref
    )
    zhalo_ref[...] = zhalo
    lines = dot(jnp.concatenate([wide(x_low), wide(x_high)], axis=0), to_cells())
    for x in range(CX):
        z_ref[x] = jac_ref[x] + lines[(x // 4) * 32 : (x // 4) * 32 + 32]
    write_planes(z_ref[...], (xlo, xhi, ylo, yhi))
    zero = jnp.zeros((1, 128), F32)
    part_ref[...] = jnp.concatenate(coarse_totals(zrec_ref, 4, sizes[2]) + [zero] * 6, axis=0)


FACES = range(1, 7)
TERMS = (
    [("g11", -1, -1), ("g12", -1, -1), ("g22", -1, -1), ("h1", -1, -1), ("h2", -1, -1)]
    + [(name, j, -1) for name in ("h2", "g12", "g22") for j in range(7)]
    + [("g22", 0, j) for j in range(7)]
    + [("g22", j, j) for j in FACES]
    + [("g22", j, k) for j in FACES for k in FACES if j < k and (j - 1) // 2 != (k - 1) // 2]
)
NAMES = ("g11", "g12", "g22", "h1", "h2")
TERMS_AT, TERMS_ROW = 96, 32


def second_kernel(
    sizes, r_ref, w1_ref, sigma_ref, kappa_ref, z_ref, zhalo_ref, part_ref, h0, h1, h2, h3,
    w_ref, xmsg_ref, terms_ref
):
    nx, ny, nz = sizes
    mx, my, mz = lax.axis_index("gx"), lax.axis_index("gy"), lax.axis_index("gz")
    xlo, xhi, ylo, yhi = low_and_high((h0, h1, h2, h3))
    xlo = jnp.where(mx > 0, xlo, 0.0)
    xhi = jnp.where(mx < nx - 1, xhi, 0.0)
    ylo = jnp.where(my > 0, ylo, 0.0)
    yhi = jnp.where(my < ny - 1, yhi, 0.0)
    face = zhalo_ref[...]
    high, low = jnp.where(mz > 0, face, 0.0), jnp.where(mz < nz - 1, face, 0.0)
    ends = ends_of(jnp.where(iota((8, 128), 1) >= HIGH_AT, high, low))
    apply_operator([z_ref[x] for x in range(CX)], xlo, xhi, ylo, yhi, ends, sigma_ref, kappa_ref, w_ref)

    r, w1, w2, sigma = r_ref[...], w1_ref[...], w_ref[...], sigma_ref[...]
    kz = kappa_ref[2]
    rows = lambda a: jnp.sum(jnp.sum(a, axis=0), axis=0, keepdims=True)
    lane1 = iota((1, 128), 1)
    pick = lambda profile, face: jnp.where(lane1 == (0 if face == 5 else CZ - 1), profile, 0.0)
    low_row = lambda a: jnp.sum(a, axis=0, keepdims=True)
    partner = {"h2": r, "g12": w1, "g22": w2}
    partner_ref = {"h2": r_ref, "g12": w1_ref, "g22": w_ref}
    z_profiles = {name: rows(kz * f) for name, f in partner.items()}
    z_sigma, z_self = rows(kz * sigma), rows(kz * kz)

    def plane(ref, f):
        if f < 3:
            return ref[0 if f == 1 else CX - 1]
        return ref[:, 0 if f == 3 else CY - 1, :]

    face_weight = {f: plane(kappa_ref.at[(f - 1) // 2], f) for f in range(1, 5)}

    def on_face(f, other):
        return low_row(face_weight[f] * plane(other, f))

    def term(name, j, k):
        if j == -1:
            a, b = {"g11": (w1, w1), "g12": (w1, w2), "g22": (w2, w2), "h1": (w1, r), "h2": (w2, r)}[name]
            return rows(a * b)
        if k == -1:
            twice = 2.0 if name == "g22" else 1.0
            if j == 0:
                return twice * rows(sigma * partner[name])
            if j > 4:
                return twice * pick(z_profiles[name], j)
            return twice * on_face(j, partner_ref[name])
        if j == 0:
            if k == 0:
                return rows(sigma * sigma)
            return 2.0 * (pick(z_sigma, k) if k > 4 else on_face(k, sigma_ref))
        if j == k:
            return pick(z_self, j) if j > 4 else on_face(j, kappa_ref.at[(j - 1) // 2])
        if k > 4:
            return 2.0 * pick(on_face(j, kappa_ref.at[2]), k)
        x, y = 0 if j == 1 else CX - 1, 0 if k == 3 else CY - 1
        return 2.0 * kappa_ref[0, x, y : y + 1, :] * kappa_ref[1, x, y : y + 1, :]

    for i, (name, j, k) in enumerate(TERMS):
        terms_ref[i : i + 1, :] = term(name, j, k)
    for i in range(len(TERMS), 128):
        if i % 8 == 0:
            terms_ref[i : i + 8, :] = jnp.zeros((8, 128), F32)
        elif i == len(TERMS):
            stop = -(-i // 8) * 8
            terms_ref[i:stop, :] = jnp.zeros((stop - i, 128), F32)
    poly = dot_t(jnp.full((8, 128), 1.0, F32), terms_ref[...])[0:1, :]
    halves = [
        jnp.where(lane1 < TERMS_AT, part_ref[h : h + 1, :], pltpu.roll(poly, TERMS_AT - TERMS_ROW * h, 1))
        for h in range(2)
    ]
    both = jnp.concatenate(halves, axis=0)
    for q in range(nx * ny):
        xmsg_ref[q] = both


def plane_kernel(sizes, xrec_ref, sums_ref, own_ref, flat_ref):
    nx, ny, nz = sizes
    mx, my, mz = lax.axis_index("gx"), lax.axis_index("gy"), lax.axis_index("gz")
    count = nx * ny
    total = xrec_ref[0]
    for q in range(count):
        for h in range(2):
            flat_ref[h, q : q + 1, :] = xrec_ref[q, h : h + 1, :]
        if q > 0:
            total = total + xrec_ref[q]
    lane, row = iota((count, 128), 1), iota((count, 128), 0)
    tx, ty = row // ny, row % ny

    def value(qx, qy, dz, valid):
        at = (qx & 3) * 24 + 8 + 8 * dz + qy
        chosen = jnp.where(qx < 4, total[0:1, :], total[1:2, :])
        return jnp.sum(jnp.where((lane == at) & valid, chosen, 0.0), axis=1, keepdims=True)

    always = row >= 0
    c = value(tx, ty, 0, always)
    near = [
        value(tx - 1, ty, 0, tx > 0),
        value(tx + 1, ty, 0, tx < nx - 1),
        value(tx, ty - 1, 0, ty > 0),
        value(tx, ty + 1, 0, ty < ny - 1),
        value(tx, ty, -1, always & (mz > 0)),
        value(tx, ty, 1, always & (mz < nz - 1)),
    ]
    v = [c] + [c - n for n in near]
    lane1 = iota((1, 128), 1)
    out = jnp.zeros((1, 128), F32)
    for h in range(2):
        terms = list(enumerate(TERMS[TERMS_ROW * h : TERMS_ROW * (h + 1)], TERMS_AT))
        first = jnp.where(lane < 0, 1.0, 0.0)
        second = first
        for j in range(-1, 7):
            amount = 1.0 if j == -1 else v[j]
            is_first = lane < 0
            is_second = is_first
            for i, (_, a, b) in terms:
                if a == j:
                    is_first = is_first | (lane == i)
                if b == j:
                    is_second = is_second | (lane == i)
            first = jnp.where(is_first, amount, first)
            second = jnp.where(is_second, amount, second)
        weights = jnp.where(lane >= TERMS_AT, flat_ref[h], 0.0)
        added = jnp.sum(weights * first * second, axis=0, keepdims=True)
        for n, name in enumerate(NAMES):
            mask = lane1 < 0
            for i, (of, _, _) in terms:
                if of == name:
                    mask = mask | (lane1 == i)
            add = jnp.sum(jnp.where(mask, added, 0.0), axis=1, keepdims=True)
            out = jnp.where(lane1 == n, out + add, out)
    sums_ref[...] = out
    mine = row == mx * ny + my
    for j in range(7):
        own = jnp.sum(jnp.where(mine & (lane == 0), v[j], 0.0))
        own_ref[j : j + 1, :] = jnp.full((1, 128), own, F32)
    own_ref[7:8, :] = jnp.zeros((1, 128), F32)


def end_kernel(all_ref, own_ref, r_ref, sigma_ref, kappa_ref, z1_ref, w1_ref, z2_ref, w2_ref, field_ref, res_ref):
    sums = all_ref[0]
    for q in range(1, all_ref.shape[0]):
        sums = sums + all_ref[q]
    lane = iota((1, 128), 1)
    spread = lambda i: jnp.sum(jnp.where(lane == i, sums, 0.0), axis=1, keepdims=True)
    g11, g12, g22, h1, h2 = [spread(i) for i in range(5)]
    inv = 1.0 / (g11 * g22 - g12 * g12)
    y1 = (g22 * h1 - g12 * h2) * inv
    y2 = (g11 * h2 - g12 * h1) * inv
    c, xlo, xhi, ylo, yhi, zlo, zhi = [own_ref[j : j + 1, :] for j in range(7)]
    lane32, row32 = iota((CY, 128), 1), iota((CY, 128), 0)
    on_y = jnp.where(row32 == 0, ylo, jnp.where(row32 == CY - 1, yhi, 0.0))
    on_z = jnp.where(lane32 == 0, zlo, jnp.where(lane32 == CZ - 1, zhi, 0.0))
    for x in range(CX):
        w2 = w2_ref[x] + sigma_ref[x] * c + kappa_ref[1, x] * on_y + kappa_ref[2, x] * on_z
        if x == 0:
            w2 = w2 + kappa_ref[0, x] * xlo
        if x == CX - 1:
            w2 = w2 + kappa_ref[0, x] * xhi
        field_ref[x] = y1 * z1_ref[x] + y2 * (z2_ref[x] + c)
        res_ref[x] = r_ref[x] - y1 * w1_ref[x] - y2 * w2


def call(kernel, out_shapes, scratch=(), name=None, inputs=pltpu.VMEM, semaphores=(), limit=24 << 20):
    vmem = pl.BlockSpec(memory_space=pltpu.VMEM)

    def run(*args):
        return pl.pallas_call(
            kernel,
            out_shape=[jax.ShapeDtypeStruct(s, F32) for s in out_shapes],
            in_specs=[pl.BlockSpec(memory_space=inputs)] * len(args),
            out_specs=[vmem] * len(out_shapes),
            scratch_shapes=[pltpu.VMEM(s, F32) for s in scratch] + list(semaphores),
            compiler_params=pltpu.CompilerParams(vmem_limit_bytes=limit),
            name=name,
        )(*args)

    return run


def shards(sizes, r, sigma, kappa, inverse_rows):
    nx, ny, nz = sizes
    field, plane, tile, coarse = (CX, CY, CZ), (CY, CZ), (8, 128), (CELLS, 128)
    planes = [plane, plane, tile, tile]
    to_xy = (nx * ny, 2, 128)

    def folded(lanes):
        pairs = []
        for up, down in lanes:
            ring = up + down[::-1]
            pairs += zip(ring, ring[1:] + ring[:1])
        return pairs

    along_x = folded([[[x * ny + y + k for x in range(nx)] for k in (0, 1)] for y in range(0, ny, 2)])
    along_y = folded([[[(x + k) * ny + y for y in range(ny)] for k in (0, 1)] for x in range(0, nx, 2)])
    back = lambda pairs: [(b, a) for a, b in pairs]

    def halo(parts):
        rings = (along_x, back(along_x), along_y, back(along_y))
        return tuple(lax.ppermute(p, ("gx", "gy"), ring) for p, ring in zip(parts, rings))

    def along_z(message):
        return lax.all_to_all(message, "gz", split_axis=0, concat_axis=0, tiled=True)

    def along_xy(message):
        return lax.all_to_all(message, ("gx", "gy"), split_axis=0, concat_axis=0, tiled=True)

    bind = lambda kernel, *a: functools.partial(kernel, sizes, *a)
    zmsg, loc, alpha, spread, *sides = call(
        bind(begin_kernel), [(nz * 5, 1, 128), (3, *coarse), coarse, tile, *planes],
        [field, field, (3, *field), tile], "begin", pltpu.HBM, [pltpu.SemaphoreType.DMA((4,))], 55100 << 10,
    )(r, sigma, kappa, inverse_rows)
    zrec = along_z(zmsg)
    halos = halo(sides)
    xmsg, own, zhalo, chain, final = call(
        bind(first_lines_kernel), [to_xy, tile, tile, (4, nz, 128), tile], [coarse], "lines_first"
    )(zrec, loc, alpha, *halos[2:])
    xrec = along_xy(xmsg)
    z1, w1, jac, zmsg, alpha = call(
        bind(first_kernel), [field, field, field, (nz * 4, 1, 128), coarse], name="operator_first"
    )(r, sigma, kappa, xrec, own, zhalo, *halos, loc, spread)
    zrec = along_z(zmsg)
    part, zhalo, z2, *sides = call(
        bind(second_lines_kernel), [tile, tile, field, *planes], [coarse], "lines_second"
    )(zrec, loc, alpha, chain, final, jac)
    halos = halo(sides)
    w2, xmsg = call(bind(second_kernel), [field, to_xy], [(128, 128)], "operator_second")(
        r, w1, sigma, kappa, z2, zhalo, part, *halos
    )
    xrec = along_xy(xmsg)
    sums, values = call(bind(plane_kernel), [(1, 128), tile], [(2, nx * ny, 128)], "plane")(xrec)
    sums = along_z(jnp.broadcast_to(sums[None], (nz, 1, 128)))
    return tuple(
        call(end_kernel, [field, field], name="end")(sums, values, r, sigma, kappa, z1, w1, z2, w2)
    )


def solution(mesh):
    sizes = (mesh.shape["gx"], mesh.shape["gy"], mesh.shape["gz"])
    spec = P("gx", "gy", "gz")

    def run(r, sigma, kappa, inverse):
        return shards(sizes, r, sigma, kappa, inverse.reshape(8, 128))

    return jax.shard_map(
        run,
        mesh=mesh,
        in_specs=(spec, spec, P(None, "gx", "gy", "gz"), P(("gx", "gy", "gz"), None)),
        out_specs=(spec, spec),
        check_vma=False,
    )
```

```python
import functools

import jax
import jax.numpy as jnp
from jax import lax
from jax.experimental import pallas as pl
from jax.experimental.pallas import tpu as pltpu
from jax.sharding import PartitionSpec as P

CX, CY, CZ = 8, 32, 128
CELLS = 16
LINES = 16
THETA = 1.0 / 128.0
WEIGHT = 0.6
PART_AT, LOW_AT, HIGH_AT = 32, 64, 96
HIGHEST = lax.Precision.HIGHEST
F32 = jnp.float32


def iota(shape, dim):
    return lax.broadcasted_iota(jnp.int32, shape, dim)


def dot(a, b):
    return lax.dot_general(
        a, b, (((1,), (0,)), ((), ())), precision=HIGHEST, preferred_element_type=F32
    )


def dot_t(a, b):
    return lax.dot_general(
        a, b, (((1,), (1,)), ((), ())), precision=HIGHEST, preferred_element_type=F32
    )


def one_where(cond):
    return jnp.where(cond, 1.0, 0.0).astype(F32)


def lines_of(field):
    low = (field[0] + field[1]) + (field[2] + field[3])
    high = (field[4] + field[5]) + (field[6] + field[7])
    stacked = jnp.concatenate([low, high], axis=0)
    by_line = one_where(iota((128, 64), 1) // 4 == iota((128, 64), 0))
    by_cell = one_where(iota((CELLS, 128), 1) // 8 == iota((CELLS, 128), 0))
    return dot_t(by_cell, dot(by_line, stacked))


def faces_of(field):
    shape = (CX, CY, 128)
    here = iota(shape, 2) == (iota(shape, 0) % 4) * 32 + iota(shape, 1)

    def packed(z):
        rows = jnp.sum(jnp.where(here, field[:, :, z : z + 1], 0.0), axis=1)
        halves = [jnp.sum(rows[i : i + 4], axis=0, keepdims=True) for i in (0, 4)]
        return jnp.concatenate(halves, axis=0)

    return packed(0), packed(CZ - 1)


def write_z_message(zmsg_ref, pairs, faces, spread_inverse, total, sizes):
    nz, count = sizes[2], 2 + len(pairs)
    mz = lax.axis_index("gz")
    lane1, lane8, row8 = iota((1, 128), 1), iota((8, 128), 1), iota((8, 128), 0)
    only = lambda v: jnp.where(lane1 < LINES, v, 0.0)
    tails = [pltpu.roll(only(a), 96, 1) + pltpu.roll(only(b), 112, 1) if a is not None else None for a, b in pairs]
    mine = spread_inverse * total
    inside = lane8 // 24 == row8 % 4
    zero = jnp.zeros((1, 128), F32)
    for p in range(nz):
        moved = jnp.where(inside, pltpu.roll(mine, (8 - 8 * p) % 128, 1), 0.0)
        zmsg_ref[p * count] = zero
        zmsg_ref[p * count + 1] = zero
        for h, tail in enumerate(tails):
            row = jnp.sum(moved[4 * h : 4 * h + 4], axis=0, keepdims=True) if h < 2 else zero
            zmsg_ref[p * count + 2 + h] = row if tail is None else row + tail

    @pl.when(mz > 0)
    def _():
        zmsg_ref[(mz - 1) * count] = faces[0][0:1]
        zmsg_ref[(mz - 1) * count + 1] = faces[0][1:2]

    @pl.when(mz < nz - 1)
    def _():
        zmsg_ref[(mz + 1) * count] = faces[1][0:1]
        zmsg_ref[(mz + 1) * count + 1] = faces[1][1:2]


def write_planes(field, planes):
    xlo, xhi, y_one, y_two = planes
    xlo[...] = field[0]
    xhi[...] = field[CX - 1]
    core = lax.axis_index("gx") % 2
    low, high = field[:, 0, :], field[:, CY - 1, :]
    y_one[...] = jnp.where(core == 0, high, low)
    y_two[...] = jnp.where(core == 0, low, high)


def y_halos(y_one, y_two):
    core = lax.axis_index("gx") % 2
    return jnp.where(core == 0, y_one, y_two), jnp.where(core == 0, y_two, y_one)


def begin_kernel(
    sizes, r_hbm, sigma_hbm, kappa_hbm, inv_hbm,
    zmsg_ref, loc_ref, alpha_ref, spread_ref, xlo, xhi, ylo, yhi,
    r_ref, sigma_ref, kappa_ref, inv_ref, sems
):
    pairs = ((kappa_hbm, kappa_ref), (sigma_hbm, sigma_ref), (r_hbm, r_ref), (inv_hbm, inv_ref))
    copies = [pltpu.make_async_copy(a, b, sems.at[i]) for i, (a, b) in enumerate(pairs)]
    for copy in copies:
        copy.start()
    for copy in copies:
        copy.wait()
    r, sigma = r_ref[...], sigma_ref[...]
    kx, ky, kz = kappa_ref[0], kappa_ref[1], kappa_ref[2]
    jac = r * (WEIGHT / (sigma + 2.0 * (kx + ky + kz)))
    write_planes(jac, (xlo, xhi, ylo, yhi))
    unused = iota((CELLS, 128), 1) >= LINES
    e = jnp.where(unused, 1.0, lines_of(sigma))
    g = jnp.where(unused, 1.0, lines_of(kz) * 0.125)
    rhs = lines_of(r)
    row = lambda a, k: a[k : k + 1, :]
    first, mid, last = row(e, 0), row(g, 0), row(e, 1)
    cur_first, cur = row(rhs, 0), row(rhs, 1)
    zero = jnp.zeros((1, 128), F32)
    for c in range(3):
        for k in (0, CELLS - 1):
            loc_ref[c, k : k + 1, :] = zero
    for k in (0, CELLS - 1):
        alpha_ref[k : k + 1, :] = zero
    for k in range(1, CELLS - 1):
        inv = 1.0 / (mid + last + row(g, k))
        mu, gam = mid * inv, row(g, k) * inv
        loc_ref[0, k : k + 1, :] = mu
        loc_ref[1, k : k + 1, :] = gam
        loc_ref[2, k : k + 1, :] = inv
        alpha_ref[k : k + 1, :] = cur * inv
        first = first + mu * last
        mid = mu * row(g, k)
        last = row(e, k + 1) + gam * last
        cur_first = cur_first + mu * cur
        cur = row(rhs, k + 1) + gam * cur
    move = one_where((iota((128, 128), 0) % 16) * 8 + iota((128, 128), 0) // 16 == iota((128, 128), 1))
    plain = dot(inv_ref[...], move)
    step = iota((8, 128), 0) % 4
    spread_inverse = plain
    for k in range(1, 4):
        spread_inverse = jnp.where(step == k, pltpu.roll(plain, 24 * k, 1), spread_inverse)
    spread_ref[...] = spread_inverse
    pairs = [(cur_first, cur), (first, mid), (last, row(g, CELLS - 1))]
    write_z_message(zmsg_ref, pairs, faces_of(jac), spread_inverse, jnp.sum(r), sizes)


def solve_chain(sizes, fresh, zrec_ref, loc_ref, alpha_ref, chain_ref, final_ref, sol_ref):
    nz = sizes[2]
    mz = lax.axis_index("gz")
    count = 5 if fresh else 4
    zero = jnp.zeros((1, 128), F32)
    columns = []
    for h in range(count - 2 if fresh else 1):
        rows = jnp.concatenate([zrec_ref[p * count + 2 + h] for p in range(nz)], axis=0)
        used = iota(rows.shape, 1) < LINES
        for shift in (32, 16):
            columns.append(jnp.where(used, pltpu.roll(rows, shift, 1), 1.0))
    part = lambda p, i: columns[i][p : p + 1, :]

    def mine(i):
        row = pltpu.roll(zrec_ref[mz * count + 2 + i // 2], 32 - 16 * (i % 2), 1)
        return jnp.where(iota((1, 128), 1) < LINES, row, 1.0)

    if fresh:
        one = zero + 1.0
        cond, cond_own, hold, ginv = zero, zero, one, one
        for p in range(nz - 1):
            a, m, b, g = part(p, 2), part(p, 3), part(p, 4), part(p, 5)
            at_first = a + cond
            s = m + at_first
            n = b * s + m * at_first
            inv = 1.0 / (n + g * s)
            chain_ref[0, p : p + 1, :] = g * m * inv
            c2 = g * s * inv
            chain_ref[1, p : p + 1, :] = c2
            cond = g * n * inv
            here = mz == p + 1
            cond_own = jnp.where(here, cond, cond_own)
            hold = jnp.where(here, c2, hold)
            ginv = jnp.where(here, g, ginv)
        left_cond, left_hold, left_ginv = cond_own, hold, 1.0 / ginv
        cond = part(nz - 1, 5)
        cond_own, hold, ginv = cond, one, one
        for p in range(nz - 1, 0, -1):
            a, m, b, g = part(p, 2), part(p, 3), part(p, 4), part(p - 1, 5)
            at_last = b + cond
            s = m + at_last
            n = a * s + m * at_last
            inv = 1.0 / (n + g * s)
            chain_ref[2, p : p + 1, :] = g * m * inv
            c2 = g * s * inv
            chain_ref[3, p : p + 1, :] = c2
            cond = g * n * inv
            here = mz == p - 1
            cond_own = jnp.where(here, cond, cond_own)
            hold = jnp.where(here, c2, hold)
            ginv = jnp.where(here, g, ginv)
        right_cond, right_hold, right_ginv = cond_own, hold, 1.0 / ginv
        for c, p in ((0, nz - 1), (1, nz - 1), (2, 0), (3, 0)):
            chain_ref[c, p : p + 1, :] = zero
        big_a = mine(2) + left_cond
        big_b = mine(4) + right_cond
        m = mine(3)
        det_inv = 1.0 / (big_a * m + big_b * m + big_a * big_b)
        f1, f2, f3 = (big_b + m) * det_inv, m * det_inv, (big_a + m) * det_inv
        final_ref[...] = jnp.concatenate(
            [f1, f2, f3, left_ginv, left_hold, right_ginv, right_hold, zero], axis=0
        )
    else:
        f1, f2, f3, left_ginv, left_hold, right_ginv, right_hold = [
            final_ref[i : i + 1, :] for i in range(7)
        ]
    chain = lambda c, p: chain_ref[c, p : p + 1, :]
    cur, cur_left = zero, zero
    for p in range(nz - 1):
        cur = chain(0, p) * (part(p, 0) + cur) + chain(1, p) * part(p, 1)
        cur_left = jnp.where(mz == p + 1, cur, cur_left)
    cur, cur_right = zero, zero
    for p in range(nz - 1, 0, -1):
        cur = chain(2, p) * (part(p, 1) + cur) + chain(3, p) * part(p, 0)
        cur_right = jnp.where(mz == p - 1, cur, cur_right)
    cur_first = mine(0) + cur_left
    cur_last = mine(1) + cur_right
    sol_first = f1 * cur_first + f2 * cur_last
    sol_last = f2 * cur_first + f3 * cur_last
    below = cur_left * left_ginv + left_hold * sol_first
    above = cur_right * right_ginv + right_hold * sol_last
    sol_ref[0:1, :] = sol_first
    sol_ref[CELLS - 1 : CELLS, :] = sol_last
    value = sol_last
    for k in range(CELLS - 2, 0, -1):
        value = alpha_ref[k : k + 1, :] + loc_ref[0, k : k + 1, :] * sol_first + loc_ref[1, k : k + 1, :] * value
        sol_ref[k : k + 1, :] = value
    lanes16 = iota((CELLS, 128), 1) < LINES
    sol = jnp.where(lanes16, sol_ref[...], 0.0) * THETA

    line, lane = iota((128, 128), 0), iota((128, 128), 1)
    picks = [
        one_where(line == lane // 16),
        one_where(line == 8 + lane // 16),
        one_where((line == (lane // 16) * 8) & (lane < 32)),
        one_where((line == (lane // 16) * 8 + 7) & (lane < 32)),
    ]
    keep = iota((CELLS, 128), 1) % 16 == iota((CELLS, 128), 0)
    x_low, x_high, y_low, y_high = [
        jnp.sum(jnp.where(keep, dot(sol, pick), 0.0), axis=0, keepdims=True) for pick in picks
    ]

    lane8, row8 = iota((8, 128), 1), iota((8, 128), 0)
    of_row = (lane8 // 8 == row8 // 4) & (lane8 < LINES)
    to_high = one_where((lane >= HIGH_AT) & ((lane - HIGH_AT) // 4 == line % 8) & (line < LINES))
    to_low = one_where(
        (lane >= LOW_AT) & (lane < HIGH_AT) & ((lane - LOW_AT) // 4 == line % 8) & (line < LINES)
    )
    lines_part = dot(jnp.where(of_row, below, 0.0), to_high) + dot(jnp.where(of_row, above, 0.0), to_low)
    face = jnp.zeros((8, 128), F32)
    for peer, at in ((jnp.maximum(mz - 1, 0), HIGH_AT), (jnp.minimum(mz + 1, nz - 1), LOW_AT)):
        packed = jnp.where(row8 < 4, zrec_ref[peer * count], zrec_ref[peer * count + 1])
        for k in range(4):
            here = (lane8 // 32 == at // 32) & (row8 % 4 == k)
            face = jnp.where(here, pltpu.roll(packed, (at - 32 * k) % 128, 1), face)
    zhalo = jnp.where(lane8 >= LOW_AT, face + THETA * lines_part, 0.0)
    return x_low, x_high, y_low, y_high, zhalo


def coarse_totals(zrec_ref, count, nz):
    totals = [zrec_ref[2], zrec_ref[3]]
    for p in range(1, nz):
        for h in range(2):
            totals[h] = totals[h] + zrec_ref[p * count + 2 + h]
    return totals


def first_lines_kernel(
    sizes, zrec_ref, loc_ref, alpha_ref, h0, h1, h2, h3, xmsg_ref, own_ref, zhalo_ref, chain_ref, final_ref, sol_ref
):
    nx, ny, nz = sizes
    mx, my = lax.axis_index("gx"), lax.axis_index("gy")
    x_low, x_high, y_low, y_high, zhalo = solve_chain(
        sizes, True, zrec_ref, loc_ref, alpha_ref, chain_ref, final_ref, sol_ref
    )
    zero = jnp.zeros((1, 128), F32)
    own_ref[...] = jnp.concatenate([x_low, x_high] + [zero] * 6, axis=0)
    zhalo_ref[...] = zhalo

    totals = coarse_totals(zrec_ref, 5, nz)
    lane1 = iota((1, 128), 1)

    def block(i, width, at, offset):
        moved = pltpu.roll(totals[i // 4], (at - 24 * (i % 4) - offset) % 128, 1)
        return jnp.where((lane1 >= at) & (lane1 < at + width), moved, 0.0)

    second = iota((2, 128), 0) == 1
    for i in range(nx):
        sums = block(i, 24, PART_AT, 0)
        if i > 0:
            sums = sums + block(i - 1, 8, PART_AT + 24, 8)
        if i < nx - 1:
            sums = sums + block(i + 1, 8, PART_AT + 32, 8)
        both = jnp.where(second, sums, 0.0)
        for j in range(ny):
            xmsg_ref[i * ny + j] = both
    here = mx * ny + my

    @pl.when(mx > 0)
    def _():
        xmsg_ref[here - ny, 0:1, :] = x_low

    @pl.when(mx < nx - 1)
    def _():
        xmsg_ref[here + ny, 0:1, :] = x_high

    @pl.when(my > 0)
    def _():
        xmsg_ref[here - 1, 0:1, :] = y_low

    @pl.when(my < ny - 1)
    def _():
        xmsg_ref[here + 1, 0:1, :] = y_high


def scale(sigma_ref, kappa_ref, x):
    return WEIGHT / (sigma_ref[x] + 2.0 * (kappa_ref[0, x] + kappa_ref[1, x] + kappa_ref[2, x]))


def ends_of(face):
    lane32, row32 = iota((CY, 128), 1), iota((CY, 128), 0)
    diagonal = (lane32 == row32 + HIGH_AT) | (lane32 == row32 + LOW_AT)
    spots = jnp.concatenate([jnp.where(diagonal, face[x : x + 1, :], 0.0) for x in range(CX)], axis=0)
    j, k = iota((128, 128), 0), iota((128, 128), 1)
    to_ends = one_where(((j >= HIGH_AT) & (k == 0)) | ((j >= LOW_AT) & (j < HIGH_AT) & (k == CZ - 1)))
    return dot(spots, to_ends)


def apply_operator(z, xlo, xhi, ylo, yhi, ends, sigma_ref, kappa_ref, w_ref):
    lane32, row32 = iota((CY, 128), 1), iota((CY, 128), 0)
    for x in range(CX):
        here_z = z[x]
        before = z[x - 1] if x > 0 else xlo
        after = z[x + 1] if x < CX - 1 else xhi
        y_less = jnp.where(row32 == 0, ylo[x : x + 1, :], pltpu.roll(here_z, 1, 0))
        y_more = jnp.where(row32 == CY - 1, yhi[x : x + 1, :], pltpu.roll(here_z, CY - 1, 0))
        z_less = jnp.where(lane32 == 0, 0.0, pltpu.roll(here_z, 1, 1))
        z_more = jnp.where(lane32 == CZ - 1, 0.0, pltpu.roll(here_z, CZ - 1, 1))
        twice = 2.0 * here_z
        w_ref[x] = (
            sigma_ref[x] * here_z
            + kappa_ref[0, x] * (twice - before - after)
            + kappa_ref[1, x] * (twice - y_less - y_more)
            + kappa_ref[2, x] * (twice - z_less - z_more - ends[x * 32 : x * 32 + 32])
        )


def wide(row):
    return jnp.where(iota((CY, 128), 1) // 16 == iota((CY, 128), 0) // 4, row, 0.0)


def thin(row):
    return jnp.where(iota((CX, 128), 1) // 16 == iota((CX, 128), 0) // 4, row, 0.0)


def to_cells():
    return one_where(iota((128, 128), 0) % 16 == iota((128, 128), 1) // 8)


def full_direction(sizes, base, xrec_ref, own_ref, zhalo_ref, halos, z_ref):
    nx, ny, nz = sizes
    mx, my, mz = lax.axis_index("gx"), lax.axis_index("gy"), lax.axis_index("gz")
    here = mx * ny + my
    sums = xrec_ref[0, 1:2, :]
    for q in range(1, nx * ny):
        sums = sums + xrec_ref[q, 1:2, :]
    lane1 = iota((1, 128), 1)
    coarse = lambda at: jnp.sum(jnp.where(lane1 == at + my, sums, 0.0))
    c_own = coarse(PART_AT + 8)
    c_zlo, c_zhi = coarse(PART_AT), coarse(PART_AT + 16)
    c_ylo, c_yhi = coarse(PART_AT + 7), coarse(PART_AT + 9)
    c_xlo, c_xhi = coarse(PART_AT + 24), coarse(PART_AT + 32)

    left = xrec_ref[jnp.maximum(here - ny, 0), 0:1, :]
    right = xrec_ref[jnp.minimum(here + ny, nx * ny - 1), 0:1, :]
    front = xrec_ref[jnp.maximum(here - 1, 0), 0:1, :]
    back = xrec_ref[jnp.minimum(here + 1, nx * ny - 1), 0:1, :]
    rows = jnp.concatenate(
        [wide(own_ref[0:1, :]), wide(own_ref[1:2, :]), wide(left), wide(right), thin(front), thin(back)],
        axis=0,
    )
    lines = dot(rows, to_cells())
    xlo, xhi = halos[0][...], halos[1][...]
    ylo, yhi = y_halos(halos[2][...], halos[3][...])
    xlo = jnp.where(mx > 0, xlo + lines[64:96] + c_xlo, 0.0)
    xhi = jnp.where(mx < nx - 1, xhi + lines[96:128] + c_xhi, 0.0)
    ylo = jnp.where(my > 0, ylo + lines[128:136] + c_ylo, 0.0)
    yhi = jnp.where(my < ny - 1, yhi + lines[136:144] + c_yhi, 0.0)
    face = zhalo_ref[...]
    high = jnp.where(mz > 0, face + c_zlo, 0.0)
    low = jnp.where(mz < nz - 1, face + c_zhi, 0.0)
    ends = ends_of(jnp.where(iota((8, 128), 1) >= HIGH_AT, high, low))
    z = [base(x) + lines[(x // 4) * 32 : (x // 4) * 32 + 32] + c_own for x in range(CX)]
    for x in range(CX):
        z_ref[x] = z[x]
    return z, xlo, xhi, ylo, yhi, ends


def first_kernel(
    sizes, r_ref, sigma_ref, kappa_ref, xrec_ref, own_ref, zhalo_ref, h0, h1, h2, h3,
    loc_ref, spread_ref, z_ref, w_ref, jac_ref, zmsg_ref, alpha_ref
):
    scales = [scale(sigma_ref, kappa_ref, x) for x in range(CX)]
    base = lambda x: scales[x] * r_ref[x]
    parts = full_direction(sizes, base, xrec_ref, own_ref, zhalo_ref, (h0, h1, h2, h3), z_ref)
    apply_operator(*parts, sigma_ref, kappa_ref, w_ref)
    field = w_ref[...]
    for x in range(CX):
        jac_ref[x] = scales[x] * w_ref[x]
    rhs = lines_of(field)
    row = lambda a, k: a[k : k + 1, :]
    cur_first, cur = row(rhs, 0), row(rhs, 1)
    zero = jnp.zeros((1, 128), F32)
    for k in (0, CELLS - 1):
        alpha_ref[k : k + 1, :] = zero
    for k in range(1, CELLS - 1):
        alpha_ref[k : k + 1, :] = cur * loc_ref[2, k : k + 1, :]
        cur_first = cur_first + loc_ref[0, k : k + 1, :] * cur
        cur = row(rhs, k + 1) + loc_ref[1, k : k + 1, :] * cur
    write_z_message(
        zmsg_ref, [(cur_first, cur), (None, None)], faces_of(jac_ref[...]), spread_ref[...], jnp.sum(field), sizes
    )


def second_lines_kernel(
    sizes, zrec_ref, loc_ref, alpha_ref, chain_ref, final_ref, jac_ref,
    part_ref, zhalo_ref, z_ref, xlo, xhi, ylo, yhi, sol_ref
):
    x_low, x_high, _, _, zhalo = solve_chain(
        sizes, False, zrec_ref, loc_ref, alpha_ref, chain_ref, final_ref, sol_ref
    )
    zhalo_ref[...] = zhalo
    lines = dot(jnp.concatenate([wide(x_low), wide(x_high)], axis=0), to_cells())
    for x in range(CX):
        z_ref[x] = jac_ref[x] + lines[(x // 4) * 32 : (x // 4) * 32 + 32]
    write_planes(z_ref[...], (xlo, xhi, ylo, yhi))
    zero = jnp.zeros((1, 128), F32)
    part_ref[...] = jnp.concatenate(coarse_totals(zrec_ref, 4, sizes[2]) + [zero] * 6, axis=0)


FACES = range(1, 7)
TERMS = (
    [("g11", -1, -1), ("g12", -1, -1), ("g22", -1, -1), ("h1", -1, -1), ("h2", -1, -1)]
    + [(name, j, -1) for name in ("h2", "g12", "g22") for j in range(7)]
    + [("g22", 0, j) for j in range(7)]
    + [("g22", j, j) for j in FACES]
    + [("g22", j, k) for j in FACES for k in FACES if j < k and (j - 1) // 2 != (k - 1) // 2]
)
NAMES = ("g11", "g12", "g22", "h1", "h2")
TERMS_AT, TERMS_ROW = 96, 32


def second_kernel(
    sizes, r_ref, w1_ref, sigma_ref, kappa_ref, z_ref, zhalo_ref, part_ref, h0, h1, h2, h3,
    w_ref, xmsg_ref, terms_ref
):
    nx, ny, nz = sizes
    mx, my, mz = lax.axis_index("gx"), lax.axis_index("gy"), lax.axis_index("gz")
    xlo = jnp.where(mx > 0, h0[...], 0.0)
    xhi = jnp.where(mx < nx - 1, h1[...], 0.0)
    ylo, yhi = y_halos(h2[...], h3[...])
    ylo = jnp.where(my > 0, ylo, 0.0)
    yhi = jnp.where(my < ny - 1, yhi, 0.0)
    face = zhalo_ref[...]
    high, low = jnp.where(mz > 0, face, 0.0), jnp.where(mz < nz - 1, face, 0.0)
    ends = ends_of(jnp.where(iota((8, 128), 1) >= HIGH_AT, high, low))
    apply_operator([z_ref[x] for x in range(CX)], xlo, xhi, ylo, yhi, ends, sigma_ref, kappa_ref, w_ref)

    r, w1, w2, sigma = r_ref[...], w1_ref[...], w_ref[...], sigma_ref[...]
    kz = kappa_ref[2]
    rows = lambda a: jnp.sum(jnp.sum(a, axis=0), axis=0, keepdims=True)
    lane1 = iota((1, 128), 1)
    pick = lambda profile, face: jnp.where(lane1 == (0 if face == 5 else CZ - 1), profile, 0.0)
    low_row = lambda a: jnp.sum(a, axis=0, keepdims=True)
    partner = {"h2": r, "g12": w1, "g22": w2}
    partner_ref = {"h2": r_ref, "g12": w1_ref, "g22": w_ref}
    z_profiles = {name: rows(kz * f) for name, f in partner.items()}
    z_sigma, z_self = rows(kz * sigma), rows(kz * kz)

    def plane(ref, f):
        if f < 3:
            return ref[0 if f == 1 else CX - 1]
        return ref[:, 0 if f == 3 else CY - 1, :]

    face_weight = {f: plane(kappa_ref.at[(f - 1) // 2], f) for f in range(1, 5)}

    def on_face(f, other):
        return low_row(face_weight[f] * plane(other, f))

    def term(name, j, k):
        if j == -1:
            a, b = {"g11": (w1, w1), "g12": (w1, w2), "g22": (w2, w2), "h1": (w1, r), "h2": (w2, r)}[name]
            return rows(a * b)
        if k == -1:
            twice = 2.0 if name == "g22" else 1.0
            if j == 0:
                return twice * rows(sigma * partner[name])
            if j > 4:
                return twice * pick(z_profiles[name], j)
            return twice * on_face(j, partner_ref[name])
        if j == 0:
            if k == 0:
                return rows(sigma * sigma)
            return 2.0 * (pick(z_sigma, k) if k > 4 else on_face(k, sigma_ref))
        if j == k:
            return pick(z_self, j) if j > 4 else on_face(j, kappa_ref.at[(j - 1) // 2])
        if k > 4:
            return 2.0 * pick(on_face(j, kappa_ref.at[2]), k)
        x, y = 0 if j == 1 else CX - 1, 0 if k == 3 else CY - 1
        return 2.0 * kappa_ref[0, x, y : y + 1, :] * kappa_ref[1, x, y : y + 1, :]

    for i, (name, j, k) in enumerate(TERMS):
        terms_ref[i : i + 1, :] = term(name, j, k)
    for i in range(len(TERMS), 128):
        if i % 8 == 0:
            terms_ref[i : i + 8, :] = jnp.zeros((8, 128), F32)
        elif i == len(TERMS):
            stop = -(-i // 8) * 8
            terms_ref[i:stop, :] = jnp.zeros((stop - i, 128), F32)
    poly = dot_t(jnp.full((8, 128), 1.0, F32), terms_ref[...])[0:1, :]
    halves = [
        jnp.where(lane1 < TERMS_AT, part_ref[h : h + 1, :], pltpu.roll(poly, TERMS_AT - TERMS_ROW * h, 1))
        for h in range(2)
    ]
    both = jnp.concatenate(halves, axis=0)
    for q in range(nx * ny):
        xmsg_ref[q] = both


def plane_kernel(sizes, xrec_ref, sums_ref, own_ref, flat_ref):
    nx, ny, nz = sizes
    mx, my, mz = lax.axis_index("gx"), lax.axis_index("gy"), lax.axis_index("gz")
    count = nx * ny
    total = xrec_ref[0]
    for q in range(count):
        for h in range(2):
            flat_ref[h, q : q + 1, :] = xrec_ref[q, h : h + 1, :]
        if q > 0:
            total = total + xrec_ref[q]
    lane, row = iota((count, 128), 1), iota((count, 128), 0)
    tx, ty = row // ny, row % ny

    def value(qx, qy, dz, valid):
        at = (qx & 3) * 24 + 8 + 8 * dz + qy
        chosen = jnp.where(qx < 4, total[0:1, :], total[1:2, :])
        return jnp.sum(jnp.where((lane == at) & valid, chosen, 0.0), axis=1, keepdims=True)

    always = row >= 0
    c = value(tx, ty, 0, always)
    near = [
        value(tx - 1, ty, 0, tx > 0),
        value(tx + 1, ty, 0, tx < nx - 1),
        value(tx, ty - 1, 0, ty > 0),
        value(tx, ty + 1, 0, ty < ny - 1),
        value(tx, ty, -1, always & (mz > 0)),
        value(tx, ty, 1, always & (mz < nz - 1)),
    ]
    v = [c] + [c - n for n in near]
    lane1 = iota((1, 128), 1)
    out = jnp.zeros((1, 128), F32)
    for h in range(2):
        terms = list(enumerate(TERMS[TERMS_ROW * h : TERMS_ROW * (h + 1)], TERMS_AT))
        first = jnp.where(lane < 0, 1.0, 0.0)
        second = first
        for j in range(-1, 7):
            amount = 1.0 if j == -1 else v[j]
            is_first = lane < 0
            is_second = is_first
            for i, (_, a, b) in terms:
                if a == j:
                    is_first = is_first | (lane == i)
                if b == j:
                    is_second = is_second | (lane == i)
            first = jnp.where(is_first, amount, first)
            second = jnp.where(is_second, amount, second)
        weights = jnp.where(lane >= TERMS_AT, flat_ref[h], 0.0)
        added = jnp.sum(weights * first * second, axis=0, keepdims=True)
        for n, name in enumerate(NAMES):
            mask = lane1 < 0
            for i, (of, _, _) in terms:
                if of == name:
                    mask = mask | (lane1 == i)
            add = jnp.sum(jnp.where(mask, added, 0.0), axis=1, keepdims=True)
            out = jnp.where(lane1 == n, out + add, out)
    sums_ref[...] = out
    mine = row == mx * ny + my
    for j in range(7):
        own = jnp.sum(jnp.where(mine & (lane == 0), v[j], 0.0))
        own_ref[j : j + 1, :] = jnp.full((1, 128), own, F32)
    own_ref[7:8, :] = jnp.zeros((1, 128), F32)


def end_kernel(all_ref, own_ref, r_ref, sigma_ref, kappa_ref, z1_ref, w1_ref, z2_ref, w2_ref, field_ref, res_ref):
    sums = all_ref[0]
    for q in range(1, all_ref.shape[0]):
        sums = sums + all_ref[q]
    lane = iota((1, 128), 1)
    spread = lambda i: jnp.sum(jnp.where(lane == i, sums, 0.0), axis=1, keepdims=True)
    g11, g12, g22, h1, h2 = [spread(i) for i in range(5)]
    inv = 1.0 / (g11 * g22 - g12 * g12)
    y1 = (g22 * h1 - g12 * h2) * inv
    y2 = (g11 * h2 - g12 * h1) * inv
    c, xlo, xhi, ylo, yhi, zlo, zhi = [own_ref[j : j + 1, :] for j in range(7)]
    lane32, row32 = iota((CY, 128), 1), iota((CY, 128), 0)
    on_y = jnp.where(row32 == 0, ylo, jnp.where(row32 == CY - 1, yhi, 0.0))
    on_z = jnp.where(lane32 == 0, zlo, jnp.where(lane32 == CZ - 1, zhi, 0.0))
    for x in range(CX):
        w2 = w2_ref[x] + sigma_ref[x] * c + kappa_ref[1, x] * on_y + kappa_ref[2, x] * on_z
        if x == 0:
            w2 = w2 + kappa_ref[0, x] * xlo
        if x == CX - 1:
            w2 = w2 + kappa_ref[0, x] * xhi
        field_ref[x] = y1 * z1_ref[x] + y2 * (z2_ref[x] + c)
        res_ref[x] = r_ref[x] - y1 * w1_ref[x] - y2 * w2


def call(kernel, out_shapes, scratch=(), name=None, inputs=pltpu.VMEM, semaphores=(), limit=24 << 20):
    vmem = pl.BlockSpec(memory_space=pltpu.VMEM)

    def run(*args):
        return pl.pallas_call(
            kernel,
            out_shape=[jax.ShapeDtypeStruct(s, F32) for s in out_shapes],
            in_specs=[pl.BlockSpec(memory_space=inputs)] * len(args),
            out_specs=[vmem] * len(out_shapes),
            scratch_shapes=[pltpu.VMEM(s, F32) for s in scratch] + list(semaphores),
            compiler_params=pltpu.CompilerParams(vmem_limit_bytes=limit),
            name=name,
        )(*args)

    return run


def shards(sizes, r, sigma, kappa, inverse_rows):
    nx, ny, nz = sizes
    field, plane, tile, coarse = (CX, CY, CZ), (CY, CZ), (8, 128), (CELLS, 128)
    planes = [plane, plane, tile, tile]
    to_xy = (nx * ny, 2, 128)

    fold = []
    for x in range(0, nx, 2):
        ring = [x * ny + y for y in range(ny)] + [(x + 1) * ny + y for y in reversed(range(ny))]
        fold += list(zip(ring, ring[1:] + ring[:1]))
    unfold = [(b, a) for a, b in fold]

    def halo(parts):
        xlo, xhi, y_one, y_two = parts
        return (
            lax.ppermute(xhi, "gx", [(i, (i + 1) % nx) for i in range(nx)]),
            lax.ppermute(xlo, "gx", [((i + 1) % nx, i) for i in range(nx)]),
            lax.ppermute(y_one, ("gx", "gy"), fold),
            lax.ppermute(y_two, ("gx", "gy"), unfold),
        )

    def along_z(message):
        return lax.all_to_all(message, "gz", split_axis=0, concat_axis=0, tiled=True)

    def along_xy(message):
        return lax.all_to_all(message, ("gx", "gy"), split_axis=0, concat_axis=0, tiled=True)

    bind = lambda kernel, *a: functools.partial(kernel, sizes, *a)
    zmsg, loc, alpha, spread, *sides = call(
        bind(begin_kernel), [(nz * 5, 1, 128), (3, *coarse), coarse, tile, *planes],
        [field, field, (3, *field), tile], "begin", pltpu.HBM, [pltpu.SemaphoreType.DMA((4,))], 55100 << 10,
    )(r, sigma, kappa, inverse_rows)
    zrec = along_z(zmsg)
    halos = halo(sides)
    xmsg, own, zhalo, chain, final = call(
        bind(first_lines_kernel), [to_xy, tile, tile, (4, nz, 128), tile], [coarse], "lines_first"
    )(zrec, loc, alpha, *halos)
    xrec = along_xy(xmsg)
    z1, w1, jac, zmsg, alpha = call(
        bind(first_kernel), [field, field, field, (nz * 4, 1, 128), coarse], name="operator_first"
    )(r, sigma, kappa, xrec, own, zhalo, *halos, loc, spread)
    zrec = along_z(zmsg)
    part, zhalo, z2, *sides = call(
        bind(second_lines_kernel), [tile, tile, field, *planes], [coarse], "lines_second"
    )(zrec, loc, alpha, chain, final, jac)
    halos = halo(sides)
    w2, xmsg = call(bind(second_kernel), [field, to_xy], [(128, 128)], "operator_second")(
        r, w1, sigma, kappa, z2, zhalo, part, *halos
    )
    xrec = along_xy(xmsg)
    sums, values = call(bind(plane_kernel), [(1, 128), tile], [(2, nx * ny, 128)], "plane")(xrec)
    sums = along_z(jnp.broadcast_to(sums[None], (nz, 1, 128)))
    return tuple(
        call(end_kernel, [field, field], name="end")(sums, values, r, sigma, kappa, z1, w1, z2, w2)
    )


def solution(mesh):
    sizes = (mesh.shape["gx"], mesh.shape["gy"], mesh.shape["gz"])
    spec = P("gx", "gy", "gz")

    def run(r, sigma, kappa, inverse):
        return shards(sizes, r, sigma, kappa, inverse.reshape(8, 128))

    return jax.shard_map(
        run,
        mesh=mesh,
        in_specs=(spec, spec, P(None, "gx", "gy", "gz"), P(("gx", "gy", "gz"), None)),
        out_specs=(spec, spec),
        check_vma=False,
    )
```

```python
import functools

import jax
import jax.numpy as jnp
from jax import lax
from jax.experimental import pallas as pl
from jax.experimental.pallas import tpu as pltpu
from jax.sharding import PartitionSpec as P

CX, CY, CZ = 8, 32, 128
CELLS = 16
LINES = 16
THETA = 1.0 / 128.0
WEIGHT = 0.6
PART_AT, LOW_AT, HIGH_AT = 32, 64, 96
HIGHEST = lax.Precision.HIGHEST
F32 = jnp.float32


def iota(shape, dim):
    return lax.broadcasted_iota(jnp.int32, shape, dim)


def dot(a, b):
    return lax.dot_general(
        a, b, (((1,), (0,)), ((), ())), precision=HIGHEST, preferred_element_type=F32
    )


def dot_t(a, b):
    return lax.dot_general(
        a, b, (((1,), (1,)), ((), ())), precision=HIGHEST, preferred_element_type=F32
    )


def one_where(cond):
    return jnp.where(cond, 1.0, 0.0).astype(F32)


def lines_of(field):
    low = (field[0] + field[1]) + (field[2] + field[3])
    high = (field[4] + field[5]) + (field[6] + field[7])
    stacked = jnp.concatenate([low, high], axis=0)
    by_line = one_where(iota((128, 64), 1) // 4 == iota((128, 64), 0))
    by_cell = one_where(iota((CELLS, 128), 1) // 8 == iota((CELLS, 128), 0))
    return dot_t(by_cell, dot(by_line, stacked))


def faces_of(field):
    shape = (CX, CY, 128)
    here = iota(shape, 2) == (iota(shape, 0) % 4) * 32 + iota(shape, 1)

    def packed(z):
        rows = jnp.sum(jnp.where(here, field[:, :, z : z + 1], 0.0), axis=1)
        halves = [jnp.sum(rows[i : i + 4], axis=0, keepdims=True) for i in (0, 4)]
        return jnp.concatenate(halves, axis=0)

    return packed(0), packed(CZ - 1)


def write_z_message(zmsg_ref, pairs, faces, spread_inverse, total, sizes):
    nz, count = sizes[2], 2 + len(pairs)
    mz = lax.axis_index("gz")
    lane1, lane8, row8 = iota((1, 128), 1), iota((8, 128), 1), iota((8, 128), 0)
    only = lambda v: jnp.where(lane1 < LINES, v, 0.0)
    tails = [pltpu.roll(only(a), 96, 1) + pltpu.roll(only(b), 112, 1) if a is not None else None for a, b in pairs]
    mine = spread_inverse * total
    inside = lane8 // 24 == row8 % 4
    zero = jnp.zeros((1, 128), F32)
    for p in range(nz):
        moved = jnp.where(inside, pltpu.roll(mine, (8 - 8 * p) % 128, 1), 0.0)
        zmsg_ref[p * count] = zero
        zmsg_ref[p * count + 1] = zero
        for h, tail in enumerate(tails):
            row = jnp.sum(moved[4 * h : 4 * h + 4], axis=0, keepdims=True) if h < 2 else zero
            zmsg_ref[p * count + 2 + h] = row if tail is None else row + tail

    @pl.when(mz > 0)
    def _():
        zmsg_ref[(mz - 1) * count] = faces[0][0:1]
        zmsg_ref[(mz - 1) * count + 1] = faces[0][1:2]

    @pl.when(mz < nz - 1)
    def _():
        zmsg_ref[(mz + 1) * count] = faces[1][0:1]
        zmsg_ref[(mz + 1) * count + 1] = faces[1][1:2]


def write_planes(field, planes):
    xlo, xhi, y_one, y_two = planes
    xlo[...] = field[0]
    xhi[...] = field[CX - 1]
    core = lax.axis_index("gx") % 2
    low, high = field[:, 0, :], field[:, CY - 1, :]
    y_one[...] = jnp.where(core == 0, high, low)
    y_two[...] = jnp.where(core == 0, low, high)


def y_halos(y_one, y_two):
    core = lax.axis_index("gx") % 2
    return jnp.where(core == 0, y_one, y_two), jnp.where(core == 0, y_two, y_one)


def begin_kernel(
    sizes, r_hbm, sigma_hbm, kappa_hbm, inv_hbm,
    zmsg_ref, loc_ref, alpha_ref, spread_ref, xlo, xhi, ylo, yhi,
    r_ref, sigma_ref, kappa_ref, inv_ref, sems
):
    pairs = ((kappa_hbm, kappa_ref), (sigma_hbm, sigma_ref), (r_hbm, r_ref), (inv_hbm, inv_ref))
    copies = [pltpu.make_async_copy(a, b, sems.at[i]) for i, (a, b) in enumerate(pairs)]
    for copy in copies:
        copy.start()
    for copy in copies:
        copy.wait()
    r, sigma = r_ref[...], sigma_ref[...]
    kx, ky, kz = kappa_ref[0], kappa_ref[1], kappa_ref[2]
    jac = r * (WEIGHT / (sigma + 2.0 * (kx + ky + kz)))
    write_planes(jac, (xlo, xhi, ylo, yhi))
    unused = iota((CELLS, 128), 1) >= LINES
    e = jnp.where(unused, 1.0, lines_of(sigma))
    g = jnp.where(unused, 1.0, lines_of(kz) * 0.125)
    rhs = lines_of(r)
    row = lambda a, k: a[k : k + 1, :]
    first, mid, last = row(e, 0), row(g, 0), row(e, 1)
    cur_first, cur = row(rhs, 0), row(rhs, 1)
    zero = jnp.zeros((1, 128), F32)
    for c in range(3):
        for k in (0, CELLS - 1):
            loc_ref[c, k : k + 1, :] = zero
    for k in (0, CELLS - 1):
        alpha_ref[k : k + 1, :] = zero
    for k in range(1, CELLS - 1):
        inv = 1.0 / (mid + last + row(g, k))
        mu, gam = mid * inv, row(g, k) * inv
        loc_ref[0, k : k + 1, :] = mu
        loc_ref[1, k : k + 1, :] = gam
        loc_ref[2, k : k + 1, :] = inv
        alpha_ref[k : k + 1, :] = cur * inv
        first = first + mu * last
        mid = mu * row(g, k)
        last = row(e, k + 1) + gam * last
        cur_first = cur_first + mu * cur
        cur = row(rhs, k + 1) + gam * cur
    move = one_where((iota((128, 128), 0) % 16) * 8 + iota((128, 128), 0) // 16 == iota((128, 128), 1))
    plain = dot(inv_ref[...], move)
    step = iota((8, 128), 0) % 4
    spread_inverse = plain
    for k in range(1, 4):
        spread_inverse = jnp.where(step == k, pltpu.roll(plain, 24 * k, 1), spread_inverse)
    spread_ref[...] = spread_inverse
    pairs = [(cur_first, cur), (first, mid), (last, row(g, CELLS - 1))]
    write_z_message(zmsg_ref, pairs, faces_of(jac), spread_inverse, jnp.sum(r), sizes)


def solve_chain(sizes, fresh, zrec_ref, loc_ref, alpha_ref, chain_ref, final_ref, sol_ref):
    nz = sizes[2]
    mz = lax.axis_index("gz")
    count = 5 if fresh else 4
    zero = jnp.zeros((1, 128), F32)
    columns = []
    for h in range(count - 2 if fresh else 1):
        rows = jnp.concatenate([zrec_ref[p * count + 2 + h] for p in range(nz)], axis=0)
        used = iota(rows.shape, 1) < LINES
        for shift in (32, 16):
            columns.append(jnp.where(used, pltpu.roll(rows, shift, 1), 1.0))
    part = lambda p, i: columns[i][p : p + 1, :]

    def mine(i):
        row = pltpu.roll(zrec_ref[mz * count + 2 + i // 2], 32 - 16 * (i % 2), 1)
        return jnp.where(iota((1, 128), 1) < LINES, row, 1.0)

    if fresh:
        one = zero + 1.0
        cond, cond_own, hold, ginv = zero, zero, one, one
        for p in range(nz - 1):
            a, m, b, g = part(p, 2), part(p, 3), part(p, 4), part(p, 5)
            at_first = a + cond
            s = m + at_first
            n = b * s + m * at_first
            inv = 1.0 / (n + g * s)
            chain_ref[0, p : p + 1, :] = g * m * inv
            c2 = g * s * inv
            chain_ref[1, p : p + 1, :] = c2
            cond = g * n * inv
            here = mz == p + 1
            cond_own = jnp.where(here, cond, cond_own)
            hold = jnp.where(here, c2, hold)
            ginv = jnp.where(here, g, ginv)
        left_cond, left_hold, left_ginv = cond_own, hold, 1.0 / ginv
        cond = part(nz - 1, 5)
        cond_own, hold, ginv = cond, one, one
        for p in range(nz - 1, 0, -1):
            a, m, b, g = part(p, 2), part(p, 3), part(p, 4), part(p - 1, 5)
            at_last = b + cond
            s = m + at_last
            n = a * s + m * at_last
            inv = 1.0 / (n + g * s)
            chain_ref[2, p : p + 1, :] = g * m * inv
            c2 = g * s * inv
            chain_ref[3, p : p + 1, :] = c2
            cond = g * n * inv
            here = mz == p - 1
            cond_own = jnp.where(here, cond, cond_own)
            hold = jnp.where(here, c2, hold)
            ginv = jnp.where(here, g, ginv)
        right_cond, right_hold, right_ginv = cond_own, hold, 1.0 / ginv
        for c, p in ((0, nz - 1), (1, nz - 1), (2, 0), (3, 0)):
            chain_ref[c, p : p + 1, :] = zero
        big_a = mine(2) + left_cond
        big_b = mine(4) + right_cond
        m = mine(3)
        det_inv = 1.0 / (big_a * m + big_b * m + big_a * big_b)
        f1, f2, f3 = (big_b + m) * det_inv, m * det_inv, (big_a + m) * det_inv
        final_ref[...] = jnp.concatenate(
            [f1, f2, f3, left_ginv, left_hold, right_ginv, right_hold, zero], axis=0
        )
    else:
        f1, f2, f3, left_ginv, left_hold, right_ginv, right_hold = [
            final_ref[i : i + 1, :] for i in range(7)
        ]
    chain = lambda c, p: chain_ref[c, p : p + 1, :]
    cur, cur_left = zero, zero
    for p in range(nz - 1):
        cur = chain(0, p) * (part(p, 0) + cur) + chain(1, p) * part(p, 1)
        cur_left = jnp.where(mz == p + 1, cur, cur_left)
    cur, cur_right = zero, zero
    for p in range(nz - 1, 0, -1):
        cur = chain(2, p) * (part(p, 1) + cur) + chain(3, p) * part(p, 0)
        cur_right = jnp.where(mz == p - 1, cur, cur_right)
    cur_first = mine(0) + cur_left
    cur_last = mine(1) + cur_right
    sol_first = f1 * cur_first + f2 * cur_last
    sol_last = f2 * cur_first + f3 * cur_last
    below = cur_left * left_ginv + left_hold * sol_first
    above = cur_right * right_ginv + right_hold * sol_last
    sol_ref[0:1, :] = sol_first
    sol_ref[CELLS - 1 : CELLS, :] = sol_last
    value = sol_last
    for k in range(CELLS - 2, 0, -1):
        value = alpha_ref[k : k + 1, :] + loc_ref[0, k : k + 1, :] * sol_first + loc_ref[1, k : k + 1, :] * value
        sol_ref[k : k + 1, :] = value
    lanes16 = iota((CELLS, 128), 1) < LINES
    sol = jnp.where(lanes16, sol_ref[...], 0.0) * THETA

    line, lane = iota((128, 128), 0), iota((128, 128), 1)
    picks = [
        one_where(line == lane // 16),
        one_where(line == 8 + lane // 16),
        one_where((line == (lane // 16) * 8) & (lane < 32)),
        one_where((line == (lane // 16) * 8 + 7) & (lane < 32)),
    ]
    keep = iota((CELLS, 128), 1) % 16 == iota((CELLS, 128), 0)
    x_low, x_high, y_low, y_high = [
        jnp.sum(jnp.where(keep, dot(sol, pick), 0.0), axis=0, keepdims=True) for pick in picks
    ]

    lane8, row8 = iota((8, 128), 1), iota((8, 128), 0)
    of_row = (lane8 // 8 == row8 // 4) & (lane8 < LINES)
    to_high = one_where((lane >= HIGH_AT) & ((lane - HIGH_AT) // 4 == line % 8) & (line < LINES))
    to_low = one_where(
        (lane >= LOW_AT) & (lane < HIGH_AT) & ((lane - LOW_AT) // 4 == line % 8) & (line < LINES)
    )
    lines_part = dot(jnp.where(of_row, below, 0.0), to_high) + dot(jnp.where(of_row, above, 0.0), to_low)
    face = jnp.zeros((8, 128), F32)
    for peer, at in ((jnp.maximum(mz - 1, 0), HIGH_AT), (jnp.minimum(mz + 1, nz - 1), LOW_AT)):
        packed = jnp.where(row8 < 4, zrec_ref[peer * count], zrec_ref[peer * count + 1])
        for k in range(4):
            here = (lane8 // 32 == at // 32) & (row8 % 4 == k)
            face = jnp.where(here, pltpu.roll(packed, (at - 32 * k) % 128, 1), face)
    zhalo = jnp.where(lane8 >= LOW_AT, face + THETA * lines_part, 0.0)
    return x_low, x_high, y_low, y_high, zhalo


def coarse_totals(zrec_ref, count, nz):
    totals = [zrec_ref[2], zrec_ref[3]]
    for p in range(1, nz):
        for h in range(2):
            totals[h] = totals[h] + zrec_ref[p * count + 2 + h]
    return totals


def first_lines_kernel(
    sizes, zrec_ref, loc_ref, alpha_ref, xmsg_ref, own_ref, zhalo_ref, chain_ref, final_ref, sol_ref
):
    nx, ny, nz = sizes
    mx, my = lax.axis_index("gx"), lax.axis_index("gy")
    x_low, x_high, y_low, y_high, zhalo = solve_chain(
        sizes, True, zrec_ref, loc_ref, alpha_ref, chain_ref, final_ref, sol_ref
    )
    zero = jnp.zeros((1, 128), F32)
    own_ref[...] = jnp.concatenate([x_low, x_high] + [zero] * 6, axis=0)
    zhalo_ref[...] = zhalo

    totals = coarse_totals(zrec_ref, 5, nz)
    lane1 = iota((1, 128), 1)

    def block(i, width, at, offset):
        moved = pltpu.roll(totals[i // 4], (at - 24 * (i % 4) - offset) % 128, 1)
        return jnp.where((lane1 >= at) & (lane1 < at + width), moved, 0.0)

    second = iota((2, 128), 0) == 1
    for i in range(nx):
        sums = block(i, 24, PART_AT, 0)
        if i > 0:
            sums = sums + block(i - 1, 8, PART_AT + 24, 8)
        if i < nx - 1:
            sums = sums + block(i + 1, 8, PART_AT + 32, 8)
        both = jnp.where(second, sums, 0.0)
        for j in range(ny):
            xmsg_ref[i * ny + j] = both
    here = mx * ny + my

    @pl.when(mx > 0)
    def _():
        xmsg_ref[here - ny, 0:1, :] = x_low

    @pl.when(mx < nx - 1)
    def _():
        xmsg_ref[here + ny, 0:1, :] = x_high

    @pl.when(my > 0)
    def _():
        xmsg_ref[here - 1, 0:1, :] = y_low

    @pl.when(my < ny - 1)
    def _():
        xmsg_ref[here + 1, 0:1, :] = y_high


def scale(sigma_ref, kappa_ref, x):
    return WEIGHT / (sigma_ref[x] + 2.0 * (kappa_ref[0, x] + kappa_ref[1, x] + kappa_ref[2, x]))


def ends_of(face):
    lane32, row32 = iota((CY, 128), 1), iota((CY, 128), 0)
    diagonal = (lane32 == row32 + HIGH_AT) | (lane32 == row32 + LOW_AT)
    spots = jnp.concatenate([jnp.where(diagonal, face[x : x + 1, :], 0.0) for x in range(CX)], axis=0)
    j, k = iota((128, 128), 0), iota((128, 128), 1)
    to_ends = one_where(((j >= HIGH_AT) & (k == 0)) | ((j >= LOW_AT) & (j < HIGH_AT) & (k == CZ - 1)))
    return dot(spots, to_ends)


def apply_operator(z, xlo, xhi, ylo, yhi, ends, sigma_ref, kappa_ref, w_ref):
    lane32, row32 = iota((CY, 128), 1), iota((CY, 128), 0)
    for x in range(CX):
        here_z = z[x]
        before = z[x - 1] if x > 0 else xlo
        after = z[x + 1] if x < CX - 1 else xhi
        y_less = jnp.where(row32 == 0, ylo[x : x + 1, :], pltpu.roll(here_z, 1, 0))
        y_more = jnp.where(row32 == CY - 1, yhi[x : x + 1, :], pltpu.roll(here_z, CY - 1, 0))
        z_less = jnp.where(lane32 == 0, 0.0, pltpu.roll(here_z, 1, 1))
        z_more = jnp.where(lane32 == CZ - 1, 0.0, pltpu.roll(here_z, CZ - 1, 1))
        twice = 2.0 * here_z
        w_ref[x] = (
            sigma_ref[x] * here_z
            + kappa_ref[0, x] * (twice - before - after)
            + kappa_ref[1, x] * (twice - y_less - y_more)
            + kappa_ref[2, x] * (twice - z_less - z_more - ends[x * 32 : x * 32 + 32])
        )


def wide(row):
    return jnp.where(iota((CY, 128), 1) // 16 == iota((CY, 128), 0) // 4, row, 0.0)


def thin(row):
    return jnp.where(iota((CX, 128), 1) // 16 == iota((CX, 128), 0) // 4, row, 0.0)


def to_cells():
    return one_where(iota((128, 128), 0) % 16 == iota((128, 128), 1) // 8)


def full_direction(sizes, base, xrec_ref, own_ref, zhalo_ref, halos, z_ref):
    nx, ny, nz = sizes
    mx, my, mz = lax.axis_index("gx"), lax.axis_index("gy"), lax.axis_index("gz")
    here = mx * ny + my
    sums = xrec_ref[0, 1:2, :]
    for q in range(1, nx * ny):
        sums = sums + xrec_ref[q, 1:2, :]
    lane1 = iota((1, 128), 1)
    coarse = lambda at: jnp.sum(jnp.where(lane1 == at + my, sums, 0.0))
    c_own = coarse(PART_AT + 8)
    c_zlo, c_zhi = coarse(PART_AT), coarse(PART_AT + 16)
    c_ylo, c_yhi = coarse(PART_AT + 7), coarse(PART_AT + 9)
    c_xlo, c_xhi = coarse(PART_AT + 24), coarse(PART_AT + 32)

    left = xrec_ref[jnp.maximum(here - ny, 0), 0:1, :]
    right = xrec_ref[jnp.minimum(here + ny, nx * ny - 1), 0:1, :]
    front = xrec_ref[jnp.maximum(here - 1, 0), 0:1, :]
    back = xrec_ref[jnp.minimum(here + 1, nx * ny - 1), 0:1, :]
    rows = jnp.concatenate(
        [wide(own_ref[0:1, :]), wide(own_ref[1:2, :]), wide(left), wide(right), thin(front), thin(back)],
        axis=0,
    )
    lines = dot(rows, to_cells())
    xlo, xhi = halos[0][...], halos[1][...]
    ylo, yhi = y_halos(halos[2][...], halos[3][...])
    xlo = jnp.where(mx > 0, xlo + lines[64:96] + c_xlo, 0.0)
    xhi = jnp.where(mx < nx - 1, xhi + lines[96:128] + c_xhi, 0.0)
    ylo = jnp.where(my > 0, ylo + lines[128:136] + c_ylo, 0.0)
    yhi = jnp.where(my < ny - 1, yhi + lines[136:144] + c_yhi, 0.0)
    face = zhalo_ref[...]
    high = jnp.where(mz > 0, face + c_zlo, 0.0)
    low = jnp.where(mz < nz - 1, face + c_zhi, 0.0)
    ends = ends_of(jnp.where(iota((8, 128), 1) >= HIGH_AT, high, low))
    z = [base(x) + lines[(x // 4) * 32 : (x // 4) * 32 + 32] + c_own for x in range(CX)]
    for x in range(CX):
        z_ref[x] = z[x]
    return z, xlo, xhi, ylo, yhi, ends


def first_kernel(
    sizes, r_ref, sigma_ref, kappa_ref, xrec_ref, own_ref, zhalo_ref, h0, h1, h2, h3,
    loc_ref, spread_ref, z_ref, w_ref, jac_ref, zmsg_ref, alpha_ref
):
    scales = [scale(sigma_ref, kappa_ref, x) for x in range(CX)]
    base = lambda x: scales[x] * r_ref[x]
    parts = full_direction(sizes, base, xrec_ref, own_ref, zhalo_ref, (h0, h1, h2, h3), z_ref)
    apply_operator(*parts, sigma_ref, kappa_ref, w_ref)
    field = w_ref[...]
    for x in range(CX):
        jac_ref[x] = scales[x] * w_ref[x]
    rhs = lines_of(field)
    row = lambda a, k: a[k : k + 1, :]
    cur_first, cur = row(rhs, 0), row(rhs, 1)
    zero = jnp.zeros((1, 128), F32)
    for k in (0, CELLS - 1):
        alpha_ref[k : k + 1, :] = zero
    for k in range(1, CELLS - 1):
        alpha_ref[k : k + 1, :] = cur * loc_ref[2, k : k + 1, :]
        cur_first = cur_first + loc_ref[0, k : k + 1, :] * cur
        cur = row(rhs, k + 1) + loc_ref[1, k : k + 1, :] * cur
    write_z_message(
        zmsg_ref, [(cur_first, cur), (None, None)], faces_of(jac_ref[...]), spread_ref[...], jnp.sum(field), sizes
    )


def second_lines_kernel(
    sizes, zrec_ref, loc_ref, alpha_ref, chain_ref, final_ref, jac_ref,
    part_ref, zhalo_ref, z_ref, xlo, xhi, ylo, yhi, sol_ref
):
    x_low, x_high, _, _, zhalo = solve_chain(
        sizes, False, zrec_ref, loc_ref, alpha_ref, chain_ref, final_ref, sol_ref
    )
    zhalo_ref[...] = zhalo
    lines = dot(jnp.concatenate([wide(x_low), wide(x_high)], axis=0), to_cells())
    for x in range(CX):
        z_ref[x] = jac_ref[x] + lines[(x // 4) * 32 : (x // 4) * 32 + 32]
    write_planes(z_ref[...], (xlo, xhi, ylo, yhi))
    zero = jnp.zeros((1, 128), F32)
    part_ref[...] = jnp.concatenate(coarse_totals(zrec_ref, 4, sizes[2]) + [zero] * 6, axis=0)


FACES = range(1, 7)
TERMS = (
    [("g11", -1, -1), ("g12", -1, -1), ("g22", -1, -1), ("h1", -1, -1), ("h2", -1, -1)]
    + [(name, j, -1) for name in ("h2", "g12", "g22") for j in range(7)]
    + [("g22", 0, j) for j in range(7)]
    + [("g22", j, j) for j in FACES]
    + [("g22", j, k) for j in FACES for k in FACES if j < k and (j - 1) // 2 != (k - 1) // 2]
)
NAMES = ("g11", "g12", "g22", "h1", "h2")
TERMS_AT, TERMS_ROW = 96, 32


def second_kernel(
    sizes, r_ref, w1_ref, sigma_ref, kappa_ref, z_ref, zhalo_ref, part_ref, h0, h1, h2, h3,
    w_ref, xmsg_ref, terms_ref
):
    nx, ny, nz = sizes
    mx, my, mz = lax.axis_index("gx"), lax.axis_index("gy"), lax.axis_index("gz")
    xlo = jnp.where(mx > 0, h0[...], 0.0)
    xhi = jnp.where(mx < nx - 1, h1[...], 0.0)
    ylo, yhi = y_halos(h2[...], h3[...])
    ylo = jnp.where(my > 0, ylo, 0.0)
    yhi = jnp.where(my < ny - 1, yhi, 0.0)
    face = zhalo_ref[...]
    high, low = jnp.where(mz > 0, face, 0.0), jnp.where(mz < nz - 1, face, 0.0)
    ends = ends_of(jnp.where(iota((8, 128), 1) >= HIGH_AT, high, low))
    apply_operator([z_ref[x] for x in range(CX)], xlo, xhi, ylo, yhi, ends, sigma_ref, kappa_ref, w_ref)

    r, w1, w2, sigma = r_ref[...], w1_ref[...], w_ref[...], sigma_ref[...]
    kz = kappa_ref[2]
    rows = lambda a: jnp.sum(jnp.sum(a, axis=0), axis=0, keepdims=True)
    lane1 = iota((1, 128), 1)
    pick = lambda profile, face: jnp.where(lane1 == (0 if face == 5 else CZ - 1), profile, 0.0)
    low_row = lambda a: jnp.sum(a, axis=0, keepdims=True)
    partner = {"h2": r, "g12": w1, "g22": w2}
    partner_ref = {"h2": r_ref, "g12": w1_ref, "g22": w_ref}
    z_profiles = {name: rows(kz * f) for name, f in partner.items()}
    z_sigma, z_self = rows(kz * sigma), rows(kz * kz)

    def plane(ref, f):
        if f < 3:
            return ref[0 if f == 1 else CX - 1]
        return ref[:, 0 if f == 3 else CY - 1, :]

    face_weight = {f: plane(kappa_ref.at[(f - 1) // 2], f) for f in range(1, 5)}

    def on_face(f, other):
        return low_row(face_weight[f] * plane(other, f))

    def term(name, j, k):
        if j == -1:
            a, b = {"g11": (w1, w1), "g12": (w1, w2), "g22": (w2, w2), "h1": (w1, r), "h2": (w2, r)}[name]
            return rows(a * b)
        if k == -1:
            twice = 2.0 if name == "g22" else 1.0
            if j == 0:
                return twice * rows(sigma * partner[name])
            if j > 4:
                return twice * pick(z_profiles[name], j)
            return twice * on_face(j, partner_ref[name])
        if j == 0:
            if k == 0:
                return rows(sigma * sigma)
            return 2.0 * (pick(z_sigma, k) if k > 4 else on_face(k, sigma_ref))
        if j == k:
            return pick(z_self, j) if j > 4 else on_face(j, kappa_ref.at[(j - 1) // 2])
        if k > 4:
            return 2.0 * pick(on_face(j, kappa_ref.at[2]), k)
        x, y = 0 if j == 1 else CX - 1, 0 if k == 3 else CY - 1
        return 2.0 * kappa_ref[0, x, y : y + 1, :] * kappa_ref[1, x, y : y + 1, :]

    for i, (name, j, k) in enumerate(TERMS):
        terms_ref[i : i + 1, :] = term(name, j, k)
    for i in range(len(TERMS), 128):
        if i % 8 == 0:
            terms_ref[i : i + 8, :] = jnp.zeros((8, 128), F32)
        elif i == len(TERMS):
            stop = -(-i // 8) * 8
            terms_ref[i:stop, :] = jnp.zeros((stop - i, 128), F32)
    poly = dot_t(jnp.full((8, 128), 1.0, F32), terms_ref[...])[0:1, :]
    halves = [
        jnp.where(lane1 < TERMS_AT, part_ref[h : h + 1, :], pltpu.roll(poly, TERMS_AT - TERMS_ROW * h, 1))
        for h in range(2)
    ]
    both = jnp.concatenate(halves, axis=0)
    for q in range(nx * ny):
        xmsg_ref[q] = both


def plane_kernel(sizes, xrec_ref, sums_ref, own_ref, flat_ref):
    nx, ny, nz = sizes
    mx, my, mz = lax.axis_index("gx"), lax.axis_index("gy"), lax.axis_index("gz")
    count = nx * ny
    total = xrec_ref[0]
    for q in range(count):
        for h in range(2):
            flat_ref[h, q : q + 1, :] = xrec_ref[q, h : h + 1, :]
        if q > 0:
            total = total + xrec_ref[q]
    lane, row = iota((count, 128), 1), iota((count, 128), 0)
    tx, ty = row // ny, row % ny

    def value(qx, qy, dz, valid):
        at = (qx & 3) * 24 + 8 + 8 * dz + qy
        chosen = jnp.where(qx < 4, total[0:1, :], total[1:2, :])
        return jnp.sum(jnp.where((lane == at) & valid, chosen, 0.0), axis=1, keepdims=True)

    always = row >= 0
    c = value(tx, ty, 0, always)
    near = [
        value(tx - 1, ty, 0, tx > 0),
        value(tx + 1, ty, 0, tx < nx - 1),
        value(tx, ty - 1, 0, ty > 0),
        value(tx, ty + 1, 0, ty < ny - 1),
        value(tx, ty, -1, always & (mz > 0)),
        value(tx, ty, 1, always & (mz < nz - 1)),
    ]
    v = [c] + [c - n for n in near]
    lane1 = iota((1, 128), 1)
    out = jnp.zeros((1, 128), F32)
    for h in range(2):
        terms = list(enumerate(TERMS[TERMS_ROW * h : TERMS_ROW * (h + 1)], TERMS_AT))
        first = jnp.where(lane < 0, 1.0, 0.0)
        second = first
        for j in range(-1, 7):
            amount = 1.0 if j == -1 else v[j]
            is_first = lane < 0
            is_second = is_first
            for i, (_, a, b) in terms:
                if a == j:
                    is_first = is_first | (lane == i)
                if b == j:
                    is_second = is_second | (lane == i)
            first = jnp.where(is_first, amount, first)
            second = jnp.where(is_second, amount, second)
        weights = jnp.where(lane >= TERMS_AT, flat_ref[h], 0.0)
        added = jnp.sum(weights * first * second, axis=0, keepdims=True)
        for n, name in enumerate(NAMES):
            mask = lane1 < 0
            for i, (of, _, _) in terms:
                if of == name:
                    mask = mask | (lane1 == i)
            add = jnp.sum(jnp.where(mask, added, 0.0), axis=1, keepdims=True)
            out = jnp.where(lane1 == n, out + add, out)
    sums_ref[...] = out
    mine = row == mx * ny + my
    for j in range(7):
        own = jnp.sum(jnp.where(mine & (lane == 0), v[j], 0.0))
        own_ref[j : j + 1, :] = jnp.full((1, 128), own, F32)
    own_ref[7:8, :] = jnp.zeros((1, 128), F32)


def end_kernel(all_ref, own_ref, r_ref, sigma_ref, kappa_ref, z1_ref, w1_ref, z2_ref, w2_ref, field_ref, res_ref):
    sums = all_ref[0]
    for q in range(1, all_ref.shape[0]):
        sums = sums + all_ref[q]
    lane = iota((1, 128), 1)
    spread = lambda i: jnp.sum(jnp.where(lane == i, sums, 0.0), axis=1, keepdims=True)
    g11, g12, g22, h1, h2 = [spread(i) for i in range(5)]
    inv = 1.0 / (g11 * g22 - g12 * g12)
    y1 = (g22 * h1 - g12 * h2) * inv
    y2 = (g11 * h2 - g12 * h1) * inv
    c, xlo, xhi, ylo, yhi, zlo, zhi = [own_ref[j : j + 1, :] for j in range(7)]
    lane32, row32 = iota((CY, 128), 1), iota((CY, 128), 0)
    on_y = jnp.where(row32 == 0, ylo, jnp.where(row32 == CY - 1, yhi, 0.0))
    on_z = jnp.where(lane32 == 0, zlo, jnp.where(lane32 == CZ - 1, zhi, 0.0))
    for x in range(CX):
        w2 = w2_ref[x] + sigma_ref[x] * c + kappa_ref[1, x] * on_y + kappa_ref[2, x] * on_z
        if x == 0:
            w2 = w2 + kappa_ref[0, x] * xlo
        if x == CX - 1:
            w2 = w2 + kappa_ref[0, x] * xhi
        field_ref[x] = y1 * z1_ref[x] + y2 * (z2_ref[x] + c)
        res_ref[x] = r_ref[x] - y1 * w1_ref[x] - y2 * w2


def call(kernel, out_shapes, scratch=(), name=None, inputs=pltpu.VMEM, semaphores=(), limit=24 << 20):
    vmem = pl.BlockSpec(memory_space=pltpu.VMEM)

    def run(*args):
        return pl.pallas_call(
            kernel,
            out_shape=[jax.ShapeDtypeStruct(s, F32) for s in out_shapes],
            in_specs=[pl.BlockSpec(memory_space=inputs)] * len(args),
            out_specs=[vmem] * len(out_shapes),
            scratch_shapes=[pltpu.VMEM(s, F32) for s in scratch] + list(semaphores),
            compiler_params=pltpu.CompilerParams(vmem_limit_bytes=limit),
            name=name,
        )(*args)

    return run


def shards(sizes, r, sigma, kappa, inverse_rows):
    nx, ny, nz = sizes
    field, plane, tile, coarse = (CX, CY, CZ), (CY, CZ), (8, 128), (CELLS, 128)
    planes = [plane, plane, tile, tile]
    to_xy = (nx * ny, 2, 128)

    fold = []
    for x in range(0, nx, 2):
        ring = [x * ny + y for y in range(ny)] + [(x + 1) * ny + y for y in reversed(range(ny))]
        fold += list(zip(ring, ring[1:] + ring[:1]))
    unfold = [(b, a) for a, b in fold]

    def halo(parts):
        xlo, xhi, y_one, y_two = parts
        return (
            lax.ppermute(xhi, "gx", [(i, (i + 1) % nx) for i in range(nx)]),
            lax.ppermute(xlo, "gx", [((i + 1) % nx, i) for i in range(nx)]),
            lax.ppermute(y_one, ("gx", "gy"), fold),
            lax.ppermute(y_two, ("gx", "gy"), unfold),
        )

    def along_z(message):
        return lax.all_to_all(message, "gz", split_axis=0, concat_axis=0, tiled=True)

    def along_xy(message):
        return lax.all_to_all(message, ("gx", "gy"), split_axis=0, concat_axis=0, tiled=True)

    bind = lambda kernel, *a: functools.partial(kernel, sizes, *a)
    zmsg, loc, alpha, spread, *sides = call(
        bind(begin_kernel), [(nz * 5, 1, 128), (3, *coarse), coarse, tile, *planes],
        [field, field, (3, *field), tile], "begin", pltpu.HBM, [pltpu.SemaphoreType.DMA((4,))], 55100 << 10,
    )(r, sigma, kappa, inverse_rows)
    zrec = along_z(zmsg)
    halos = halo(sides)
    xmsg, own, zhalo, chain, final = call(
        bind(first_lines_kernel), [to_xy, tile, tile, (4, nz, 128), tile], [coarse], "lines_first"
    )(zrec, loc, alpha)
    xrec = along_xy(xmsg)
    z1, w1, jac, zmsg, alpha = call(
        bind(first_kernel), [field, field, field, (nz * 4, 1, 128), coarse], name="operator_first"
    )(r, sigma, kappa, xrec, own, zhalo, *halos, loc, spread)
    zrec = along_z(zmsg)
    part, zhalo, z2, *sides = call(
        bind(second_lines_kernel), [tile, tile, field, *planes], [coarse], "lines_second"
    )(zrec, loc, alpha, chain, final, jac)
    halos = halo(sides)
    w2, xmsg = call(bind(second_kernel), [field, to_xy], [(128, 128)], "operator_second")(
        r, w1, sigma, kappa, z2, zhalo, part, *halos
    )
    xrec = along_xy(xmsg)
    sums, values = call(bind(plane_kernel), [(1, 128), tile], [(2, nx * ny, 128)], "plane")(xrec)
    sums = along_z(jnp.broadcast_to(sums[None], (nz, 1, 128)))
    return tuple(
        call(end_kernel, [field, field], name="end")(sums, values, r, sigma, kappa, z1, w1, z2, w2)
    )


def solution(mesh):
    sizes = (mesh.shape["gx"], mesh.shape["gy"], mesh.shape["gz"])
    spec = P("gx", "gy", "gz")

    def run(r, sigma, kappa, inverse):
        return shards(sizes, r, sigma, kappa, inverse.reshape(8, 128))

    return jax.shard_map(
        run,
        mesh=mesh,
        in_specs=(spec, spec, P(None, "gx", "gy", "gz"), P(("gx", "gy", "gz"), None)),
        out_specs=(spec, spec),
        check_vma=False,
    )
```

```python
import functools

import jax
import jax.numpy as jnp
from jax import lax
from jax.experimental import pallas as pl
from jax.experimental.pallas import tpu as pltpu
from jax.sharding import PartitionSpec as P

CX, CY, CZ = 8, 32, 128
CELLS = 16
LINES = 16
THETA = 1.0 / 128.0
WEIGHT = 0.6
PART_AT, LOW_AT, HIGH_AT = 32, 64, 96
HIGHEST = lax.Precision.HIGHEST
F32 = jnp.float32


def iota(shape, dim):
    return lax.broadcasted_iota(jnp.int32, shape, dim)


def dot(a, b):
    return lax.dot_general(
        a, b, (((1,), (0,)), ((), ())), precision=HIGHEST, preferred_element_type=F32
    )


def dot_t(a, b):
    return lax.dot_general(
        a, b, (((1,), (1,)), ((), ())), precision=HIGHEST, preferred_element_type=F32
    )


def one_where(cond):
    return jnp.where(cond, 1.0, 0.0).astype(F32)


def lines_of(field):
    low = (field[0] + field[1]) + (field[2] + field[3])
    high = (field[4] + field[5]) + (field[6] + field[7])
    stacked = jnp.concatenate([low, high], axis=0)
    by_line = one_where(iota((128, 64), 1) // 4 == iota((128, 64), 0))
    by_cell = one_where(iota((CELLS, 128), 1) // 8 == iota((CELLS, 128), 0))
    return dot_t(by_cell, dot(by_line, stacked))


def faces_of(field):
    shape = (CX, CY, 128)
    here = iota(shape, 2) == (iota(shape, 0) % 4) * 32 + iota(shape, 1)

    def packed(z):
        rows = jnp.sum(jnp.where(here, field[:, :, z : z + 1], 0.0), axis=1)
        halves = [jnp.sum(rows[i : i + 4], axis=0, keepdims=True) for i in (0, 4)]
        return jnp.concatenate(halves, axis=0)

    return packed(0), packed(CZ - 1)


def write_z_message(zmsg_ref, pairs, faces, spread_inverse, total, sizes):
    nz, count = sizes[2], 2 + len(pairs)
    mz = lax.axis_index("gz")
    lane1, lane8, row8 = iota((1, 128), 1), iota((8, 128), 1), iota((8, 128), 0)
    only = lambda v: jnp.where(lane1 < LINES, v, 0.0)
    tails = [pltpu.roll(only(a), 96, 1) + pltpu.roll(only(b), 112, 1) if a is not None else None for a, b in pairs]
    mine = spread_inverse * total
    inside = lane8 // 24 == row8 % 4
    zero = jnp.zeros((1, 128), F32)
    for p in range(nz):
        moved = jnp.where(inside, pltpu.roll(mine, (8 - 8 * p) % 128, 1), 0.0)
        zmsg_ref[p * count] = zero
        zmsg_ref[p * count + 1] = zero
        for h, tail in enumerate(tails):
            row = jnp.sum(moved[4 * h : 4 * h + 4], axis=0, keepdims=True) if h < 2 else zero
            zmsg_ref[p * count + 2 + h] = row if tail is None else row + tail

    @pl.when(mz > 0)
    def _():
        zmsg_ref[(mz - 1) * count] = faces[0][0:1]
        zmsg_ref[(mz - 1) * count + 1] = faces[0][1:2]

    @pl.when(mz < nz - 1)
    def _():
        zmsg_ref[(mz + 1) * count] = faces[1][0:1]
        zmsg_ref[(mz + 1) * count + 1] = faces[1][1:2]


def write_planes(field, planes):
    xlo, xhi, y_one, y_two = planes
    xlo[...] = field[0]
    xhi[...] = field[CX - 1]
    core = lax.axis_index("gx") % 2
    low, high = field[:, 0, :], field[:, CY - 1, :]
    y_one[...] = jnp.where(core == 0, high, low)
    y_two[...] = jnp.where(core == 0, low, high)


def y_halos(y_one, y_two):
    core = lax.axis_index("gx") % 2
    return jnp.where(core == 0, y_one, y_two), jnp.where(core == 0, y_two, y_one)


def begin_kernel(
    sizes, r_hbm, sigma_hbm, kappa_hbm, inv_hbm,
    zmsg_ref, loc_ref, alpha_ref, spread_ref, xlo, xhi, ylo, yhi,
    r_ref, sigma_ref, kappa_ref, inv_ref, sems
):
    pairs = ((kappa_hbm, kappa_ref), (sigma_hbm, sigma_ref), (r_hbm, r_ref), (inv_hbm, inv_ref))
    copies = [pltpu.make_async_copy(a, b, sems.at[i]) for i, (a, b) in enumerate(pairs)]
    for copy in copies:
        copy.start()
    for copy in copies:
        copy.wait()
    r, sigma = r_ref[...], sigma_ref[...]
    kx, ky, kz = kappa_ref[0], kappa_ref[1], kappa_ref[2]
    jac = r * (WEIGHT / (sigma + 2.0 * (kx + ky + kz)))
    write_planes(jac, (xlo, xhi, ylo, yhi))
    unused = iota((CELLS, 128), 1) >= LINES
    e = jnp.where(unused, 1.0, lines_of(sigma))
    g = jnp.where(unused, 1.0, lines_of(kz) * 0.125)
    rhs = lines_of(r)
    row = lambda a, k: a[k : k + 1, :]
    first, mid, last = row(e, 0), row(g, 0), row(e, 1)
    cur_first, cur = row(rhs, 0), row(rhs, 1)
    zero = jnp.zeros((1, 128), F32)
    for c in range(3):
        for k in (0, CELLS - 1):
            loc_ref[c, k : k + 1, :] = zero
    for k in (0, CELLS - 1):
        alpha_ref[k : k + 1, :] = zero
    for k in range(1, CELLS - 1):
        inv = 1.0 / (mid + last + row(g, k))
        mu, gam = mid * inv, row(g, k) * inv
        loc_ref[0, k : k + 1, :] = mu
        loc_ref[1, k : k + 1, :] = gam
        loc_ref[2, k : k + 1, :] = inv
        alpha_ref[k : k + 1, :] = cur * inv
        first = first + mu * last
        mid = mu * row(g, k)
        last = row(e, k + 1) + gam * last
        cur_first = cur_first + mu * cur
        cur = row(rhs, k + 1) + gam * cur
    move = one_where((iota((128, 128), 0) % 16) * 8 + iota((128, 128), 0) // 16 == iota((128, 128), 1))
    plain = dot(inv_ref[...], move)
    step = iota((8, 128), 0) % 4
    spread_inverse = plain
    for k in range(1, 4):
        spread_inverse = jnp.where(step == k, pltpu.roll(plain, 24 * k, 1), spread_inverse)
    spread_ref[...] = spread_inverse
    pairs = [(cur_first, cur), (first, mid), (last, row(g, CELLS - 1))]
    write_z_message(zmsg_ref, pairs, faces_of(jac), spread_inverse, jnp.sum(r), sizes)


def solve_chain(sizes, fresh, zrec_ref, loc_ref, alpha_ref, chain_ref, final_ref, sol_ref):
    nz = sizes[2]
    mz = lax.axis_index("gz")
    count = 5 if fresh else 4
    zero = jnp.zeros((1, 128), F32)
    columns = []
    for h in range(count - 2 if fresh else 1):
        rows = jnp.concatenate([zrec_ref[p * count + 2 + h] for p in range(nz)], axis=0)
        used = iota(rows.shape, 1) < LINES
        for shift in (32, 16):
            columns.append(jnp.where(used, pltpu.roll(rows, shift, 1), 1.0))
    part = lambda p, i: columns[i][p : p + 1, :]

    def mine(i):
        row = pltpu.roll(zrec_ref[mz * count + 2 + i // 2], 32 - 16 * (i % 2), 1)
        return jnp.where(iota((1, 128), 1) < LINES, row, 1.0)

    if fresh:
        one = zero + 1.0
        cond, cond_own, hold, ginv = zero, zero, one, one
        for p in range(nz - 1):
            a, m, b, g = part(p, 2), part(p, 3), part(p, 4), part(p, 5)
            at_first = a + cond
            s = m + at_first
            n = b * s + m * at_first
            inv = 1.0 / (n + g * s)
            chain_ref[0, p : p + 1, :] = g * m * inv
            c2 = g * s * inv
            chain_ref[1, p : p + 1, :] = c2
            cond = g * n * inv
            here = mz == p + 1
            cond_own = jnp.where(here, cond, cond_own)
            hold = jnp.where(here, c2, hold)
            ginv = jnp.where(here, g, ginv)
        left_cond, left_hold, left_ginv = cond_own, hold, 1.0 / ginv
        cond = part(nz - 1, 5)
        cond_own, hold, ginv = cond, one, one
        for p in range(nz - 1, 0, -1):
            a, m, b, g = part(p, 2), part(p, 3), part(p, 4), part(p - 1, 5)
            at_last = b + cond
            s = m + at_last
            n = a * s + m * at_last
            inv = 1.0 / (n + g * s)
            chain_ref[2, p : p + 1, :] = g * m * inv
            c2 = g * s * inv
            chain_ref[3, p : p + 1, :] = c2
            cond = g * n * inv
            here = mz == p - 1
            cond_own = jnp.where(here, cond, cond_own)
            hold = jnp.where(here, c2, hold)
            ginv = jnp.where(here, g, ginv)
        right_cond, right_hold, right_ginv = cond_own, hold, 1.0 / ginv
        for c, p in ((0, nz - 1), (1, nz - 1), (2, 0), (3, 0)):
            chain_ref[c, p : p + 1, :] = zero
        big_a = mine(2) + left_cond
        big_b = mine(4) + right_cond
        m = mine(3)
        det_inv = 1.0 / (big_a * m + big_b * m + big_a * big_b)
        f1, f2, f3 = (big_b + m) * det_inv, m * det_inv, (big_a + m) * det_inv
        final_ref[...] = jnp.concatenate(
            [f1, f2, f3, left_ginv, left_hold, right_ginv, right_hold, zero], axis=0
        )
    else:
        f1, f2, f3, left_ginv, left_hold, right_ginv, right_hold = [
            final_ref[i : i + 1, :] for i in range(7)
        ]
    chain = lambda c, p: chain_ref[c, p : p + 1, :]
    cur, cur_left = zero, zero
    for p in range(nz - 1):
        cur = chain(0, p) * (part(p, 0) + cur) + chain(1, p) * part(p, 1)
        cur_left = jnp.where(mz == p + 1, cur, cur_left)
    cur, cur_right = zero, zero
    for p in range(nz - 1, 0, -1):
        cur = chain(2, p) * (part(p, 1) + cur) + chain(3, p) * part(p, 0)
        cur_right = jnp.where(mz == p - 1, cur, cur_right)
    cur_first = mine(0) + cur_left
    cur_last = mine(1) + cur_right
    sol_first = f1 * cur_first + f2 * cur_last
    sol_last = f2 * cur_first + f3 * cur_last
    below = cur_left * left_ginv + left_hold * sol_first
    above = cur_right * right_ginv + right_hold * sol_last
    sol_ref[0:1, :] = sol_first
    sol_ref[CELLS - 1 : CELLS, :] = sol_last
    value = sol_last
    for k in range(CELLS - 2, 0, -1):
        value = alpha_ref[k : k + 1, :] + loc_ref[0, k : k + 1, :] * sol_first + loc_ref[1, k : k + 1, :] * value
        sol_ref[k : k + 1, :] = value
    lanes16 = iota((CELLS, 128), 1) < LINES
    sol = jnp.where(lanes16, sol_ref[...], 0.0) * THETA

    line, lane = iota((128, 128), 0), iota((128, 128), 1)
    picks = [
        one_where(line == lane // 16),
        one_where(line == 8 + lane // 16),
        one_where((line == (lane // 16) * 8) & (lane < 32)),
        one_where((line == (lane // 16) * 8 + 7) & (lane < 32)),
    ]
    keep = iota((CELLS, 128), 1) % 16 == iota((CELLS, 128), 0)
    x_low, x_high, y_low, y_high = [
        jnp.sum(jnp.where(keep, dot(sol, pick), 0.0), axis=0, keepdims=True) for pick in picks
    ]

    lane8, row8 = iota((8, 128), 1), iota((8, 128), 0)
    of_row = (lane8 // 8 == row8 // 4) & (lane8 < LINES)
    to_high = one_where((lane >= HIGH_AT) & ((lane - HIGH_AT) // 4 == line % 8) & (line < LINES))
    to_low = one_where(
        (lane >= LOW_AT) & (lane < HIGH_AT) & ((lane - LOW_AT) // 4 == line % 8) & (line < LINES)
    )
    lines_part = dot(jnp.where(of_row, below, 0.0), to_high) + dot(jnp.where(of_row, above, 0.0), to_low)
    face = jnp.zeros((8, 128), F32)
    for peer, at in ((jnp.maximum(mz - 1, 0), HIGH_AT), (jnp.minimum(mz + 1, nz - 1), LOW_AT)):
        packed = jnp.where(row8 < 4, zrec_ref[peer * count], zrec_ref[peer * count + 1])
        for k in range(4):
            here = (lane8 // 32 == at // 32) & (row8 % 4 == k)
            face = jnp.where(here, pltpu.roll(packed, (at - 32 * k) % 128, 1), face)
    zhalo = jnp.where(lane8 >= LOW_AT, face + THETA * lines_part, 0.0)
    return x_low, x_high, y_low, y_high, zhalo


def coarse_totals(zrec_ref, count, nz):
    totals = [zrec_ref[2], zrec_ref[3]]
    for p in range(1, nz):
        for h in range(2):
            totals[h] = totals[h] + zrec_ref[p * count + 2 + h]
    return totals


def first_lines_kernel(
    sizes, zrec_ref, loc_ref, alpha_ref, h0, h1, xmsg_ref, own_ref, zhalo_ref, chain_ref, final_ref, sol_ref
):
    nx, ny, nz = sizes
    mx, my = lax.axis_index("gx"), lax.axis_index("gy")
    x_low, x_high, y_low, y_high, zhalo = solve_chain(
        sizes, True, zrec_ref, loc_ref, alpha_ref, chain_ref, final_ref, sol_ref
    )
    zero = jnp.zeros((1, 128), F32)
    own_ref[...] = jnp.concatenate([x_low, x_high] + [zero] * 6, axis=0)
    zhalo_ref[...] = zhalo

    totals = coarse_totals(zrec_ref, 5, nz)
    lane1 = iota((1, 128), 1)

    def block(i, width, at, offset):
        moved = pltpu.roll(totals[i // 4], (at - 24 * (i % 4) - offset) % 128, 1)
        return jnp.where((lane1 >= at) & (lane1 < at + width), moved, 0.0)

    second = iota((2, 128), 0) == 1
    for i in range(nx):
        sums = block(i, 24, PART_AT, 0)
        if i > 0:
            sums = sums + block(i - 1, 8, PART_AT + 24, 8)
        if i < nx - 1:
            sums = sums + block(i + 1, 8, PART_AT + 32, 8)
        both = jnp.where(second, sums, 0.0)
        for j in range(ny):
            xmsg_ref[i * ny + j] = both
    here = mx * ny + my

    @pl.when(mx > 0)
    def _():
        xmsg_ref[here - ny, 0:1, :] = x_low

    @pl.when(mx < nx - 1)
    def _():
        xmsg_ref[here + ny, 0:1, :] = x_high

    @pl.when(my > 0)
    def _():
        xmsg_ref[here - 1, 0:1, :] = y_low

    @pl.when(my < ny - 1)
    def _():
        xmsg_ref[here + 1, 0:1, :] = y_high


def scale(sigma_ref, kappa_ref, x):
    return WEIGHT / (sigma_ref[x] + 2.0 * (kappa_ref[0, x] + kappa_ref[1, x] + kappa_ref[2, x]))


def ends_of(face):
    lane32, row32 = iota((CY, 128), 1), iota((CY, 128), 0)
    diagonal = (lane32 == row32 + HIGH_AT) | (lane32 == row32 + LOW_AT)
    spots = jnp.concatenate([jnp.where(diagonal, face[x : x + 1, :], 0.0) for x in range(CX)], axis=0)
    j, k = iota((128, 128), 0), iota((128, 128), 1)
    to_ends = one_where(((j >= HIGH_AT) & (k == 0)) | ((j >= LOW_AT) & (j < HIGH_AT) & (k == CZ - 1)))
    return dot(spots, to_ends)


def apply_operator(z, xlo, xhi, ylo, yhi, ends, sigma_ref, kappa_ref, w_ref):
    lane32, row32 = iota((CY, 128), 1), iota((CY, 128), 0)
    for x in range(CX):
        here_z = z[x]
        before = z[x - 1] if x > 0 else xlo
        after = z[x + 1] if x < CX - 1 else xhi
        y_less = jnp.where(row32 == 0, ylo[x : x + 1, :], pltpu.roll(here_z, 1, 0))
        y_more = jnp.where(row32 == CY - 1, yhi[x : x + 1, :], pltpu.roll(here_z, CY - 1, 0))
        z_less = jnp.where(lane32 == 0, 0.0, pltpu.roll(here_z, 1, 1))
        z_more = jnp.where(lane32 == CZ - 1, 0.0, pltpu.roll(here_z, CZ - 1, 1))
        twice = 2.0 * here_z
        w_ref[x] = (
            sigma_ref[x] * here_z
            + kappa_ref[0, x] * (twice - before - after)
            + kappa_ref[1, x] * (twice - y_less - y_more)
            + kappa_ref[2, x] * (twice - z_less - z_more - ends[x * 32 : x * 32 + 32])
        )


def wide(row):
    return jnp.where(iota((CY, 128), 1) // 16 == iota((CY, 128), 0) // 4, row, 0.0)


def thin(row):
    return jnp.where(iota((CX, 128), 1) // 16 == iota((CX, 128), 0) // 4, row, 0.0)


def to_cells():
    return one_where(iota((128, 128), 0) % 16 == iota((128, 128), 1) // 8)


def full_direction(sizes, base, xrec_ref, own_ref, zhalo_ref, halos, z_ref):
    nx, ny, nz = sizes
    mx, my, mz = lax.axis_index("gx"), lax.axis_index("gy"), lax.axis_index("gz")
    here = mx * ny + my
    sums = xrec_ref[0, 1:2, :]
    for q in range(1, nx * ny):
        sums = sums + xrec_ref[q, 1:2, :]
    lane1 = iota((1, 128), 1)
    coarse = lambda at: jnp.sum(jnp.where(lane1 == at + my, sums, 0.0))
    c_own = coarse(PART_AT + 8)
    c_zlo, c_zhi = coarse(PART_AT), coarse(PART_AT + 16)
    c_ylo, c_yhi = coarse(PART_AT + 7), coarse(PART_AT + 9)
    c_xlo, c_xhi = coarse(PART_AT + 24), coarse(PART_AT + 32)

    left = xrec_ref[jnp.maximum(here - ny, 0), 0:1, :]
    right = xrec_ref[jnp.minimum(here + ny, nx * ny - 1), 0:1, :]
    front = xrec_ref[jnp.maximum(here - 1, 0), 0:1, :]
    back = xrec_ref[jnp.minimum(here + 1, nx * ny - 1), 0:1, :]
    rows = jnp.concatenate(
        [wide(own_ref[0:1, :]), wide(own_ref[1:2, :]), wide(left), wide(right), thin(front), thin(back)],
        axis=0,
    )
    lines = dot(rows, to_cells())
    xlo, xhi = halos[0][...], halos[1][...]
    ylo, yhi = y_halos(halos[2][...], halos[3][...])
    xlo = jnp.where(mx > 0, xlo + lines[64:96] + c_xlo, 0.0)
    xhi = jnp.where(mx < nx - 1, xhi + lines[96:128] + c_xhi, 0.0)
    ylo = jnp.where(my > 0, ylo + lines[128:136] + c_ylo, 0.0)
    yhi = jnp.where(my < ny - 1, yhi + lines[136:144] + c_yhi, 0.0)
    face = zhalo_ref[...]
    high = jnp.where(mz > 0, face + c_zlo, 0.0)
    low = jnp.where(mz < nz - 1, face + c_zhi, 0.0)
    ends = ends_of(jnp.where(iota((8, 128), 1) >= HIGH_AT, high, low))
    z = [base(x) + lines[(x // 4) * 32 : (x // 4) * 32 + 32] + c_own for x in range(CX)]
    for x in range(CX):
        z_ref[x] = z[x]
    return z, xlo, xhi, ylo, yhi, ends


def first_kernel(
    sizes, r_ref, sigma_ref, kappa_ref, xrec_ref, own_ref, zhalo_ref, h0, h1, h2, h3,
    loc_ref, spread_ref, z_ref, w_ref, jac_ref, zmsg_ref, alpha_ref
):
    scales = [scale(sigma_ref, kappa_ref, x) for x in range(CX)]
    base = lambda x: scales[x] * r_ref[x]
    parts = full_direction(sizes, base, xrec_ref, own_ref, zhalo_ref, (h0, h1, h2, h3), z_ref)
    apply_operator(*parts, sigma_ref, kappa_ref, w_ref)
    field = w_ref[...]
    for x in range(CX):
        jac_ref[x] = scales[x] * w_ref[x]
    rhs = lines_of(field)
    row = lambda a, k: a[k : k + 1, :]
    cur_first, cur = row(rhs, 0), row(rhs, 1)
    zero = jnp.zeros((1, 128), F32)
    for k in (0, CELLS - 1):
        alpha_ref[k : k + 1, :] = zero
    for k in range(1, CELLS - 1):
        alpha_ref[k : k + 1, :] = cur * loc_ref[2, k : k + 1, :]
        cur_first = cur_first + loc_ref[0, k : k + 1, :] * cur
        cur = row(rhs, k + 1) + loc_ref[1, k : k + 1, :] * cur
    write_z_message(
        zmsg_ref, [(cur_first, cur), (None, None)], faces_of(jac_ref[...]), spread_ref[...], jnp.sum(field), sizes
    )


def second_lines_kernel(
    sizes, zrec_ref, loc_ref, alpha_ref, chain_ref, final_ref, jac_ref,
    part_ref, zhalo_ref, z_ref, xlo, xhi, ylo, yhi, sol_ref
):
    x_low, x_high, _, _, zhalo = solve_chain(
        sizes, False, zrec_ref, loc_ref, alpha_ref, chain_ref, final_ref, sol_ref
    )
    zhalo_ref[...] = zhalo
    lines = dot(jnp.concatenate([wide(x_low), wide(x_high)], axis=0), to_cells())
    for x in range(CX):
        z_ref[x] = jac_ref[x] + lines[(x // 4) * 32 : (x // 4) * 32 + 32]
    write_planes(z_ref[...], (xlo, xhi, ylo, yhi))
    zero = jnp.zeros((1, 128), F32)
    part_ref[...] = jnp.concatenate(coarse_totals(zrec_ref, 4, sizes[2]) + [zero] * 6, axis=0)


FACES = range(1, 7)
TERMS = (
    [("g11", -1, -1), ("g12", -1, -1), ("g22", -1, -1), ("h1", -1, -1), ("h2", -1, -1)]
    + [(name, j, -1) for name in ("h2", "g12", "g22") for j in range(7)]
    + [("g22", 0, j) for j in range(7)]
    + [("g22", j, j) for j in FACES]
    + [("g22", j, k) for j in FACES for k in FACES if j < k and (j - 1) // 2 != (k - 1) // 2]
)
NAMES = ("g11", "g12", "g22", "h1", "h2")
TERMS_AT, TERMS_ROW = 96, 32


def second_kernel(
    sizes, r_ref, w1_ref, sigma_ref, kappa_ref, z_ref, zhalo_ref, part_ref, h0, h1, h2, h3,
    w_ref, xmsg_ref, terms_ref
):
    nx, ny, nz = sizes
    mx, my, mz = lax.axis_index("gx"), lax.axis_index("gy"), lax.axis_index("gz")
    xlo = jnp.where(mx > 0, h0[...], 0.0)
    xhi = jnp.where(mx < nx - 1, h1[...], 0.0)
    ylo, yhi = y_halos(h2[...], h3[...])
    ylo = jnp.where(my > 0, ylo, 0.0)
    yhi = jnp.where(my < ny - 1, yhi, 0.0)
    face = zhalo_ref[...]
    high, low = jnp.where(mz > 0, face, 0.0), jnp.where(mz < nz - 1, face, 0.0)
    ends = ends_of(jnp.where(iota((8, 128), 1) >= HIGH_AT, high, low))
    apply_operator([z_ref[x] for x in range(CX)], xlo, xhi, ylo, yhi, ends, sigma_ref, kappa_ref, w_ref)

    r, w1, w2, sigma = r_ref[...], w1_ref[...], w_ref[...], sigma_ref[...]
    kz = kappa_ref[2]
    rows = lambda a: jnp.sum(jnp.sum(a, axis=0), axis=0, keepdims=True)
    lane1 = iota((1, 128), 1)
    pick = lambda profile, face: jnp.where(lane1 == (0 if face == 5 else CZ - 1), profile, 0.0)
    low_row = lambda a: jnp.sum(a, axis=0, keepdims=True)
    partner = {"h2": r, "g12": w1, "g22": w2}
    partner_ref = {"h2": r_ref, "g12": w1_ref, "g22": w_ref}
    z_profiles = {name: rows(kz * f) for name, f in partner.items()}
    z_sigma, z_self = rows(kz * sigma), rows(kz * kz)

    def plane(ref, f):
        if f < 3:
            return ref[0 if f == 1 else CX - 1]
        return ref[:, 0 if f == 3 else CY - 1, :]

    face_weight = {f: plane(kappa_ref.at[(f - 1) // 2], f) for f in range(1, 5)}

    def on_face(f, other):
        return low_row(face_weight[f] * plane(other, f))

    def term(name, j, k):
        if j == -1:
            a, b = {"g11": (w1, w1), "g12": (w1, w2), "g22": (w2, w2), "h1": (w1, r), "h2": (w2, r)}[name]
            return rows(a * b)
        if k == -1:
            twice = 2.0 if name == "g22" else 1.0
            if j == 0:
                return twice * rows(sigma * partner[name])
            if j > 4:
                return twice * pick(z_profiles[name], j)
            return twice * on_face(j, partner_ref[name])
        if j == 0:
            if k == 0:
                return rows(sigma * sigma)
            return 2.0 * (pick(z_sigma, k) if k > 4 else on_face(k, sigma_ref))
        if j == k:
            return pick(z_self, j) if j > 4 else on_face(j, kappa_ref.at[(j - 1) // 2])
        if k > 4:
            return 2.0 * pick(on_face(j, kappa_ref.at[2]), k)
        x, y = 0 if j == 1 else CX - 1, 0 if k == 3 else CY - 1
        return 2.0 * kappa_ref[0, x, y : y + 1, :] * kappa_ref[1, x, y : y + 1, :]

    for i, (name, j, k) in enumerate(TERMS):
        terms_ref[i : i + 1, :] = term(name, j, k)
    for i in range(len(TERMS), 128):
        if i % 8 == 0:
            terms_ref[i : i + 8, :] = jnp.zeros((8, 128), F32)
        elif i == len(TERMS):
            stop = -(-i // 8) * 8
            terms_ref[i:stop, :] = jnp.zeros((stop - i, 128), F32)
    poly = dot_t(jnp.full((8, 128), 1.0, F32), terms_ref[...])[0:1, :]
    halves = [
        jnp.where(lane1 < TERMS_AT, part_ref[h : h + 1, :], pltpu.roll(poly, TERMS_AT - TERMS_ROW * h, 1))
        for h in range(2)
    ]
    both = jnp.concatenate(halves, axis=0)
    for q in range(nx * ny):
        xmsg_ref[q] = both


def plane_kernel(sizes, xrec_ref, sums_ref, own_ref, flat_ref):
    nx, ny, nz = sizes
    mx, my, mz = lax.axis_index("gx"), lax.axis_index("gy"), lax.axis_index("gz")
    count = nx * ny
    total = xrec_ref[0]
    for q in range(count):
        for h in range(2):
            flat_ref[h, q : q + 1, :] = xrec_ref[q, h : h + 1, :]
        if q > 0:
            total = total + xrec_ref[q]
    lane, row = iota((count, 128), 1), iota((count, 128), 0)
    tx, ty = row // ny, row % ny

    def value(qx, qy, dz, valid):
        at = (qx & 3) * 24 + 8 + 8 * dz + qy
        chosen = jnp.where(qx < 4, total[0:1, :], total[1:2, :])
        return jnp.sum(jnp.where((lane == at) & valid, chosen, 0.0), axis=1, keepdims=True)

    always = row >= 0
    c = value(tx, ty, 0, always)
    near = [
        value(tx - 1, ty, 0, tx > 0),
        value(tx + 1, ty, 0, tx < nx - 1),
        value(tx, ty - 1, 0, ty > 0),
        value(tx, ty + 1, 0, ty < ny - 1),
        value(tx, ty, -1, always & (mz > 0)),
        value(tx, ty, 1, always & (mz < nz - 1)),
    ]
    v = [c] + [c - n for n in near]
    lane1 = iota((1, 128), 1)
    out = jnp.zeros((1, 128), F32)
    for h in range(2):
        terms = list(enumerate(TERMS[TERMS_ROW * h : TERMS_ROW * (h + 1)], TERMS_AT))
        first = jnp.where(lane < 0, 1.0, 0.0)
        second = first
        for j in range(-1, 7):
            amount = 1.0 if j == -1 else v[j]
            is_first = lane < 0
            is_second = is_first
            for i, (_, a, b) in terms:
                if a == j:
                    is_first = is_first | (lane == i)
                if b == j:
                    is_second = is_second | (lane == i)
            first = jnp.where(is_first, amount, first)
            second = jnp.where(is_second, amount, second)
        weights = jnp.where(lane >= TERMS_AT, flat_ref[h], 0.0)
        added = jnp.sum(weights * first * second, axis=0, keepdims=True)
        for n, name in enumerate(NAMES):
            mask = lane1 < 0
            for i, (of, _, _) in terms:
                if of == name:
                    mask = mask | (lane1 == i)
            add = jnp.sum(jnp.where(mask, added, 0.0), axis=1, keepdims=True)
            out = jnp.where(lane1 == n, out + add, out)
    sums_ref[...] = out
    mine = row == mx * ny + my
    for j in range(7):
        own = jnp.sum(jnp.where(mine & (lane == 0), v[j], 0.0))
        own_ref[j : j + 1, :] = jnp.full((1, 128), own, F32)
    own_ref[7:8, :] = jnp.zeros((1, 128), F32)


def end_kernel(all_ref, own_ref, r_ref, sigma_ref, kappa_ref, z1_ref, w1_ref, z2_ref, w2_ref, field_ref, res_ref):
    sums = all_ref[0]
    for q in range(1, all_ref.shape[0]):
        sums = sums + all_ref[q]
    lane = iota((1, 128), 1)
    spread = lambda i: jnp.sum(jnp.where(lane == i, sums, 0.0), axis=1, keepdims=True)
    g11, g12, g22, h1, h2 = [spread(i) for i in range(5)]
    inv = 1.0 / (g11 * g22 - g12 * g12)
    y1 = (g22 * h1 - g12 * h2) * inv
    y2 = (g11 * h2 - g12 * h1) * inv
    c, xlo, xhi, ylo, yhi, zlo, zhi = [own_ref[j : j + 1, :] for j in range(7)]
    lane32, row32 = iota((CY, 128), 1), iota((CY, 128), 0)
    on_y = jnp.where(row32 == 0, ylo, jnp.where(row32 == CY - 1, yhi, 0.0))
    on_z = jnp.where(lane32 == 0, zlo, jnp.where(lane32 == CZ - 1, zhi, 0.0))
    for x in range(CX):
        w2 = w2_ref[x] + sigma_ref[x] * c + kappa_ref[1, x] * on_y + kappa_ref[2, x] * on_z
        if x == 0:
            w2 = w2 + kappa_ref[0, x] * xlo
        if x == CX - 1:
            w2 = w2 + kappa_ref[0, x] * xhi
        field_ref[x] = y1 * z1_ref[x] + y2 * (z2_ref[x] + c)
        res_ref[x] = r_ref[x] - y1 * w1_ref[x] - y2 * w2


def call(kernel, out_shapes, scratch=(), name=None, inputs=pltpu.VMEM, semaphores=(), limit=24 << 20):
    vmem = pl.BlockSpec(memory_space=pltpu.VMEM)

    def run(*args):
        return pl.pallas_call(
            kernel,
            out_shape=[jax.ShapeDtypeStruct(s, F32) for s in out_shapes],
            in_specs=[pl.BlockSpec(memory_space=inputs)] * len(args),
            out_specs=[vmem] * len(out_shapes),
            scratch_shapes=[pltpu.VMEM(s, F32) for s in scratch] + list(semaphores),
            compiler_params=pltpu.CompilerParams(vmem_limit_bytes=limit),
            name=name,
        )(*args)

    return run


def shards(sizes, r, sigma, kappa, inverse_rows):
    nx, ny, nz = sizes
    field, plane, tile, coarse = (CX, CY, CZ), (CY, CZ), (8, 128), (CELLS, 128)
    planes = [plane, plane, tile, tile]
    to_xy = (nx * ny, 2, 128)

    fold = []
    for x in range(0, nx, 2):
        ring = [x * ny + y for y in range(ny)] + [(x + 1) * ny + y for y in reversed(range(ny))]
        fold += list(zip(ring, ring[1:] + ring[:1]))
    unfold = [(b, a) for a, b in fold]

    def halo(parts):
        xlo, xhi, y_one, y_two = parts
        return (
            lax.ppermute(xhi, "gx", [(i, (i + 1) % nx) for i in range(nx)]),
            lax.ppermute(xlo, "gx", [((i + 1) % nx, i) for i in range(nx)]),
            lax.ppermute(y_one, ("gx", "gy"), fold),
            lax.ppermute(y_two, ("gx", "gy"), unfold),
        )

    def along_z(message):
        return lax.all_to_all(message, "gz", split_axis=0, concat_axis=0, tiled=True)

    def along_xy(message):
        return lax.all_to_all(message, ("gx", "gy"), split_axis=0, concat_axis=0, tiled=True)

    bind = lambda kernel, *a: functools.partial(kernel, sizes, *a)
    zmsg, loc, alpha, spread, *sides = call(
        bind(begin_kernel), [(nz * 5, 1, 128), (3, *coarse), coarse, tile, *planes],
        [field, field, (3, *field), tile], "begin", pltpu.HBM, [pltpu.SemaphoreType.DMA((4,))], 55100 << 10,
    )(r, sigma, kappa, inverse_rows)
    zrec = along_z(zmsg)
    halos = halo(sides)
    xmsg, own, zhalo, chain, final = call(
        bind(first_lines_kernel), [to_xy, tile, tile, (4, nz, 128), tile], [coarse], "lines_first"
    )(zrec, loc, alpha, *halos[:2])
    xrec = along_xy(xmsg)
    z1, w1, jac, zmsg, alpha = call(
        bind(first_kernel), [field, field, field, (nz * 4, 1, 128), coarse], name="operator_first"
    )(r, sigma, kappa, xrec, own, zhalo, *halos, loc, spread)
    zrec = along_z(zmsg)
    part, zhalo, z2, *sides = call(
        bind(second_lines_kernel), [tile, tile, field, *planes], [coarse], "lines_second"
    )(zrec, loc, alpha, chain, final, jac)
    halos = halo(sides)
    w2, xmsg = call(bind(second_kernel), [field, to_xy], [(128, 128)], "operator_second")(
        r, w1, sigma, kappa, z2, zhalo, part, *halos
    )
    xrec = along_xy(xmsg)
    sums, values = call(bind(plane_kernel), [(1, 128), tile], [(2, nx * ny, 128)], "plane")(xrec)
    sums = along_z(jnp.broadcast_to(sums[None], (nz, 1, 128)))
    return tuple(
        call(end_kernel, [field, field], name="end")(sums, values, r, sigma, kappa, z1, w1, z2, w2)
    )


def solution(mesh):
    sizes = (mesh.shape["gx"], mesh.shape["gy"], mesh.shape["gz"])
    spec = P("gx", "gy", "gz")

    def run(r, sigma, kappa, inverse):
        return shards(sizes, r, sigma, kappa, inverse.reshape(8, 128))

    return jax.shard_map(
        run,
        mesh=mesh,
        in_specs=(spec, spec, P(None, "gx", "gy", "gz"), P(("gx", "gy", "gz"), None)),
        out_specs=(spec, spec),
        check_vma=False,
    )
```
